512 devices in a mesh: date: 128 (over z, y, x_lo), az: 4 (over x_hi, core).
Axes of the slice: x: 4 (x_hi: 2, x_lo: 2; x = x_hi * 2 + x_lo), y: 4, z: 16, core: 2. Of those that a mesh axis runs over, the one named last changes fastest.
Arguments:
- slabs: float32 [128, 2, 128, 2048], P('date', None, 'az'), may hold values from -6 to 6
Outputs:
- interferos: float32 [5, 2, 128, 32, 128], P(None, None, 'date', 'az')
- coherence: float32 [5, 128, 32, 128], P(None, 'date', 'az')
The draws below stay inside these ranges and needn't reach their ends.
All inputs are finite; a program needn't handle non-finite values.
Results may differ from the reference program's by a relative error of at most 0.0003.
Values sent between devices are 32-bit elements; how exact they have to be, the bound alone decides.
No kernel may reach another device: no remote copies, remote signals or barrier semaphores. Data moves between devices by JAX's collectives and lax.ppermute only.
A program may use at most 64 MiB of HBM per device.

```python
import jax
import jax.numpy as jnp
from jax import lax

RG = 2048
LOOK_AZ = 4
LOOK_RG = 16
WIN = 5
SPAN = 5
DATES = 128
AZ = 128


def block_levels(rng, shape, pieces, smallest, high):
    level = 1.0
    for dim, shards_of in pieces:
        steps = jax.random.uniform(jax.random.fold_in(jax.random.fold_in(rng, 6), dim), (shards_of,), jnp.float32, smallest / len(pieces), high / len(pieces))
        level = level * jnp.repeat(jnp.exp(steps), shape[dim] // shards_of).reshape((-1,) + (1,) * (len(shape) - 1 - dim))
    return level


def centred(own_key, extent, width, limit, split=(), kind=jnp.bfloat16):
    gain = block_levels(own_key, extent, split, -0.22, 0.18) if split else 1.0
    values = jax.random.normal(own_key, extent, jnp.float32) * width * gain
    return jnp.minimum(jnp.maximum(values, -limit), limit).astype(kind)


def setup_inputs(seed: int = 0) -> dict:
    keys = jax.random.split(jax.random.key(seed), 2)
    slabs = centred(keys[0], (DATES, 2, AZ, RG), 1.0, 6.0, ((0, 128), (2, 4)), jnp.float32)
    return {"slabs": slabs}


def multilook(field):
    rows, cols = field.shape
    return field.reshape(rows // LOOK_AZ, LOOK_AZ, cols // LOOK_RG, LOOK_RG).mean(axis=(1, 3))

def boxsum(field):
    half = WIN // 2
    padded = jnp.pad(field, ((half, half), (half, half)))
    rows, cols = field.shape
    total = jnp.zeros_like(field)
    for shift_a in range(WIN):
        for shift_r in range(WIN):
            total = total + padded[shift_a:shift_a + rows, shift_r:shift_r + cols]
    return total

def reference(slabs):

    def per_date(index):
        own_img = lax.dynamic_index_in_dim(slabs, index, 0, keepdims=False)
        own_box = boxsum(multilook(own_img[0] * own_img[0] + own_img[1] * own_img[1]))
        looks_out = []
        coher_out = []
        for gap in range(1, SPAN + 1):
            later = jnp.minimum(index + gap, DATES - 1).astype(jnp.int32)
            other = lax.dynamic_index_in_dim(slabs, later, 0, keepdims=False)
            real_part = multilook(own_img[0] * other[0] + own_img[1] * other[1])
            imag_part = multilook(own_img[1] * other[0] - own_img[0] * other[1])
            other_box = boxsum(multilook(other[0] * other[0] + other[1] * other[1]))
            real_box = boxsum(real_part)
            imag_box = boxsum(imag_part)
            value = jnp.sqrt(real_box * real_box + imag_box * imag_box) / jnp.sqrt(own_box * other_box + 1e-06)
            paired = index + gap < DATES
            looks_out.append(jnp.where(paired, jnp.stack([real_part, imag_part]), 0.0))
            coher_out.append(jnp.where(paired, value, 0.0))
        return (jnp.stack(looks_out), jnp.stack(coher_out))
    looks_all, coher_all = lax.map(per_date, jnp.arange(DATES, dtype=jnp.int32))
    return (jnp.transpose(looks_all, (1, 2, 0, 3, 4)), jnp.transpose(coher_all, (1, 0, 2, 3)))
```

```python
import jax
import jax.numpy as jnp
from jax import lax
from jax.experimental import pallas as pl
from jax.experimental.pallas import tpu as pltpu
from jax.sharding import PartitionSpec as P

LOOK_AZ = 4
LOOK_RG = 16
WIN = 5
SPAN = 5
GROUP = 8
FIELDS = 3 * SPAN + 1
SUB = 16


def cut_kernel(slab_ref, out_ref):
    planes, lines, samples = slab_ref.shape
    width = samples // SUB
    for plane in range(planes):
        for line in range(0, lines, LOOK_AZ):
            for block in range(SUB):
                part = slab_ref[plane, line : line + LOOK_AZ, block * width : (block + 1) * width]
                start = ((line // LOOK_AZ) * planes + plane) * LOOK_AZ * SUB + block
                out_ref[pl.ds(start, LOOK_AZ, stride=SUB), :] = part


def cut(slab):
    planes, lines, samples = slab.shape
    rows = planes * lines * SUB
    return pl.pallas_call(
        cut_kernel,
        out_shape=jax.ShapeDtypeStruct((rows, samples // SUB), jnp.float32),
        name="cut",
    )(slab)


def look_kernel(own_ref, later_ref, out_ref, sums, cells):
    width = own_ref.shape[-1]

    def date(index):
        ref, at = (own_ref, index) if index < GROUP else (later_ref, index - GROUP)
        return [ref[at, k] for k in range(LOOK_AZ)], [ref[at, LOOK_AZ + k] for k in range(LOOK_AZ)]

    def put(row, terms):
        total = terms[0]
        for term in terms[1:]:
            total = total + term
        sums[row * SUB : (row + 1) * SUB, :] = total

    first_power = 2 * SPAN * GROUP
    for index in range(GROUP + SPAN):
        real, imag = date(index)
        put(first_power + index, [v * v for v in real + imag])
        if index >= GROUP:
            continue
        for gap in range(1, SPAN + 1):
            other_real, other_imag = date(index + gap)
            row = index * 2 * SPAN + gap - 1
            put(row, [a * b for a, b in zip(real + imag, other_real + other_imag)])
            put(row + SPAN, [a * b - c * d for a, b, c, d in zip(imag, other_real, real, other_imag)])

    cols = cells.shape[-1]
    per_block = width // LOOK_RG
    sample = lax.broadcasted_iota(jnp.int32, (width, cols), 0)
    lane = lax.broadcasted_iota(jnp.int32, (width, cols), 1)
    weight = jnp.where(sample // LOOK_RG == lane % per_block, 1.0 / (LOOK_AZ * LOOK_RG), 0.0)
    looks = jnp.dot(sums[...], weight, precision=lax.Precision.HIGHEST, preferred_element_type=jnp.float32)
    looks = looks.reshape(looks.shape[0] // SUB, SUB, cols)
    block = lax.broadcasted_iota(jnp.int32, (1, SUB, cols), 1)
    lane = lax.broadcasted_iota(jnp.int32, (1, SUB, cols), 2)
    cells[...] = jnp.sum(jnp.where(lane // per_block == block, looks, 0.0), axis=1)
    for index in range(GROUP):
        cross = cells[index * 2 * SPAN : (index + 1) * 2 * SPAN, :]
        power = cells[first_power + index : first_power + index + SPAN + 1, :]
        for tile in range(out_ref.shape[1]):
            out_ref[index, tile, : 2 * SPAN, :] = cross
            out_ref[index, tile, 2 * SPAN :, :] = power


def look(own, later, tiles, cols):
    rows = 2 * SPAN * GROUP + GROUP + SPAN
    return pl.pallas_call(
        look_kernel,
        out_shape=jax.ShapeDtypeStruct((GROUP, tiles, FIELDS, cols), jnp.float32),
        scratch_shapes=[
            pltpu.VMEM((rows * SUB, own.shape[-1]), jnp.float32),
            pltpu.VMEM((rows, cols), jnp.float32),
        ],
        compiler_params=pltpu.CompilerParams(vmem_limit_bytes=24 * 1024 * 1024),
        name="look",
    )(own, later)


def coherence_kernel(dates, tiles, place_ref, rows_ref, looks_ref, coher_ref):
    date = place_ref[0]
    tile = place_ref[1]
    cols = rows_ref.shape[-1]
    half = WIN // 2
    lane = lax.broadcasted_iota(jnp.int32, (FIELDS, cols), 1)
    rows = []
    for offset in range(-half, GROUP + half):
        other = tile + offset // GROUP
        inside = jnp.logical_and(other >= 0, other < tiles)
        row = rows_ref[offset % GROUP, jnp.clip(other, 0, tiles - 1)]
        rows.append(row if 0 <= offset < GROUP else jnp.where(inside, row, 0.0))
    for r in range(GROUP):
        tall = rows[r]
        for shift in range(1, WIN):
            tall = tall + rows[r + shift]
        boxed = tall
        for shift in range(1, half + 1):
            boxed = boxed + jnp.where(lane >= shift, pltpu.roll(tall, shift, 1), 0.0)
            boxed = boxed + jnp.where(lane < cols - shift, pltpu.roll(tall, cols - shift, 1), 0.0)
        real = boxed[:SPAN]
        imag = boxed[SPAN : 2 * SPAN]
        own = boxed[2 * SPAN : 2 * SPAN + 1]
        later = boxed[2 * SPAN + 1 :]
        value = jnp.sqrt(real * real + imag * imag) / jnp.sqrt(own * later + 1e-06)
        for gap in range(1, SPAN + 1):
            paired = date + gap < dates
            coher_ref[gap - 1, 0, r : r + 1, :] = jnp.where(paired, value[gap - 1 : gap], 0.0)
            for part in range(2):
                field = part * SPAN + gap - 1
                looks_ref[gap - 1, part, 0, r : r + 1, :] = jnp.where(paired, rows[r + half][field : field + 1], 0.0)


def finish(place, rows, dates):
    _, tiles, _, cols = rows.shape

    def kernel(*refs):
        coherence_kernel(dates, tiles, *refs)

    return pl.pallas_call(
        kernel,
        in_specs=[pl.BlockSpec(memory_space=pltpu.SMEM), pl.BlockSpec(memory_space=pltpu.VMEM)],
        out_shape=(
            jax.ShapeDtypeStruct((SPAN, 2, 1, GROUP, cols), jnp.float32),
            jax.ShapeDtypeStruct((SPAN, 1, GROUP, cols), jnp.float32),
        ),
        name="finish",
    )(place, rows)


def local(slabs):
    dates, tiles = lax.axis_size("date"), lax.axis_size("az")
    _, planes, lines, samples = slabs.shape
    cols = samples // LOOK_RG
    groups = [list(range(g, g + GROUP)) for g in range(0, dates, GROUP)]
    wide = [list(range(g * tiles, (g + GROUP) * tiles)) for g in range(0, dates, GROUP)]
    pieces = cut(slabs[0]).reshape(GROUP, planes * LOOK_AZ, SUB, samples // SUB)
    own = lax.all_to_all(pieces, "date", 0, 0, axis_index_groups=groups, tiled=True)
    back = [(i, (i - GROUP) % dates) for i in range(dates)]
    later = lax.ppermute(own[:SPAN], "date", back)
    fields = look(own, later, tiles, cols)
    fields = fields.reshape(GROUP * tiles, FIELDS, cols)
    rows = lax.all_to_all(fields, ("date", "az"), 0, 0, axis_index_groups=wide, tiled=True)
    place = jnp.stack([lax.axis_index("date"), lax.axis_index("az")]).astype(jnp.int32)
    return finish(place, rows.reshape(GROUP, tiles, FIELDS, cols), dates)


def solution(mesh):
    in_specs = (P("date", None, "az", None),)
    out_specs = (P(None, None, "date", "az", None), P(None, "date", "az", None))
    return jax.shard_map(local, mesh=mesh, in_specs=in_specs, out_specs=out_specs, check_vma=False)
```

```python
import jax
import jax.numpy as jnp
from jax import lax
from jax.experimental import pallas as pl
from jax.experimental.pallas import tpu as pltpu
from jax.sharding import PartitionSpec as P

LOOK_AZ = 4
LOOK_RG = 16
WIN = 5
SPAN = 5
GROUP = 8
FIELDS = 3 * SPAN + 1
SUB = 16


def cut_kernel(slab_ref, out_ref):
    planes, lines, _ = slab_ref.shape
    width = out_ref.shape[-1]
    for plane in range(planes):
        for line in range(0, lines, 8):
            for block in range(SUB):
                part = slab_ref[plane, line : line + 8, block * width : (block + 1) * width]
                start = (line * planes + plane) * SUB + block
                out_ref[pl.ds(start, 8, stride=planes * SUB), :] = part


def cut(slab):
    planes, lines, samples = slab.shape
    rows = planes * lines * SUB
    return pl.pallas_call(
        cut_kernel,
        out_shape=jax.ShapeDtypeStruct((rows, samples // SUB), jnp.float32),
        compiler_params=pltpu.CompilerParams(vmem_limit_bytes=4 * 1024 * 1024),
        name="cut",
    )(slab)


def look_kernel(own_ref, later_ref, out_ref, sums, cells):
    width = own_ref.shape[-1]

    def date(index):
        ref, at = (own_ref, index) if index < GROUP else (later_ref, index - GROUP)
        return [ref[at, 2 * k] for k in range(LOOK_AZ)], [ref[at, 2 * k + 1] for k in range(LOOK_AZ)]

    def put(row, terms):
        total = terms[0]
        for term in terms[1:]:
            total = total + term
        sums[row * SUB : (row + 1) * SUB, :] = total

    first_power = 2 * SPAN * GROUP
    for index in range(GROUP + SPAN):
        real, imag = date(index)
        put(first_power + index, [v * v for v in real + imag])
        if index >= GROUP:
            continue
        for gap in range(1, SPAN + 1):
            other_real, other_imag = date(index + gap)
            row = index * 2 * SPAN + gap - 1
            put(row, [a * b for a, b in zip(real + imag, other_real + other_imag)])
            put(row + SPAN, [a * b - c * d for a, b, c, d in zip(imag, other_real, real, other_imag)])

    cols = cells.shape[-1]
    per_block = width // LOOK_RG
    sample = lax.broadcasted_iota(jnp.int32, (width, cols), 0)
    lane = lax.broadcasted_iota(jnp.int32, (width, cols), 1)
    weight = jnp.where(sample // LOOK_RG == lane % per_block, 1.0 / (LOOK_AZ * LOOK_RG), 0.0)
    looks = jnp.dot(sums[...], weight, precision=lax.Precision.HIGHEST, preferred_element_type=jnp.float32)
    looks = looks.reshape(looks.shape[0] // SUB, SUB, cols)
    block = lax.broadcasted_iota(jnp.int32, (1, SUB, cols), 1)
    lane = lax.broadcasted_iota(jnp.int32, (1, SUB, cols), 2)
    cells[...] = jnp.sum(jnp.where(lane // per_block == block, looks, 0.0), axis=1)
    for index in range(GROUP):
        cross = cells[index * 2 * SPAN : (index + 1) * 2 * SPAN, :]
        power = cells[first_power + index : first_power + index + SPAN + 1, :]
        for tile in range(out_ref.shape[1]):
            out_ref[index, tile, : 2 * SPAN, :] = cross
            out_ref[index, tile, 2 * SPAN :, :] = power


def look(own, later, tiles, cols):
    rows = 2 * SPAN * GROUP + GROUP + SPAN
    return pl.pallas_call(
        look_kernel,
        out_shape=jax.ShapeDtypeStruct((GROUP, tiles, FIELDS, cols), jnp.float32),
        scratch_shapes=[
            pltpu.VMEM((rows * SUB, own.shape[-1]), jnp.float32),
            pltpu.VMEM((rows, cols), jnp.float32),
        ],
        compiler_params=pltpu.CompilerParams(vmem_limit_bytes=8 * 1024 * 1024),
        name="look",
    )(own, later)


def coherence_kernel(rows_ref, looks_ref, coher_ref):
    date, dates = lax.axis_index("date"), lax.axis_size("date")
    tile = lax.axis_index("az")
    tiles, cols = rows_ref.shape[1], rows_ref.shape[-1]
    half = WIN // 2
    lane = lax.broadcasted_iota(jnp.int32, (FIELDS, cols), 1)
    rows = []
    for offset in range(-half, GROUP + half):
        other = tile + offset // GROUP
        inside = jnp.logical_and(other >= 0, other < tiles)
        row = rows_ref[offset % GROUP, jnp.clip(other, 0, tiles - 1)]
        rows.append(row if 0 <= offset < GROUP else jnp.where(inside, row, 0.0))
    for r in range(GROUP):
        tall = rows[r]
        for shift in range(1, WIN):
            tall = tall + rows[r + shift]
        boxed = tall
        for shift in range(1, half + 1):
            boxed = boxed + jnp.where(lane >= shift, pltpu.roll(tall, shift, 1), 0.0)
            boxed = boxed + jnp.where(lane < cols - shift, pltpu.roll(tall, cols - shift, 1), 0.0)
        real = boxed[:SPAN]
        imag = boxed[SPAN : 2 * SPAN]
        own = boxed[2 * SPAN : 2 * SPAN + 1]
        later = boxed[2 * SPAN + 1 :]
        value = jnp.sqrt(real * real + imag * imag) / jnp.sqrt(own * later + 1e-06)
        for gap in range(1, SPAN + 1):
            paired = date + gap < dates
            coher_ref[gap - 1, 0, r : r + 1, :] = jnp.where(paired, value[gap - 1 : gap], 0.0)
            for part in range(2):
                field = part * SPAN + gap - 1
                looks_ref[gap - 1, part, 0, r : r + 1, :] = jnp.where(paired, rows[r + half][field : field + 1], 0.0)


def finish(rows):
    cols = rows.shape[-1]
    return pl.pallas_call(
        coherence_kernel,
        out_shape=(
            jax.ShapeDtypeStruct((SPAN, 2, 1, GROUP, cols), jnp.float32),
            jax.ShapeDtypeStruct((SPAN, 1, GROUP, cols), jnp.float32),
        ),
        compiler_params=pltpu.CompilerParams(vmem_limit_bytes=4 * 1024 * 1024),
        name="finish",
    )(rows)


def local(slabs):
    dates, tiles = lax.axis_size("date"), lax.axis_size("az")
    _, planes, lines, samples = slabs.shape
    cols = samples // LOOK_RG
    groups = [list(range(g, g + GROUP)) for g in range(0, dates, GROUP)]
    wide = [list(range(g * tiles, (g + GROUP) * tiles)) for g in range(0, dates, GROUP)]
    pieces = cut(slabs[0]).reshape(GROUP, LOOK_AZ * planes, SUB, samples // SUB)
    own = lax.all_to_all(pieces, "date", 0, 0, axis_index_groups=groups, tiled=True)
    back = [(i, (i - GROUP) % dates) for i in range(dates)]
    later = lax.ppermute(own[:SPAN], "date", back)
    fields = look(own, later, tiles, cols)
    fields = fields.reshape(GROUP * tiles, FIELDS, cols)
    rows = lax.all_to_all(fields, ("date", "az"), 0, 0, axis_index_groups=wide, tiled=True)
    return finish(rows.reshape(GROUP, tiles, FIELDS, cols))


def solution(mesh):
    in_specs = (P("date", None, "az", None),)
    out_specs = (P(None, None, "date", "az", None), P(None, "date", "az", None))
    return jax.shard_map(local, mesh=mesh, in_specs=in_specs, out_specs=out_specs, check_vma=False)
```

```python
import jax
import jax.numpy as jnp
from jax import lax
from jax.experimental import pallas as pl
from jax.experimental.pallas import tpu as pltpu
from jax.sharding import PartitionSpec as P

LOOK_AZ = 4
LOOK_RG = 16
WIN = 5
SPAN = 5
GROUP = 8
FIELDS = 3 * SPAN + 1
SUB = 16


def cut_kernel(slab_ref, out_ref):
    planes, lines, _ = slab_ref.shape
    width = out_ref.shape[-1]
    for plane in range(planes):
        for line in range(0, lines, 8):
            for block in range(SUB):
                part = slab_ref[plane, line : line + 8, block * width : (block + 1) * width]
                start = (line * planes + plane) * SUB + block
                out_ref[pl.ds(start, 8, stride=planes * SUB), :] = part


def cut(slab):
    planes, lines, samples = slab.shape
    rows = planes * lines * SUB
    return pl.pallas_call(
        cut_kernel,
        out_shape=jax.ShapeDtypeStruct((rows, samples // SUB), jnp.float32),
        compiler_params=pltpu.CompilerParams(vmem_limit_bytes=4 * 1024 * 1024),
        name="cut",
    )(slab)


def look_kernel(own_ref, later_ref, out_ref, sums, cells):
    width = own_ref.shape[-1]

    def date(index):
        ref, at = (own_ref, index) if index < GROUP else (later_ref, index - GROUP)
        return [ref[at, 2 * k] for k in range(LOOK_AZ)], [ref[at, 2 * k + 1] for k in range(LOOK_AZ)]

    def put(row, terms):
        total = terms[0]
        for term in terms[1:]:
            total = total + term
        sums[row * SUB : (row + 1) * SUB, :] = total

    first_power = 2 * SPAN * GROUP
    for index in range(GROUP + SPAN):
        real, imag = date(index)
        put(first_power + index, [v * v for v in real + imag])
        if index >= GROUP:
            continue
        for gap in range(1, SPAN + 1):
            other_real, other_imag = date(index + gap)
            row = index * 2 * SPAN + gap - 1
            put(row, [a * b for a, b in zip(real + imag, other_real + other_imag)])
            put(row + SPAN, [a * b - c * d for a, b, c, d in zip(imag, other_real, real, other_imag)])

    cols = cells.shape[-1]
    per_block = width // LOOK_RG
    sample = lax.broadcasted_iota(jnp.int32, (width, cols), 0)
    lane = lax.broadcasted_iota(jnp.int32, (width, cols), 1)
    weight = jnp.where(sample // LOOK_RG == lane % per_block, 1.0 / (LOOK_AZ * LOOK_RG), 0.0)
    looks = jnp.dot(sums[...], weight, precision=lax.Precision.HIGHEST, preferred_element_type=jnp.float32)
    looks = looks.reshape(looks.shape[0] // SUB, SUB, cols)
    block = lax.broadcasted_iota(jnp.int32, (1, SUB, cols), 1)
    lane = lax.broadcasted_iota(jnp.int32, (1, SUB, cols), 2)
    cells[...] = jnp.sum(jnp.where(lane // per_block == block, looks, 0.0), axis=1)
    for index in range(GROUP):
        cross = cells[index * 2 * SPAN : (index + 1) * 2 * SPAN, :]
        power = cells[first_power + index : first_power + index + SPAN + 1, :]
        out_ref[index, : 2 * SPAN, :] = cross
        out_ref[index, 2 * SPAN :, :] = power


def look(own, later, cols):
    rows = 2 * SPAN * GROUP + GROUP + SPAN
    return pl.pallas_call(
        look_kernel,
        out_shape=jax.ShapeDtypeStruct((GROUP, FIELDS, cols), jnp.float32),
        scratch_shapes=[
            pltpu.VMEM((rows * SUB, own.shape[-1]), jnp.float32),
            pltpu.VMEM((rows, cols), jnp.float32),
        ],
        compiler_params=pltpu.CompilerParams(vmem_limit_bytes=8 * 1024 * 1024),
        name="look",
    )(own, later)


def coherence_kernel(rows_ref, before_ref, after_ref, looks_ref, coher_ref):
    date, dates = lax.axis_index("date"), lax.axis_size("date")
    tile, tiles = lax.axis_index("az"), lax.axis_size("az")
    cols = rows_ref.shape[-1]
    half = WIN // 2
    lane = lax.broadcasted_iota(jnp.int32, (FIELDS, cols), 1)
    rows = [jnp.where(tile > 0, before_ref[k], 0.0) for k in range(half)]
    rows += [rows_ref[k] for k in range(GROUP)]
    rows += [jnp.where(tile < tiles - 1, after_ref[k], 0.0) for k in range(half)]
    for r in range(GROUP):
        tall = rows[r]
        for shift in range(1, WIN):
            tall = tall + rows[r + shift]
        boxed = tall
        for shift in range(1, half + 1):
            boxed = boxed + jnp.where(lane >= shift, pltpu.roll(tall, shift, 1), 0.0)
            boxed = boxed + jnp.where(lane < cols - shift, pltpu.roll(tall, cols - shift, 1), 0.0)
        real = boxed[:SPAN]
        imag = boxed[SPAN : 2 * SPAN]
        own = boxed[2 * SPAN : 2 * SPAN + 1]
        later = boxed[2 * SPAN + 1 :]
        value = jnp.sqrt(real * real + imag * imag) / jnp.sqrt(own * later + 1e-06)
        for gap in range(1, SPAN + 1):
            paired = date + gap < dates
            coher_ref[gap - 1, 0, r : r + 1, :] = jnp.where(paired, value[gap - 1 : gap], 0.0)
            for part in range(2):
                field = part * SPAN + gap - 1
                looks_ref[gap - 1, part, 0, r : r + 1, :] = jnp.where(paired, rows[r + half][field : field + 1], 0.0)


def finish(rows, before, after):
    cols = rows.shape[-1]
    return pl.pallas_call(
        coherence_kernel,
        out_shape=(
            jax.ShapeDtypeStruct((SPAN, 2, 1, GROUP, cols), jnp.float32),
            jax.ShapeDtypeStruct((SPAN, 1, GROUP, cols), jnp.float32),
        ),
        compiler_params=pltpu.CompilerParams(vmem_limit_bytes=4 * 1024 * 1024),
        name="finish",
    )(rows, before, after)


def local(slabs):
    dates, tiles = lax.axis_size("date"), lax.axis_size("az")
    _, planes, lines, samples = slabs.shape
    half = WIN // 2
    groups = [list(range(g, g + GROUP)) for g in range(0, dates, GROUP)]
    pieces = cut(slabs[0]).reshape(GROUP, LOOK_AZ * planes, SUB, samples // SUB)
    own = lax.all_to_all(pieces, "date", 0, 0, axis_index_groups=groups, tiled=True)
    back = [(i, (i - GROUP) % dates) for i in range(dates)]
    later = lax.ppermute(own[:SPAN], "date", back)
    fields = look(own, later, samples // LOOK_RG)
    rows = lax.all_to_all(fields, "date", 0, 0, axis_index_groups=groups, tiled=True)
    up = [(i, (i + 1) % tiles) for i in range(tiles)]
    down = [(j, i) for i, j in up]
    before = lax.ppermute(rows[GROUP - half :], "az", up)
    after = lax.ppermute(rows[:half], "az", down)
    return finish(rows, before, after)


def solution(mesh):
    in_specs = (P("date", None, "az", None),)
    out_specs = (P(None, None, "date", "az", None), P(None, "date", "az", None))
    return jax.shard_map(local, mesh=mesh, in_specs=in_specs, out_specs=out_specs, check_vma=False)
```

```python
import jax
import jax.numpy as jnp
from jax import lax
from jax.experimental import pallas as pl
from jax.experimental.pallas import tpu as pltpu
from jax.sharding import PartitionSpec as P

LOOK_AZ = 4
LOOK_RG = 16
WIN = 5
SPAN = 5
GROUP = 8
FIELDS = 3 * SPAN + 1
SUB = 16


def cut_kernel(slab_ref, out_ref):
    planes, lines, _ = slab_ref.shape
    width = out_ref.shape[-1]
    for plane in range(planes):
        for line in range(0, lines, 8):
            for block in range(SUB):
                part = slab_ref[plane, line : line + 8, block * width : (block + 1) * width]
                start = (line * planes + plane) * SUB + block
                out_ref[pl.ds(start, 8, stride=planes * SUB), :] = part


def cut(slab):
    planes, lines, samples = slab.shape
    rows = planes * lines * SUB
    return pl.pallas_call(
        cut_kernel,
        out_shape=jax.ShapeDtypeStruct((rows, samples // SUB), jnp.float32),
        compiler_params=pltpu.CompilerParams(vmem_limit_bytes=4 * 1024 * 1024),
        name="cut",
    )(slab)


def inside(index):
    return min(SPAN, GROUP - 1 - index)


def look_at(date, pairs, powers, sums, cols):
    width = sums.shape[-1]
    count = 0

    def put(terms):
        nonlocal count
        total = terms[0]
        for term in terms[1:]:
            total = total + term
        sums[count * SUB : (count + 1) * SUB, :] = total
        count += 1

    for index, gaps in pairs:
        real, imag = date(index)
        others = [date(index + gap) for gap in gaps]
        for other_real, other_imag in others:
            put([a * b for a, b in zip(real + imag, other_real + other_imag)])
        for other_real, other_imag in others:
            put([a * b - c * d for a, b, c, d in zip(imag, other_real, real, other_imag)])
    for index in powers:
        real, imag = date(index)
        put([v * v for v in real + imag])

    per_block = width // LOOK_RG
    sample = lax.broadcasted_iota(jnp.int32, (width, cols), 0)
    lane = lax.broadcasted_iota(jnp.int32, (width, cols), 1)
    weight = jnp.where(sample // LOOK_RG == lane % per_block, 1.0 / (LOOK_AZ * LOOK_RG), 0.0)
    looks = jnp.dot(
        sums[: count * SUB, :], weight, precision=lax.Precision.HIGHEST, preferred_element_type=jnp.float32
    )
    looks = looks.reshape(count, SUB, cols)
    block = lax.broadcasted_iota(jnp.int32, (1, SUB, cols), 1)
    lane = lax.broadcasted_iota(jnp.int32, (1, SUB, cols), 2)
    return jnp.sum(jnp.where(lane // per_block == block, looks, 0.0), axis=1)


def planes_of(ref, at):
    return [ref[at, 2 * k] for k in range(LOOK_AZ)], [ref[at, 2 * k + 1] for k in range(LOOK_AZ)]


OWN_PAIRS = [(d, range(1, inside(d) + 1)) for d in range(GROUP)]
LATER_PAIRS = [(d, range(inside(d) + 1, SPAN + 1)) for d in range(GROUP) if inside(d) < SPAN]
OWN_ROWS = sum(2 * len(gaps) for _, gaps in OWN_PAIRS)
LATER_ROWS = sum(2 * len(gaps) for _, gaps in LATER_PAIRS)


def own_kernel(own_ref, out_ref, sums):
    out_ref[...] = look_at(lambda d: planes_of(own_ref, d), OWN_PAIRS, range(GROUP), sums, out_ref.shape[-1])


def later_kernel(own_ref, later_ref, looks_ref, out_ref, sums, cells):
    def date(index):
        return planes_of(own_ref, index) if index < GROUP else planes_of(later_ref, index - GROUP)

    cells[...] = look_at(date, LATER_PAIRS, range(GROUP, GROUP + SPAN), sums, out_ref.shape[-1])
    own_at = later_at = 0
    for index in range(GROUP):
        near, far = inside(index), SPAN - inside(index)
        piece = out_ref.at[index, 0]
        for part in range(2):
            if near:
                piece[part * SPAN : part * SPAN + near, :] = looks_ref[own_at : own_at + near, :]
            if far:
                piece[part * SPAN + near : (part + 1) * SPAN, :] = cells[later_at : later_at + far, :]
            own_at += near
            later_at += far
        piece[2 * SPAN : 2 * SPAN + 1 + near, :] = looks_ref[OWN_ROWS + index : OWN_ROWS + index + 1 + near, :]
        if far:
            piece[2 * SPAN + 1 + near :, :] = cells[LATER_ROWS : LATER_ROWS + far, :]
        for tile in range(1, out_ref.shape[1]):
            out_ref[index, tile] = out_ref[index, 0]


def look_own(own, cols):
    rows = OWN_ROWS + GROUP
    return pl.pallas_call(
        own_kernel,
        out_shape=jax.ShapeDtypeStruct((rows, cols), jnp.float32),
        scratch_shapes=[pltpu.VMEM((rows * SUB, own.shape[-1]), jnp.float32)],
        compiler_params=pltpu.CompilerParams(vmem_limit_bytes=8 * 1024 * 1024),
        cost_estimate=pl.CostEstimate(
            flops=12 * rows * SUB * cols * cols, bytes_accessed=own.size * 4, transcendentals=0
        ),
        name="look_own",
    )(own)


def look_later(own, later, looks, tiles):
    cols = looks.shape[-1]
    rows = LATER_ROWS + SPAN
    return pl.pallas_call(
        later_kernel,
        out_shape=jax.ShapeDtypeStruct((GROUP, tiles, FIELDS, cols), jnp.float32),
        scratch_shapes=[
            pltpu.VMEM((rows * SUB, own.shape[-1]), jnp.float32),
            pltpu.VMEM((rows, cols), jnp.float32),
        ],
        compiler_params=pltpu.CompilerParams(vmem_limit_bytes=8 * 1024 * 1024),
        name="look_later",
    )(own, later, looks)


def coherence_kernel(rows_ref, looks_ref, coher_ref):
    date, dates = lax.axis_index("date"), lax.axis_size("date")
    tile = lax.axis_index("az")
    tiles, cols = rows_ref.shape[1], rows_ref.shape[-1]
    half = WIN // 2
    lane = lax.broadcasted_iota(jnp.int32, (FIELDS, cols), 1)
    rows = []
    for offset in range(-half, GROUP + half):
        other = tile + offset // GROUP
        inside = jnp.logical_and(other >= 0, other < tiles)
        row = rows_ref[offset % GROUP, jnp.clip(other, 0, tiles - 1)]
        rows.append(row if 0 <= offset < GROUP else jnp.where(inside, row, 0.0))
    for r in range(GROUP):
        tall = rows[r]
        for shift in range(1, WIN):
            tall = tall + rows[r + shift]
        boxed = tall
        for shift in range(1, half + 1):
            boxed = boxed + jnp.where(lane >= shift, pltpu.roll(tall, shift, 1), 0.0)
            boxed = boxed + jnp.where(lane < cols - shift, pltpu.roll(tall, cols - shift, 1), 0.0)
        real = boxed[:SPAN]
        imag = boxed[SPAN : 2 * SPAN]
        own = boxed[2 * SPAN : 2 * SPAN + 1]
        later = boxed[2 * SPAN + 1 :]
        value = jnp.sqrt(real * real + imag * imag) / jnp.sqrt(own * later + 1e-06)
        for gap in range(1, SPAN + 1):
            paired = date + gap < dates
            coher_ref[gap - 1, 0, r : r + 1, :] = jnp.where(paired, value[gap - 1 : gap], 0.0)
            for part in range(2):
                field = part * SPAN + gap - 1
                looks_ref[gap - 1, part, 0, r : r + 1, :] = jnp.where(paired, rows[r + half][field : field + 1], 0.0)


def finish(rows):
    cols = rows.shape[-1]
    return pl.pallas_call(
        coherence_kernel,
        out_shape=(
            jax.ShapeDtypeStruct((SPAN, 2, 1, GROUP, cols), jnp.float32),
            jax.ShapeDtypeStruct((SPAN, 1, GROUP, cols), jnp.float32),
        ),
        compiler_params=pltpu.CompilerParams(vmem_limit_bytes=4 * 1024 * 1024),
        name="finish",
    )(rows)


def local(slabs):
    dates, tiles = lax.axis_size("date"), lax.axis_size("az")
    _, planes, lines, samples = slabs.shape
    cols = samples // LOOK_RG
    groups = [list(range(g, g + GROUP)) for g in range(0, dates, GROUP)]
    wide = [list(range(g * tiles, (g + GROUP) * tiles)) for g in range(0, dates, GROUP)]
    pieces = cut(slabs[0]).reshape(GROUP, LOOK_AZ * planes, SUB, samples // SUB)
    own = lax.all_to_all(pieces, "date", 0, 0, axis_index_groups=groups, tiled=True)
    back = [(i, i - GROUP) for i in range(GROUP, dates)]
    later = lax.ppermute(own[:SPAN], "date", back)
    fields = look_later(own, later, look_own(own, cols), tiles)
    fields = fields.reshape(GROUP * tiles, FIELDS, cols)
    rows = lax.all_to_all(fields, ("date", "az"), 0, 0, axis_index_groups=wide, tiled=True)
    return finish(rows.reshape(GROUP, tiles, FIELDS, cols))


def solution(mesh):
    in_specs = (P("date", None, "az", None),)
    out_specs = (P(None, None, "date", "az", None), P(None, "date", "az", None))
    return jax.shard_map(local, mesh=mesh, in_specs=in_specs, out_specs=out_specs, check_vma=False)
```

```python
import jax
import jax.numpy as jnp
from jax import lax
from jax.experimental import pallas as pl
from jax.experimental.pallas import tpu as pltpu
from jax.sharding import PartitionSpec as P

LOOK_AZ = 4
LOOK_RG = 16
WIN = 5
SPAN = 5
GROUP = 8
FIELDS = 3 * SPAN + 1
LIMIT = 127 * 512 * 1024
SUB = 16


def cut_kernel(slab_ref, out_ref):
    planes, lines, _ = slab_ref.shape
    width = out_ref.shape[-1]
    for plane in range(planes):
        for line in range(0, lines, 8):
            for block in range(SUB):
                part = slab_ref[plane, line : line + 8, block * width : (block + 1) * width]
                start = (line * planes + plane) * SUB + block
                out_ref[pl.ds(start, 8, stride=planes * SUB), :] = part


def cut(slab):
    planes, lines, samples = slab.shape
    rows = planes * lines * SUB
    return pl.pallas_call(
        cut_kernel,
        out_shape=jax.ShapeDtypeStruct((rows, samples // SUB), jnp.float32),
        compiler_params=pltpu.CompilerParams(vmem_limit_bytes=4 * 1024 * 1024),
        name="cut",
    )(slab)


def look_at(date, pairs, powers, sums, cols):
    width = sums.shape[-1]
    count = 0

    def put(terms):
        nonlocal count
        total = terms[0]
        for term in terms[1:]:
            total = total + term
        sums[count * SUB : (count + 1) * SUB, :] = total
        count += 1

    for index, other_index in pairs:
        (real, imag), (other_real, other_imag) = date(index), date(other_index)
        put([a * b for a, b in zip(real + imag, other_real + other_imag)])
    for index, other_index in pairs:
        (real, imag), (other_real, other_imag) = date(index), date(other_index)
        put([a * b - c * d for a, b, c, d in zip(imag, other_real, real, other_imag)])
    for index in powers:
        real, imag = date(index)
        put([v * v for v in real + imag])

    per_block = width // LOOK_RG
    sample = lax.broadcasted_iota(jnp.int32, (width, cols), 0)
    lane = lax.broadcasted_iota(jnp.int32, (width, cols), 1)
    weight = jnp.where(sample // LOOK_RG == lane % per_block, 1.0 / (LOOK_AZ * LOOK_RG), 0.0)
    looks = jnp.dot(
        sums[: count * SUB, :], weight, precision=lax.Precision.HIGHEST, preferred_element_type=jnp.float32
    )
    looks = looks.reshape(count, SUB, cols)
    block = lax.broadcasted_iota(jnp.int32, (1, SUB, cols), 1)
    lane = lax.broadcasted_iota(jnp.int32, (1, SUB, cols), 2)
    return jnp.sum(jnp.where(lane // per_block == block, looks, 0.0), axis=1)


def planes_of(ref, at):
    return [ref[at, 2 * k] for k in range(LOOK_AZ)], [ref[at, 2 * k + 1] for k in range(LOOK_AZ)]


OWN_PAIRS = [(d, d + s) for s in range(1, SPAN + 1) for d in range(GROUP - s)]
LATER_PAIRS = [(d, d + s) for s in range(1, SPAN + 1) for d in range(GROUP - s, GROUP)]
OWN_ROWS = 2 * len(OWN_PAIRS) + GROUP
LATER_ROWS = 2 * len(LATER_PAIRS) + SPAN


def own_kernel(own_ref, out_ref, sums):
    out_ref[...] = look_at(lambda d: planes_of(own_ref, d), OWN_PAIRS, range(GROUP), sums, out_ref.shape[-1])


def later_kernel(own_ref, later_ref, out_ref, sums):
    def date(index):
        return planes_of(own_ref, index) if index < GROUP else planes_of(later_ref, index - GROUP)

    out_ref[...] = look_at(date, LATER_PAIRS, range(GROUP, GROUP + SPAN), sums, out_ref.shape[-1])


def look(kernel, rows, cols, name, *arrays):
    return pl.pallas_call(
        kernel,
        out_shape=jax.ShapeDtypeStruct((rows, cols), jnp.float32),
        scratch_shapes=[pltpu.VMEM((rows * SUB, arrays[0].shape[-1]), jnp.float32)],
        compiler_params=pltpu.CompilerParams(vmem_limit_bytes=8 * 1024 * 1024),
        cost_estimate=pl.CostEstimate(
            flops=12 * rows * SUB * cols * cols, bytes_accessed=arrays[0].size * 4, transcendentals=0
        ),
        name=name,
    )(*arrays)


def coherence_kernel(own_ref, later_ref, looks_ref, coher_ref, own_rows, later_rows, fields, arrived):
    date, dates = lax.axis_index("date"), lax.axis_size("date")
    tile, tiles = lax.axis_index("az"), lax.axis_size("az")
    member = lax.rem(date, GROUP)
    cols = fields.shape[-1]
    half = WIN // 2
    copies = []
    for offset in range(-half, GROUP + half):
        other = jnp.clip(tile + offset // GROUP, 0, tiles - 1)
        source = (offset % GROUP) * tiles + other
        count = len(copies)
        for k, (ref, held) in enumerate(((own_ref, own_rows), (later_ref, later_rows))):
            copies.append(pltpu.make_async_copy(ref.at[source], held.at[offset + half], arrived.at[count + k]))
            copies[-1].start()
    for copy in copies:
        copy.wait()

    def pick(at, own_at, later_at, gap):
        is_own = member + gap < GROUP
        mine = jnp.clip(own_at + member, 0, OWN_ROWS - 1)
        next_one = jnp.clip(later_at + member + gap - GROUP, 0, LATER_ROWS - 1)
        for row in range(GROUP + 2 * half):
            own = own_rows[row, pl.ds(mine, 1), :]
            later = later_rows[row, pl.ds(next_one, 1), :]
            fields[row, at : at + 1, :] = jnp.where(is_own, own, later)

    own_at = later_at = 0
    own_pairs, later_pairs = len(OWN_PAIRS), len(LATER_PAIRS)
    for gap in range(1, SPAN + 1):
        for part in range(2):
            pick(part * SPAN + gap - 1, own_at + part * own_pairs, later_at + part * later_pairs, gap)
        own_at += GROUP - gap
        later_at += gap
    for gap in range(SPAN + 1):
        pick(2 * SPAN + gap, 2 * own_pairs + gap, 2 * later_pairs, gap)

    lane = lax.broadcasted_iota(jnp.int32, (FIELDS, cols), 1)
    rows = [jnp.where(tile > 0, fields[k], 0.0) for k in range(half)]
    rows += [fields[half + k] for k in range(GROUP)]
    rows += [jnp.where(tile < tiles - 1, fields[half + GROUP + k], 0.0) for k in range(half)]
    for r in range(GROUP):
        tall = rows[r]
        for shift in range(1, WIN):
            tall = tall + rows[r + shift]
        boxed = tall
        for shift in range(1, half + 1):
            boxed = boxed + jnp.where(lane >= shift, pltpu.roll(tall, shift, 1), 0.0)
            boxed = boxed + jnp.where(lane < cols - shift, pltpu.roll(tall, cols - shift, 1), 0.0)
        real = boxed[:SPAN]
        imag = boxed[SPAN : 2 * SPAN]
        own = boxed[2 * SPAN : 2 * SPAN + 1]
        later = boxed[2 * SPAN + 1 :]
        value = jnp.sqrt(real * real + imag * imag) / jnp.sqrt(own * later + 1e-06)
        for gap in range(1, SPAN + 1):
            paired = date + gap < dates
            coher_ref[gap - 1, 0, r : r + 1, :] = jnp.where(paired, value[gap - 1 : gap], 0.0)
            for part in range(2):
                field = part * SPAN + gap - 1
                looks_ref[gap - 1, part, 0, r : r + 1, :] = jnp.where(paired, rows[r + half][field : field + 1], 0.0)


def finish(own, later):
    cols = own.shape[-1]
    rows = GROUP + 2 * (WIN // 2)
    return pl.pallas_call(
        coherence_kernel,
        in_specs=[pl.BlockSpec(memory_space=pl.ANY)] * 2,
        out_shape=(
            jax.ShapeDtypeStruct((SPAN, 2, 1, GROUP, cols), jnp.float32),
            jax.ShapeDtypeStruct((SPAN, 1, GROUP, cols), jnp.float32),
        ),
        scratch_shapes=[
            pltpu.VMEM((rows, OWN_ROWS, cols), jnp.float32),
            pltpu.VMEM((rows, LATER_ROWS, cols), jnp.float32),
            pltpu.VMEM((rows, FIELDS, cols), jnp.float32),
            pltpu.SemaphoreType.DMA((2 * rows,)),
        ],
        compiler_params=pltpu.CompilerParams(vmem_limit_bytes=LIMIT),
        name="finish",
    )(own, later)


def local(slabs):
    dates, tiles = lax.axis_size("date"), lax.axis_size("az")
    _, planes, lines, samples = slabs.shape
    cols = samples // LOOK_RG
    groups = [list(range(g, g + GROUP)) for g in range(0, dates, GROUP)]
    wide = [list(range(g * tiles, (g + GROUP) * tiles)) for g in range(0, dates, GROUP)]
    pieces = cut(slabs[0]).reshape(GROUP, LOOK_AZ * planes, SUB, samples // SUB)
    own = lax.all_to_all(pieces, "date", 0, 0, axis_index_groups=groups, tiled=True)
    back = [(i, i - GROUP) for i in range(GROUP, dates)]
    later = lax.ppermute(own[:SPAN], "date", back)
    mine = look(own_kernel, OWN_ROWS, cols, "look_own", own)
    mine = lax.all_gather(mine, ("date", "az"), axis_index_groups=wide)
    later, mine = lax.optimization_barrier((later, mine))
    theirs = look(later_kernel, LATER_ROWS, cols, "look_later", own, later)
    theirs = lax.all_gather(theirs, ("date", "az"), axis_index_groups=wide)
    return finish(mine, theirs)


def solution(mesh):
    in_specs = (P("date", None, "az", None),)
    out_specs = (P(None, None, "date", "az", None), P(None, "date", "az", None))
    return jax.shard_map(local, mesh=mesh, in_specs=in_specs, out_specs=out_specs, check_vma=False)
```

```python
import functools

import jax
import jax.numpy as jnp
from jax import lax
from jax.experimental import pallas as pl
from jax.experimental.pallas import tpu as pltpu
from jax.sharding import PartitionSpec as P

LOOK_AZ = 4
LOOK_RG = 16
WIN = 5
SPAN = 5
GROUP = 8
FIELDS = 3 * SPAN + 1
SUB = 16


def cut_kernel(slab_ref, out_ref, held, arrived):
    planes, lines, _ = slab_ref.shape
    width = out_ref.shape[-1]
    parts = [(plane, line) for line in range(0, lines, 8) for plane in range(planes)]
    copies = []
    for plane, line in parts:
        here = (plane, pl.ds(line, 8))
        copies.append(pltpu.make_async_copy(slab_ref.at[here], held.at[here], arrived.at[len(copies)]))
        copies[-1].start()
    for (plane, line), copy in zip(parts, copies):
        copy.wait()
        for block in range(SUB):
            part = held[plane, line : line + 8, block * width : (block + 1) * width]
            start = (line * planes + plane) * SUB + block
            out_ref[pl.ds(start, 8, stride=planes * SUB), :] = part


def cut(slab):
    planes, lines, samples = slab.shape
    rows = planes * lines * SUB
    slab = pltpu.with_memory_space_constraint(slab, pltpu.HBM)
    return pl.pallas_call(
        cut_kernel,
        in_specs=[pl.BlockSpec(memory_space=pl.ANY)],
        out_shape=jax.ShapeDtypeStruct((rows, samples // SUB), jnp.float32),
        scratch_shapes=[
            pltpu.VMEM(slab.shape, jnp.float32),
            pltpu.SemaphoreType.DMA((planes * lines // 8,)),
        ],
        compiler_params=pltpu.CompilerParams(vmem_limit_bytes=4 * 1024 * 1024),
        name="cut",
    )(slab)


def inside(index):
    return min(SPAN, GROUP - 1 - index)


def look_at(date, pairs, powers, sums, cols):
    width = sums.shape[-1]
    count = 0

    def put(terms):
        nonlocal count
        total = terms[0]
        for term in terms[1:]:
            total = total + term
        sums[count * SUB : (count + 1) * SUB, :] = total
        count += 1

    for index, gaps in pairs:
        real, imag = date(index)
        others = [date(index + gap) for gap in gaps]
        for other_real, other_imag in others:
            put([a * b for a, b in zip(real + imag, other_real + other_imag)])
        for other_real, other_imag in others:
            put([a * b - c * d for a, b, c, d in zip(imag, other_real, real, other_imag)])
    for index in powers:
        real, imag = date(index)
        put([v * v for v in real + imag])

    per_block = width // LOOK_RG
    sample = lax.broadcasted_iota(jnp.int32, (width, cols), 0)
    lane = lax.broadcasted_iota(jnp.int32, (width, cols), 1)
    weight = jnp.where(sample // LOOK_RG == lane % per_block, 1.0 / (LOOK_AZ * LOOK_RG), 0.0)
    looks = jnp.dot(
        sums[: count * SUB, :], weight, precision=lax.Precision.HIGHEST, preferred_element_type=jnp.float32
    )
    looks = looks.reshape(count, SUB, cols)
    block = lax.broadcasted_iota(jnp.int32, (1, SUB, cols), 1)
    lane = lax.broadcasted_iota(jnp.int32, (1, SUB, cols), 2)
    return jnp.sum(jnp.where(lane // per_block == block, looks, 0.0), axis=1)


def planes_of(ref, at):
    return [ref[at, 2 * k] for k in range(LOOK_AZ)], [ref[at, 2 * k + 1] for k in range(LOOK_AZ)]


OWN_PAIRS = [(d, range(1, inside(d) + 1)) for d in range(GROUP)]
LATER_PAIRS = [(d, range(inside(d) + 1, SPAN + 1)) for d in range(GROUP) if inside(d) < SPAN]
OWN_ROWS = sum(2 * len(gaps) for _, gaps in OWN_PAIRS)
LATER_ROWS = sum(2 * len(gaps) for _, gaps in LATER_PAIRS)


def own_kernel(own_ref, out_ref, sums):
    out_ref[...] = look_at(lambda d: planes_of(own_ref, d), OWN_PAIRS, range(GROUP), sums, out_ref.shape[-1])


def later_kernel(own_ref, later_ref, looks_ref, out_ref, sums, cells):
    def date(index):
        return planes_of(own_ref, index) if index < GROUP else planes_of(later_ref, index - GROUP)

    cells[...] = look_at(date, LATER_PAIRS, range(GROUP, GROUP + SPAN), sums, out_ref.shape[-1])
    own_at = later_at = 0
    for index in range(GROUP):
        near, far = inside(index), SPAN - inside(index)
        piece = out_ref.at[index, 0]
        for part in range(2):
            if near:
                piece[part * SPAN : part * SPAN + near, :] = looks_ref[own_at : own_at + near, :]
            if far:
                piece[part * SPAN + near : (part + 1) * SPAN, :] = cells[later_at : later_at + far, :]
            own_at += near
            later_at += far
        piece[2 * SPAN : 2 * SPAN + 1 + near, :] = looks_ref[OWN_ROWS + index : OWN_ROWS + index + 1 + near, :]
        if far:
            piece[2 * SPAN + 1 + near :, :] = cells[LATER_ROWS : LATER_ROWS + far, :]
        for tile in range(1, out_ref.shape[1]):
            out_ref[index, tile] = out_ref[index, 0]


def look_own(own, cols):
    rows = OWN_ROWS + GROUP
    return pl.pallas_call(
        own_kernel,
        out_shape=jax.ShapeDtypeStruct((rows, cols), jnp.float32),
        scratch_shapes=[pltpu.VMEM((rows * SUB, own.shape[-1]), jnp.float32)],
        compiler_params=pltpu.CompilerParams(vmem_limit_bytes=8 * 1024 * 1024),
        cost_estimate=pl.CostEstimate(
            flops=12 * rows * SUB * cols * cols, bytes_accessed=own.size * 4, transcendentals=0
        ),
        name="look_own",
    )(own)


def look_later(own, later, looks, tiles):
    cols = looks.shape[-1]
    rows = LATER_ROWS + SPAN
    return pl.pallas_call(
        later_kernel,
        out_shape=jax.ShapeDtypeStruct((GROUP, tiles, FIELDS, cols), jnp.float32),
        scratch_shapes=[
            pltpu.VMEM((rows * SUB, own.shape[-1]), jnp.float32),
            pltpu.VMEM((rows, cols), jnp.float32),
        ],
        compiler_params=pltpu.CompilerParams(vmem_limit_bytes=8 * 1024 * 1024),
        name="look_later",
    )(own, later, looks)


def coherence_kernel(tiles, rows_ref, looks_out, coher_out, looks_ref, values, coher_ref, sent):
    date, dates = lax.axis_index("date"), lax.axis_size("date")
    tile = lax.axis_index("az")
    cols = rows_ref.shape[-1]
    half = WIN // 2
    for gap in range(1, SPAN + 1):
        for part in range(2):
            start = tile * FIELDS + part * SPAN + gap - 1
            look = rows_ref[pl.ds(start, GROUP, stride=tiles * FIELDS), :]
            looks_ref[gap - 1, part, 0] = jnp.where(date + gap < dates, look, 0.0)
    looks_sent = pltpu.make_async_copy(looks_ref, looks_out, sent.at[0])
    looks_sent.start()

    lane = lax.broadcasted_iota(jnp.int32, (FIELDS, cols), 1)
    rows = []
    for offset in range(-half, GROUP + half):
        other = tile + offset // GROUP
        start = (offset % GROUP * tiles + jnp.clip(other, 0, tiles - 1)) * FIELDS
        row = rows_ref[pl.ds(pl.multiple_of(start, FIELDS), FIELDS), :]
        if not 0 <= offset < GROUP:
            row = jnp.where(jnp.logical_and(other >= 0, other < tiles), row, 0.0)
        rows.append(row)
    for r in range(GROUP):
        tall = rows[r]
        for shift in range(1, WIN):
            tall = tall + rows[r + shift]
        boxed = tall
        for shift in range(1, half + 1):
            boxed = boxed + jnp.where(lane >= shift, pltpu.roll(tall, shift, 1), 0.0)
            boxed = boxed + jnp.where(lane < cols - shift, pltpu.roll(tall, cols - shift, 1), 0.0)
        real = boxed[:SPAN]
        imag = boxed[SPAN : 2 * SPAN]
        own = boxed[2 * SPAN : 2 * SPAN + 1]
        later = boxed[2 * SPAN + 1 :]
        value = jnp.sqrt(real * real + imag * imag) / jnp.sqrt(own * later + 1e-06)
        values[r * GROUP : r * GROUP + SPAN, :] = value
    for gap in range(1, SPAN + 1):
        value = values[pl.ds(gap - 1, GROUP, stride=GROUP), :]
        coher_ref[gap - 1, 0] = jnp.where(date + gap < dates, value, 0.0)
    coher_sent = pltpu.make_async_copy(coher_ref, coher_out, sent.at[1])
    coher_sent.start()
    looks_sent.wait()
    coher_sent.wait()


def finish(rows, tiles):
    cols = rows.shape[-1]
    looks = (SPAN, 2, 1, GROUP, cols)
    coher = (SPAN, 1, GROUP, cols)
    return pl.pallas_call(
        functools.partial(coherence_kernel, tiles),
        out_shape=(jax.ShapeDtypeStruct(looks, jnp.float32), jax.ShapeDtypeStruct(coher, jnp.float32)),
        out_specs=(pl.BlockSpec(memory_space=pl.ANY), pl.BlockSpec(memory_space=pl.ANY)),
        scratch_shapes=[
            pltpu.VMEM(looks, jnp.float32),
            pltpu.VMEM((GROUP * GROUP, cols), jnp.float32),
            pltpu.VMEM(coher, jnp.float32),
            pltpu.SemaphoreType.DMA((2,)),
        ],
        compiler_params=pltpu.CompilerParams(vmem_limit_bytes=4 * 1024 * 1024),
        name="finish",
    )(rows)


def local(slabs):
    dates, tiles = lax.axis_size("date"), lax.axis_size("az")
    _, planes, lines, samples = slabs.shape
    cols = samples // LOOK_RG
    groups = [list(range(g, g + GROUP)) for g in range(0, dates, GROUP)]
    wide = [list(range(g * tiles, (g + GROUP) * tiles)) for g in range(0, dates, GROUP)]
    pieces = cut(slabs[0]).reshape(GROUP, LOOK_AZ * planes, SUB, samples // SUB)
    own = lax.all_to_all(pieces, "date", 0, 0, axis_index_groups=groups, tiled=True)
    back = [(i, i - GROUP) for i in range(GROUP, dates)]
    later = lax.ppermute(own[:SPAN], "date", back)
    fields = look_later(own, later, look_own(own, cols), tiles)
    fields = fields.reshape(GROUP * tiles, FIELDS, cols)
    rows = lax.all_to_all(fields, ("date", "az"), 0, 0, axis_index_groups=wide, tiled=True)
    return finish(rows.reshape(GROUP * tiles * FIELDS, cols), tiles)


def solution(mesh):
    in_specs = (P("date", None, "az", None),)
    out_specs = (P(None, None, "date", "az", None), P(None, "date", "az", None))
    return jax.shard_map(local, mesh=mesh, in_specs=in_specs, out_specs=out_specs, check_vma=False)
```

```python
import functools

import jax
import jax.numpy as jnp
from jax import lax
from jax.experimental import pallas as pl
from jax.experimental.pallas import tpu as pltpu
from jax.sharding import PartitionSpec as P

LOOK_AZ = 4
LOOK_RG = 16
WIN = 5
SPAN = 5
GROUP = 8
FIELDS = 3 * SPAN + 1
HALF = 8
SUB = 2 * HALF


def cut_kernel(slab_ref, first_ref, second_ref, held, arrived):
    planes, lines, _ = slab_ref.shape
    width = first_ref.shape[-1]
    parts = [(plane, line) for line in range(0, lines, 8) for plane in range(planes)]
    copies = []
    for plane, line in parts:
        here = (plane, pl.ds(line, 8))
        copies.append(pltpu.make_async_copy(slab_ref.at[here], held.at[here], arrived.at[len(copies)]))
        copies[-1].start()
    for (plane, line), copy in zip(parts, copies):
        copy.wait()
        for block in range(SUB):
            part = held[plane, line : line + 8, block * width : (block + 1) * width]
            out_ref = first_ref if block < HALF else second_ref
            start = (line * planes + plane) * HALF + block % HALF
            out_ref[pl.ds(start, 8, stride=planes * HALF), :] = part


def cut(slab):
    planes, lines, samples = slab.shape
    out = jax.ShapeDtypeStruct((planes * lines * HALF, samples // SUB), jnp.float32)
    slab = pltpu.with_memory_space_constraint(slab, pltpu.HBM)
    return pl.pallas_call(
        cut_kernel,
        in_specs=[pl.BlockSpec(memory_space=pl.ANY)],
        out_shape=(out, out),
        scratch_shapes=[
            pltpu.VMEM(slab.shape, jnp.float32),
            pltpu.SemaphoreType.DMA((planes * lines // 8,)),
        ],
        compiler_params=pltpu.CompilerParams(vmem_limit_bytes=4 * 1024 * 1024),
        name="cut",
    )(slab)


def inside(index):
    return min(SPAN, GROUP - 1 - index)


def look_at(date, pairs, powers, sums, cols):
    width = sums.shape[-1]
    count = 0

    def put(terms):
        nonlocal count
        total = terms[0]
        for term in terms[1:]:
            total = total + term
        sums[count * SUB : (count + 1) * SUB, :] = total
        count += 1

    for index, gaps in pairs:
        real, imag = date(index)
        others = [date(index + gap) for gap in gaps]
        for other_real, other_imag in others:
            put([a * b for a, b in zip(real + imag, other_real + other_imag)])
        for other_real, other_imag in others:
            put([a * b - c * d for a, b, c, d in zip(imag, other_real, real, other_imag)])
    for index in powers:
        real, imag = date(index)
        put([v * v for v in real + imag])

    per_block = width // LOOK_RG
    sample = lax.broadcasted_iota(jnp.int32, (width, cols), 0)
    lane = lax.broadcasted_iota(jnp.int32, (width, cols), 1)
    weight = jnp.where(sample // LOOK_RG == lane % per_block, 1.0 / (LOOK_AZ * LOOK_RG), 0.0)
    looks = jnp.dot(
        sums[: count * SUB, :], weight, precision=lax.Precision.HIGHEST, preferred_element_type=jnp.float32
    )
    looks = looks.reshape(count, SUB, cols)
    block = lax.broadcasted_iota(jnp.int32, (1, SUB, cols), 1)
    lane = lax.broadcasted_iota(jnp.int32, (1, SUB, cols), 2)
    return jnp.sum(jnp.where(lane // per_block == block, looks, 0.0), axis=1)


def planes_of(refs, at):
    lines = [jnp.concatenate([ref[at, k] for ref in refs], axis=0) for k in range(2 * LOOK_AZ)]
    return lines[0::2], lines[1::2]


OWN_PAIRS = [(d, range(1, inside(d) + 1)) for d in range(GROUP)]
LATER_PAIRS = [(d, range(inside(d) + 1, SPAN + 1)) for d in range(GROUP) if inside(d) < SPAN]
OWN_ROWS = sum(2 * len(gaps) for _, gaps in OWN_PAIRS)
LATER_ROWS = sum(2 * len(gaps) for _, gaps in LATER_PAIRS)


def own_kernel(first_ref, second_ref, out_ref, sums):
    out_ref[...] = look_at(lambda d: planes_of((first_ref, second_ref), d), OWN_PAIRS, range(GROUP), sums, out_ref.shape[-1])


def later_kernel(first_ref, second_ref, later_first_ref, later_second_ref, looks_ref, out_ref, sums, cells):
    def date(index):
        if index < GROUP:
            return planes_of((first_ref, second_ref), index)
        return planes_of((later_first_ref, later_second_ref), index - GROUP)

    cells[...] = look_at(date, LATER_PAIRS, range(GROUP, GROUP + SPAN), sums, out_ref.shape[-1])
    own_at = later_at = 0
    for index in range(GROUP):
        near, far = inside(index), SPAN - inside(index)
        piece = out_ref.at[index, 0]
        for part in range(2):
            if near:
                piece[part * SPAN : part * SPAN + near, :] = looks_ref[own_at : own_at + near, :]
            if far:
                piece[part * SPAN + near : (part + 1) * SPAN, :] = cells[later_at : later_at + far, :]
            own_at += near
            later_at += far
        piece[2 * SPAN : 2 * SPAN + 1 + near, :] = looks_ref[OWN_ROWS + index : OWN_ROWS + index + 1 + near, :]
        if far:
            piece[2 * SPAN + 1 + near :, :] = cells[LATER_ROWS : LATER_ROWS + far, :]
        for tile in range(1, out_ref.shape[1]):
            out_ref[index, tile] = out_ref[index, 0]


def look_own(own, cols):
    rows = OWN_ROWS + GROUP
    return pl.pallas_call(
        own_kernel,
        out_shape=jax.ShapeDtypeStruct((rows, cols), jnp.float32),
        scratch_shapes=[pltpu.VMEM((rows * SUB, own[0].shape[-1]), jnp.float32)],
        compiler_params=pltpu.CompilerParams(vmem_limit_bytes=8 * 1024 * 1024),
        cost_estimate=pl.CostEstimate(
            flops=12 * rows * SUB * cols * cols, bytes_accessed=own[0].size * 8, transcendentals=0
        ),
        name="look_own",
    )(*own)


def look_later(own, later, looks, tiles):
    cols = looks.shape[-1]
    rows = LATER_ROWS + SPAN
    return pl.pallas_call(
        later_kernel,
        out_shape=jax.ShapeDtypeStruct((GROUP, tiles, FIELDS, cols), jnp.float32),
        scratch_shapes=[
            pltpu.VMEM((rows * SUB, own[0].shape[-1]), jnp.float32),
            pltpu.VMEM((rows, cols), jnp.float32),
        ],
        compiler_params=pltpu.CompilerParams(vmem_limit_bytes=8 * 1024 * 1024),
        name="look_later",
    )(*own, *later, looks)


def coherence_kernel(tiles, rows_ref, looks_out, coher_out, looks_ref, values, coher_ref, sent):
    date, dates = lax.axis_index("date"), lax.axis_size("date")
    tile = lax.axis_index("az")
    cols = rows_ref.shape[-1]
    half = WIN // 2
    for gap in range(1, SPAN + 1):
        for part in range(2):
            start = tile * FIELDS + part * SPAN + gap - 1
            look = rows_ref[pl.ds(start, GROUP, stride=tiles * FIELDS), :]
            looks_ref[gap - 1, part, 0] = jnp.where(date + gap < dates, look, 0.0)
    looks_sent = pltpu.make_async_copy(looks_ref, looks_out, sent.at[0])
    looks_sent.start()

    lane = lax.broadcasted_iota(jnp.int32, (FIELDS, cols), 1)
    rows = []
    for offset in range(-half, GROUP + half):
        other = tile + offset // GROUP
        start = (offset % GROUP * tiles + jnp.clip(other, 0, tiles - 1)) * FIELDS
        row = rows_ref[pl.ds(pl.multiple_of(start, FIELDS), FIELDS), :]
        if not 0 <= offset < GROUP:
            row = jnp.where(jnp.logical_and(other >= 0, other < tiles), row, 0.0)
        rows.append(row)
    for r in range(GROUP):
        tall = rows[r]
        for shift in range(1, WIN):
            tall = tall + rows[r + shift]
        boxed = tall
        for shift in range(1, half + 1):
            boxed = boxed + jnp.where(lane >= shift, pltpu.roll(tall, shift, 1), 0.0)
            boxed = boxed + jnp.where(lane < cols - shift, pltpu.roll(tall, cols - shift, 1), 0.0)
        real = boxed[:SPAN]
        imag = boxed[SPAN : 2 * SPAN]
        own = boxed[2 * SPAN : 2 * SPAN + 1]
        later = boxed[2 * SPAN + 1 :]
        value = jnp.sqrt(real * real + imag * imag) / jnp.sqrt(own * later + 1e-06)
        values[r * GROUP : r * GROUP + SPAN, :] = value
    for gap in range(1, SPAN + 1):
        value = values[pl.ds(gap - 1, GROUP, stride=GROUP), :]
        coher_ref[gap - 1, 0] = jnp.where(date + gap < dates, value, 0.0)
    coher_sent = pltpu.make_async_copy(coher_ref, coher_out, sent.at[1])
    coher_sent.start()
    looks_sent.wait()
    coher_sent.wait()


def finish(rows, tiles):
    cols = rows.shape[-1]
    looks = (SPAN, 2, 1, GROUP, cols)
    coher = (SPAN, 1, GROUP, cols)
    return pl.pallas_call(
        functools.partial(coherence_kernel, tiles),
        out_shape=(jax.ShapeDtypeStruct(looks, jnp.float32), jax.ShapeDtypeStruct(coher, jnp.float32)),
        out_specs=(pl.BlockSpec(memory_space=pl.ANY), pl.BlockSpec(memory_space=pl.ANY)),
        scratch_shapes=[
            pltpu.VMEM(looks, jnp.float32),
            pltpu.VMEM((GROUP * GROUP, cols), jnp.float32),
            pltpu.VMEM(coher, jnp.float32),
            pltpu.SemaphoreType.DMA((2,)),
        ],
        compiler_params=pltpu.CompilerParams(vmem_limit_bytes=4 * 1024 * 1024),
        name="finish",
    )(rows)


def local(slabs):
    dates, tiles = lax.axis_size("date"), lax.axis_size("az")
    _, planes, lines, samples = slabs.shape
    cols = samples // LOOK_RG
    groups = [list(range(g, g + GROUP)) for g in range(0, dates, GROUP)]
    wide = [list(range(g * tiles, (g + GROUP) * tiles)) for g in range(0, dates, GROUP)]
    pieces = [half.reshape(GROUP, LOOK_AZ * planes, HALF, samples // SUB) for half in cut(slabs[0])]
    own = [lax.all_to_all(half, "date", 0, 0, axis_index_groups=groups, tiled=True) for half in pieces]
    back = [(i, i - GROUP) for i in range(GROUP, dates)]
    later = [lax.ppermute(half[:SPAN], "date", back) for half in own]
    fields = look_later(own, later, look_own(own, cols), tiles)
    fields = fields.reshape(GROUP * tiles, FIELDS, cols)
    rows = lax.all_to_all(fields, ("date", "az"), 0, 0, axis_index_groups=wide, tiled=True)
    return finish(rows.reshape(GROUP * tiles * FIELDS, cols), tiles)


def solution(mesh):
    in_specs = (P("date", None, "az", None),)
    out_specs = (P(None, None, "date", "az", None), P(None, "date", "az", None))
    return jax.shard_map(local, mesh=mesh, in_specs=in_specs, out_specs=out_specs, check_vma=False)
```

```python
import functools

import jax
import jax.numpy as jnp
from jax import lax
from jax.experimental import pallas as pl
from jax.experimental.pallas import tpu as pltpu
from jax.sharding import PartitionSpec as P

LOOK_AZ = 4
LOOK_RG = 16
WIN = 5
SPAN = 5
GROUP = 8
FIELDS = 3 * SPAN + 1
SUB = 16


def cut_kernel(slab_ref, out_ref, held, arrived):
    planes, lines, _ = slab_ref.shape
    width = out_ref.shape[-1]
    parts = [(plane, line) for line in range(0, lines, 8) for plane in range(planes)]
    copies = []
    for plane, line in parts:
        here = (plane, pl.ds(line, 8))
        copies.append(pltpu.make_async_copy(slab_ref.at[here], held.at[here], arrived.at[len(copies)]))
        copies[-1].start()
    for (plane, line), copy in zip(parts, copies):
        copy.wait()
        for block in range(SUB):
            part = held[plane, line : line + 8, block * width : (block + 1) * width]
            start = (line * planes + plane) * SUB + block
            out_ref[pl.ds(start, 8, stride=planes * SUB), :] = part


def cut(slab):
    planes, lines, samples = slab.shape
    rows = planes * lines * SUB
    slab = pltpu.with_memory_space_constraint(slab, pltpu.HBM)
    return pl.pallas_call(
        cut_kernel,
        in_specs=[pl.BlockSpec(memory_space=pl.ANY)],
        out_shape=jax.ShapeDtypeStruct((rows, samples // SUB), jnp.float32),
        scratch_shapes=[
            pltpu.VMEM(slab.shape, jnp.float32),
            pltpu.SemaphoreType.DMA((planes * lines // 8,)),
        ],
        compiler_params=pltpu.CompilerParams(vmem_limit_bytes=4 * 1024 * 1024),
        name="cut",
    )(slab)


def inside(index):
    return min(SPAN, GROUP - 1 - index)


def look_at(date, pairs, powers, sums, cols):
    width = sums.shape[-1]
    count = 0

    def put(terms):
        nonlocal count
        total = terms[0]
        for term in terms[1:]:
            total = total + term
        sums[count * SUB : (count + 1) * SUB, :] = total
        count += 1

    for index, gaps in pairs:
        real, imag = date(index)
        others = [date(index + gap) for gap in gaps]
        for other_real, other_imag in others:
            put([a * b for a, b in zip(real + imag, other_real + other_imag)])
        for other_real, other_imag in others:
            put([a * b - c * d for a, b, c, d in zip(imag, other_real, real, other_imag)])
    for index in powers:
        real, imag = date(index)
        put([v * v for v in real + imag])

    per_block = width // LOOK_RG
    sample = lax.broadcasted_iota(jnp.int32, (width, cols), 0)
    lane = lax.broadcasted_iota(jnp.int32, (width, cols), 1)
    weight = jnp.where(sample // LOOK_RG == lane % per_block, 1.0 / (LOOK_AZ * LOOK_RG), 0.0)
    looks = jnp.dot(
        sums[: count * SUB, :], weight, precision=lax.Precision.HIGHEST, preferred_element_type=jnp.float32
    )
    looks = looks.reshape(count, SUB, cols)
    block = lax.broadcasted_iota(jnp.int32, (1, SUB, cols), 1)
    lane = lax.broadcasted_iota(jnp.int32, (1, SUB, cols), 2)
    return jnp.sum(jnp.where(lane // per_block == block, looks, 0.0), axis=1)


def planes_of(ref, at):
    return [ref[at, 2 * k] for k in range(LOOK_AZ)], [ref[at, 2 * k + 1] for k in range(LOOK_AZ)]


OWN_PAIRS = [(d, range(1, inside(d) + 1)) for d in range(GROUP)]
LATER_PAIRS = [(d, range(inside(d) + 1, SPAN + 1)) for d in range(GROUP) if inside(d) < SPAN]
OWN_ROWS = sum(2 * len(gaps) for _, gaps in OWN_PAIRS)
LATER_ROWS = sum(2 * len(gaps) for _, gaps in LATER_PAIRS)


def own_kernel(own_ref, out_ref, sums):
    out_ref[...] = look_at(lambda d: planes_of(own_ref, d), OWN_PAIRS, range(GROUP), sums, out_ref.shape[-1])


def later_kernel(own_ref, later_ref, looks_ref, out_ref, sums, cells):
    def date(index):
        return planes_of(own_ref, index) if index < GROUP else planes_of(later_ref, index - GROUP)

    cells[...] = look_at(date, LATER_PAIRS, range(GROUP, GROUP + SPAN), sums, out_ref.shape[-1])
    own_at = later_at = 0
    for index in range(GROUP):
        near, far = inside(index), SPAN - inside(index)
        piece = out_ref.at[0, index]
        for part in range(2):
            if near:
                piece[part * SPAN : part * SPAN + near, :] = looks_ref[own_at : own_at + near, :]
            if far:
                piece[part * SPAN + near : (part + 1) * SPAN, :] = cells[later_at : later_at + far, :]
            own_at += near
            later_at += far
        piece[2 * SPAN : 2 * SPAN + 1 + near, :] = looks_ref[OWN_ROWS + index : OWN_ROWS + index + 1 + near, :]
        if far:
            piece[2 * SPAN + 1 + near :, :] = cells[LATER_ROWS : LATER_ROWS + far, :]
        for tile in range(1, out_ref.shape[0]):
            out_ref[tile, index] = out_ref[0, index]


def look_own(own, cols):
    rows = OWN_ROWS + GROUP
    return pl.pallas_call(
        own_kernel,
        out_shape=jax.ShapeDtypeStruct((rows, cols), jnp.float32),
        scratch_shapes=[pltpu.VMEM((rows * SUB, own.shape[-1]), jnp.float32)],
        compiler_params=pltpu.CompilerParams(vmem_limit_bytes=8 * 1024 * 1024),
        cost_estimate=pl.CostEstimate(
            flops=12 * rows * SUB * cols * cols, bytes_accessed=own.size * 4, transcendentals=0
        ),
        name="look_own",
    )(own)


def look_later(own, later, looks, tiles):
    cols = looks.shape[-1]
    rows = LATER_ROWS + SPAN
    return pl.pallas_call(
        later_kernel,
        out_shape=jax.ShapeDtypeStruct((tiles, GROUP, FIELDS, cols), jnp.float32),
        scratch_shapes=[
            pltpu.VMEM((rows * SUB, own.shape[-1]), jnp.float32),
            pltpu.VMEM((rows, cols), jnp.float32),
        ],
        compiler_params=pltpu.CompilerParams(vmem_limit_bytes=8 * 1024 * 1024),
        name="look_later",
    )(own, later, looks)


def coherence_kernel(tiles, rows_ref, looks_out, coher_out, looks_ref, values, coher_ref, sent):
    date, dates = lax.axis_index("date"), lax.axis_size("date")
    tile = lax.axis_index("az")
    cols = rows_ref.shape[-1]
    half = WIN // 2
    for gap in range(1, SPAN + 1):
        for part in range(2):
            start = tile * (GROUP * FIELDS) + part * SPAN + gap - 1
            look = rows_ref[pl.ds(start, GROUP, stride=FIELDS), :]
            looks_ref[gap - 1, part, 0] = jnp.where(date + gap < dates, look, 0.0)
    looks_sent = pltpu.make_async_copy(looks_ref, looks_out, sent.at[0])
    looks_sent.start()

    lane = lax.broadcasted_iota(jnp.int32, (FIELDS, cols), 1)
    rows = []
    for offset in range(-half, GROUP + half):
        other = tile + offset // GROUP
        start = (jnp.clip(other, 0, tiles - 1) * GROUP + offset % GROUP) * FIELDS
        row = rows_ref[pl.ds(pl.multiple_of(start, FIELDS), FIELDS), :]
        if not 0 <= offset < GROUP:
            row = jnp.where(jnp.logical_and(other >= 0, other < tiles), row, 0.0)
        rows.append(row)
    for r in range(GROUP):
        tall = rows[r]
        for shift in range(1, WIN):
            tall = tall + rows[r + shift]
        boxed = tall
        for shift in range(1, half + 1):
            boxed = boxed + jnp.where(lane >= shift, pltpu.roll(tall, shift, 1), 0.0)
            boxed = boxed + jnp.where(lane < cols - shift, pltpu.roll(tall, cols - shift, 1), 0.0)
        real = boxed[:SPAN]
        imag = boxed[SPAN : 2 * SPAN]
        own = boxed[2 * SPAN : 2 * SPAN + 1]
        later = boxed[2 * SPAN + 1 :]
        value = jnp.sqrt(real * real + imag * imag) / jnp.sqrt(own * later + 1e-06)
        values[r * GROUP : r * GROUP + SPAN, :] = value
    for gap in range(1, SPAN + 1):
        value = values[pl.ds(gap - 1, GROUP, stride=GROUP), :]
        coher_ref[gap - 1, 0] = jnp.where(date + gap < dates, value, 0.0)
    coher_sent = pltpu.make_async_copy(coher_ref, coher_out, sent.at[1])
    coher_sent.start()
    looks_sent.wait()
    coher_sent.wait()


def finish(rows, tiles):
    cols = rows.shape[-1]
    looks = (SPAN, 2, 1, GROUP, cols)
    coher = (SPAN, 1, GROUP, cols)
    return pl.pallas_call(
        functools.partial(coherence_kernel, tiles),
        out_shape=(jax.ShapeDtypeStruct(looks, jnp.float32), jax.ShapeDtypeStruct(coher, jnp.float32)),
        out_specs=(pl.BlockSpec(memory_space=pl.ANY), pl.BlockSpec(memory_space=pl.ANY)),
        scratch_shapes=[
            pltpu.VMEM(looks, jnp.float32),
            pltpu.VMEM((GROUP * GROUP, cols), jnp.float32),
            pltpu.VMEM(coher, jnp.float32),
            pltpu.SemaphoreType.DMA((2,)),
        ],
        compiler_params=pltpu.CompilerParams(vmem_limit_bytes=4 * 1024 * 1024),
        name="finish",
    )(rows)


def local(slabs):
    dates, tiles = lax.axis_size("date"), lax.axis_size("az")
    _, planes, lines, samples = slabs.shape
    cols = samples // LOOK_RG
    groups = [list(range(g, g + GROUP)) for g in range(0, dates, GROUP)]
    wide = [[(g + d) * tiles + a for a in range(tiles) for d in range(GROUP)] for g in range(0, dates, GROUP)]
    pieces = cut(slabs[0]).reshape(GROUP, LOOK_AZ * planes, SUB, samples // SUB)
    own = lax.all_to_all(pieces, "date", 0, 0, axis_index_groups=groups, tiled=True)
    back = [(i, i - GROUP) for i in range(GROUP, dates)]
    later = lax.ppermute(own[:SPAN], "date", back)
    fields = look_later(own, later, look_own(own, cols), tiles)
    fields = fields.reshape(GROUP * tiles, FIELDS, cols)
    rows = lax.all_to_all(fields, ("date", "az"), 0, 0, axis_index_groups=wide, tiled=True)
    return finish(rows.reshape(GROUP * tiles * FIELDS, cols), tiles)


def solution(mesh):
    in_specs = (P("date", None, "az", None),)
    out_specs = (P(None, None, "date", "az", None), P(None, "date", "az", None))
    return jax.shard_map(local, mesh=mesh, in_specs=in_specs, out_specs=out_specs, check_vma=False)
```

```python
import functools

import jax
import jax.numpy as jnp
from jax import lax
from jax.experimental import pallas as pl
from jax.experimental.pallas import tpu as pltpu
from jax.sharding import PartitionSpec as P

LOOK_AZ = 4
LOOK_RG = 16
WIN = 5
SPAN = 5
GROUP = 8
FIELDS = 3 * SPAN + 1
NEAR = 3
SUB = 16


def cut_kernel(slab_ref, out_ref, held, arrived):
    planes, lines, _ = slab_ref.shape
    width = out_ref.shape[-1]
    parts = [(plane, line) for line in range(0, lines, 8) for plane in range(planes)]
    copies = []
    for plane, line in parts:
        here = (plane, pl.ds(line, 8))
        copies.append(pltpu.make_async_copy(slab_ref.at[here], held.at[here], arrived.at[len(copies)]))
        copies[-1].start()
    for (plane, line), copy in zip(parts, copies):
        copy.wait()
        for block in range(SUB):
            part = held[plane, line : line + 8, block * width : (block + 1) * width]
            start = (line * planes + plane) * SUB + block
            out_ref[pl.ds(start, 8, stride=planes * SUB), :] = part


def cut(slab):
    planes, lines, samples = slab.shape
    rows = planes * lines * SUB
    slab = pltpu.with_memory_space_constraint(slab, pltpu.HBM)
    return pl.pallas_call(
        cut_kernel,
        in_specs=[pl.BlockSpec(memory_space=pl.ANY)],
        out_shape=jax.ShapeDtypeStruct((rows, samples // SUB), jnp.float32),
        scratch_shapes=[
            pltpu.VMEM(slab.shape, jnp.float32),
            pltpu.SemaphoreType.DMA((planes * lines // 8,)),
        ],
        compiler_params=pltpu.CompilerParams(vmem_limit_bytes=4 * 1024 * 1024),
        name="cut",
    )(slab)


def inside(index):
    return min(SPAN, GROUP - 1 - index)


def look_at(date, pairs, powers, sums, cols):
    width = sums.shape[-1]
    count = 0

    def put(terms):
        nonlocal count
        total = terms[0]
        for term in terms[1:]:
            total = total + term
        sums[count * SUB : (count + 1) * SUB, :] = total
        count += 1

    for index, gaps in pairs:
        real, imag = date(index)
        others = [date(index + gap) for gap in gaps]
        for other_real, other_imag in others:
            put([a * b for a, b in zip(real + imag, other_real + other_imag)])
        for other_real, other_imag in others:
            put([a * b - c * d for a, b, c, d in zip(imag, other_real, real, other_imag)])
    for index in powers:
        real, imag = date(index)
        put([v * v for v in real + imag])

    per_block = width // LOOK_RG
    sample = lax.broadcasted_iota(jnp.int32, (width, cols), 0)
    lane = lax.broadcasted_iota(jnp.int32, (width, cols), 1)
    weight = jnp.where(sample // LOOK_RG == lane % per_block, 1.0 / (LOOK_AZ * LOOK_RG), 0.0)
    looks = jnp.dot(
        sums[: count * SUB, :], weight, precision=lax.Precision.HIGHEST, preferred_element_type=jnp.float32
    )
    looks = looks.reshape(count, SUB, cols)
    block = lax.broadcasted_iota(jnp.int32, (1, SUB, cols), 1)
    lane = lax.broadcasted_iota(jnp.int32, (1, SUB, cols), 2)
    return jnp.sum(jnp.where(lane // per_block == block, looks, 0.0), axis=1)


def planes_of(ref, at):
    return [ref[at, 2 * k] for k in range(LOOK_AZ)], [ref[at, 2 * k + 1] for k in range(LOOK_AZ)]


OWN_PAIRS = [(d, range(1, inside(d) + 1)) for d in range(GROUP)]
LATER_PAIRS = [(d, range(inside(d) + 1, SPAN + 1)) for d in range(GROUP) if inside(d) < SPAN]
OWN_ROWS = sum(2 * len(gaps) for _, gaps in OWN_PAIRS)
LATER_ROWS = sum(2 * len(gaps) for _, gaps in LATER_PAIRS)


def own_kernel(own_ref, out_ref, sums):
    out_ref[...] = look_at(lambda d: planes_of(own_ref, d), OWN_PAIRS, range(GROUP), sums, out_ref.shape[-1])


def later_kernel(own_ref, near_ref, far_ref, looks_ref, out_ref, sums, cells):
    def date(index):
        if index < GROUP:
            return planes_of(own_ref, index)
        return planes_of(near_ref, index - GROUP) if index < GROUP + NEAR else planes_of(far_ref, index - GROUP - NEAR)

    cells[...] = look_at(date, LATER_PAIRS, range(GROUP, GROUP + SPAN), sums, out_ref.shape[-1])
    own_at = later_at = 0
    for index in range(GROUP):
        near, far = inside(index), SPAN - inside(index)
        piece = out_ref.at[index, 0]
        for part in range(2):
            if near:
                piece[part * SPAN : part * SPAN + near, :] = looks_ref[own_at : own_at + near, :]
            if far:
                piece[part * SPAN + near : (part + 1) * SPAN, :] = cells[later_at : later_at + far, :]
            own_at += near
            later_at += far
        piece[2 * SPAN : 2 * SPAN + 1 + near, :] = looks_ref[OWN_ROWS + index : OWN_ROWS + index + 1 + near, :]
        if far:
            piece[2 * SPAN + 1 + near :, :] = cells[LATER_ROWS : LATER_ROWS + far, :]
        for tile in range(1, out_ref.shape[1]):
            out_ref[index, tile] = out_ref[index, 0]


def look_own(own, cols):
    rows = OWN_ROWS + GROUP
    return pl.pallas_call(
        own_kernel,
        out_shape=jax.ShapeDtypeStruct((rows, cols), jnp.float32),
        scratch_shapes=[pltpu.VMEM((rows * SUB, own.shape[-1]), jnp.float32)],
        compiler_params=pltpu.CompilerParams(vmem_limit_bytes=8 * 1024 * 1024),
        cost_estimate=pl.CostEstimate(
            flops=12 * rows * SUB * cols * cols, bytes_accessed=own.size * 4, transcendentals=0
        ),
        name="look_own",
    )(own)


def look_later(own, later, looks, tiles):
    cols = looks.shape[-1]
    rows = LATER_ROWS + SPAN
    return pl.pallas_call(
        later_kernel,
        out_shape=jax.ShapeDtypeStruct((GROUP, tiles, FIELDS, cols), jnp.float32),
        scratch_shapes=[
            pltpu.VMEM((rows * SUB, own.shape[-1]), jnp.float32),
            pltpu.VMEM((rows, cols), jnp.float32),
        ],
        compiler_params=pltpu.CompilerParams(vmem_limit_bytes=8 * 1024 * 1024),
        name="look_later",
    )(own, *later, looks)


def coherence_kernel(tiles, rows_ref, looks_out, coher_out, looks_ref, values, coher_ref, sent):
    date, dates = lax.axis_index("date"), lax.axis_size("date")
    tile = lax.axis_index("az")
    cols = rows_ref.shape[-1]
    half = WIN // 2
    for gap in range(1, SPAN + 1):
        for part in range(2):
            start = tile * FIELDS + part * SPAN + gap - 1
            look = rows_ref[pl.ds(start, GROUP, stride=tiles * FIELDS), :]
            looks_ref[gap - 1, part, 0] = jnp.where(date + gap < dates, look, 0.0)
    looks_sent = pltpu.make_async_copy(looks_ref, looks_out, sent.at[0])
    looks_sent.start()

    lane = lax.broadcasted_iota(jnp.int32, (FIELDS, cols), 1)
    rows = []
    for offset in range(-half, GROUP + half):
        other = tile + offset // GROUP
        start = (offset % GROUP * tiles + jnp.clip(other, 0, tiles - 1)) * FIELDS
        row = rows_ref[pl.ds(pl.multiple_of(start, FIELDS), FIELDS), :]
        if not 0 <= offset < GROUP:
            row = jnp.where(jnp.logical_and(other >= 0, other < tiles), row, 0.0)
        rows.append(row)
    for r in range(GROUP):
        tall = rows[r]
        for shift in range(1, WIN):
            tall = tall + rows[r + shift]
        boxed = tall
        for shift in range(1, half + 1):
            boxed = boxed + jnp.where(lane >= shift, pltpu.roll(tall, shift, 1), 0.0)
            boxed = boxed + jnp.where(lane < cols - shift, pltpu.roll(tall, cols - shift, 1), 0.0)
        real = boxed[:SPAN]
        imag = boxed[SPAN : 2 * SPAN]
        own = boxed[2 * SPAN : 2 * SPAN + 1]
        later = boxed[2 * SPAN + 1 :]
        value = jnp.sqrt(real * real + imag * imag) / jnp.sqrt(own * later + 1e-06)
        values[r * GROUP : r * GROUP + SPAN, :] = value
    for gap in range(1, SPAN + 1):
        value = values[pl.ds(gap - 1, GROUP, stride=GROUP), :]
        coher_ref[gap - 1, 0] = jnp.where(date + gap < dates, value, 0.0)
    coher_sent = pltpu.make_async_copy(coher_ref, coher_out, sent.at[1])
    coher_sent.start()
    looks_sent.wait()
    coher_sent.wait()


def finish(rows, tiles):
    cols = rows.shape[-1]
    looks = (SPAN, 2, 1, GROUP, cols)
    coher = (SPAN, 1, GROUP, cols)
    return pl.pallas_call(
        functools.partial(coherence_kernel, tiles),
        out_shape=(jax.ShapeDtypeStruct(looks, jnp.float32), jax.ShapeDtypeStruct(coher, jnp.float32)),
        out_specs=(pl.BlockSpec(memory_space=pl.ANY), pl.BlockSpec(memory_space=pl.ANY)),
        scratch_shapes=[
            pltpu.VMEM(looks, jnp.float32),
            pltpu.VMEM((GROUP * GROUP, cols), jnp.float32),
            pltpu.VMEM(coher, jnp.float32),
            pltpu.SemaphoreType.DMA((2,)),
        ],
        compiler_params=pltpu.CompilerParams(vmem_limit_bytes=4 * 1024 * 1024),
        name="finish",
    )(rows)


def local(slabs):
    dates, tiles = lax.axis_size("date"), lax.axis_size("az")
    _, planes, lines, samples = slabs.shape
    cols = samples // LOOK_RG
    groups = [list(range(g, g + GROUP)) for g in range(0, dates, GROUP)]
    wide = [list(range(g * tiles, (g + GROUP) * tiles)) for g in range(0, dates, GROUP)]
    pieces = cut(slabs[0]).reshape(GROUP, LOOK_AZ * planes, SUB, samples // SUB)
    own = lax.all_to_all(pieces, "date", 0, 0, axis_index_groups=groups, tiled=True)
    back = [(i, i - GROUP) for i in range(GROUP, dates)]
    later = [lax.ppermute(part, "date", back) for part in (own[:NEAR], own[NEAR:SPAN])]
    fields = look_later(own, later, look_own(own, cols), tiles)
    fields = fields.reshape(GROUP * tiles, FIELDS, cols)
    rows = lax.all_to_all(fields, ("date", "az"), 0, 0, axis_index_groups=wide, tiled=True)
    return finish(rows.reshape(GROUP * tiles * FIELDS, cols), tiles)


def solution(mesh):
    in_specs = (P("date", None, "az", None),)
    out_specs = (P(None, None, "date", "az", None), P(None, "date", "az", None))
    return jax.shard_map(local, mesh=mesh, in_specs=in_specs, out_specs=out_specs, check_vma=False)
```

```python
import functools

import jax
import jax.numpy as jnp
from jax import lax
from jax.experimental import pallas as pl
from jax.experimental.pallas import tpu as pltpu
from jax.sharding import PartitionSpec as P

LOOK_AZ = 4
LOOK_RG = 16
WIN = 5
SPAN = 5
GROUP = 8
FIELDS = 3 * SPAN + 1
SUB = 16


def cut_kernel(slab_ref, out_ref, held, arrived):
    planes, lines, _ = slab_ref.shape
    width = out_ref.shape[-1]
    parts = [(plane, line) for line in range(0, lines, 8) for plane in range(planes)]
    copies = []
    for plane, line in parts:
        here = (plane, pl.ds(line, 8))
        copies.append(pltpu.make_async_copy(slab_ref.at[here], held.at[here], arrived.at[len(copies)]))
        copies[-1].start()
    for (plane, line), copy in zip(parts, copies):
        copy.wait()
        for block in range(SUB):
            part = held[plane, line : line + 8, block * width : (block + 1) * width]
            start = (line * planes + plane) * SUB + block
            out_ref[pl.ds(start, 8, stride=planes * SUB), :] = part


def cut(slab):
    planes, lines, samples = slab.shape
    rows = planes * lines * SUB
    slab = pltpu.with_memory_space_constraint(slab, pltpu.HBM)
    return pl.pallas_call(
        cut_kernel,
        in_specs=[pl.BlockSpec(memory_space=pl.ANY)],
        out_shape=jax.ShapeDtypeStruct((rows, samples // SUB), jnp.float32),
        scratch_shapes=[
            pltpu.VMEM(slab.shape, jnp.float32),
            pltpu.SemaphoreType.DMA((planes * lines // 8,)),
        ],
        compiler_params=pltpu.CompilerParams(vmem_limit_bytes=4 * 1024 * 1024),
        name="cut",
    )(slab)


def inside(index):
    return min(SPAN, GROUP - 1 - index)


def look_at(date, pairs, powers, sums, cols):
    width = sums.shape[-1]
    count = 0

    def put(terms):
        nonlocal count
        total = terms[0]
        for term in terms[1:]:
            total = total + term
        sums[count * SUB : (count + 1) * SUB, :] = total
        count += 1

    for index, gaps in pairs:
        real, imag = date(index)
        others = [date(index + gap) for gap in gaps]
        for other_real, other_imag in others:
            put([a * b for a, b in zip(real + imag, other_real + other_imag)])
        for other_real, other_imag in others:
            put([a * b - c * d for a, b, c, d in zip(imag, other_real, real, other_imag)])
    for index in powers:
        real, imag = date(index)
        put([v * v for v in real + imag])

    per_block = width // LOOK_RG
    sample = lax.broadcasted_iota(jnp.int32, (width, cols), 0)
    lane = lax.broadcasted_iota(jnp.int32, (width, cols), 1)
    weight = jnp.where(sample // LOOK_RG == lane % per_block, 1.0 / (LOOK_AZ * LOOK_RG), 0.0)
    looks = jnp.dot(
        sums[: count * SUB, :], weight, precision=lax.Precision.HIGHEST, preferred_element_type=jnp.float32
    )
    looks = looks.reshape(count, SUB, cols)
    block = lax.broadcasted_iota(jnp.int32, (1, SUB, cols), 1)
    lane = lax.broadcasted_iota(jnp.int32, (1, SUB, cols), 2)
    return jnp.sum(jnp.where(lane // per_block == block, looks, 0.0), axis=1)


def planes_of(ref, at):
    return [ref[at, 2 * k] for k in range(LOOK_AZ)], [ref[at, 2 * k + 1] for k in range(LOOK_AZ)]


OWN_PAIRS = [(d, range(1, inside(d) + 1)) for d in range(GROUP)]
LATER_PAIRS = [(d, range(inside(d) + 1, SPAN + 1)) for d in range(GROUP) if inside(d) < SPAN]
OWN_ROWS = sum(2 * len(gaps) for _, gaps in OWN_PAIRS)
LATER_ROWS = sum(2 * len(gaps) for _, gaps in LATER_PAIRS)


def own_kernel(own_ref, out_ref, sums):
    out_ref[...] = look_at(lambda d: planes_of(own_ref, d), OWN_PAIRS, range(GROUP), sums, out_ref.shape[-1])


def later_kernel(own_ref, later_ref, looks_ref, out_ref, sums, cells):
    def date(index):
        return planes_of(own_ref, index) if index < GROUP else planes_of(later_ref, index - GROUP)

    cells[...] = look_at(date, LATER_PAIRS, range(GROUP, GROUP + SPAN), sums, out_ref.shape[-1])
    own_at = later_at = 0
    for index in range(GROUP):
        near, far = inside(index), SPAN - inside(index)
        piece = out_ref.at[index]
        for part in range(2):
            if near:
                piece[part * SPAN : part * SPAN + near, :] = looks_ref[own_at : own_at + near, :]
            if far:
                piece[part * SPAN + near : (part + 1) * SPAN, :] = cells[later_at : later_at + far, :]
            own_at += near
            later_at += far
        piece[2 * SPAN : 2 * SPAN + 1 + near, :] = looks_ref[OWN_ROWS + index : OWN_ROWS + index + 1 + near, :]
        if far:
            piece[2 * SPAN + 1 + near :, :] = cells[LATER_ROWS : LATER_ROWS + far, :]


def look_own(own, cols):
    rows = OWN_ROWS + GROUP
    return pl.pallas_call(
        own_kernel,
        out_shape=jax.ShapeDtypeStruct((rows, cols), jnp.float32),
        scratch_shapes=[pltpu.VMEM((rows * SUB, own.shape[-1]), jnp.float32)],
        compiler_params=pltpu.CompilerParams(vmem_limit_bytes=8 * 1024 * 1024),
        cost_estimate=pl.CostEstimate(
            flops=12 * rows * SUB * cols * cols, bytes_accessed=own.size * 4, transcendentals=0
        ),
        name="look_own",
    )(own)


def look_later(own, later, looks):
    cols = looks.shape[-1]
    rows = LATER_ROWS + SPAN
    return pl.pallas_call(
        later_kernel,
        out_shape=jax.ShapeDtypeStruct((GROUP, FIELDS, cols), jnp.float32),
        scratch_shapes=[
            pltpu.VMEM((rows * SUB, own.shape[-1]), jnp.float32),
            pltpu.VMEM((rows, cols), jnp.float32),
        ],
        compiler_params=pltpu.CompilerParams(vmem_limit_bytes=8 * 1024 * 1024),
        name="look_later",
    )(own, later, looks)


def coherence_kernel(tiles, rows_ref, looks_out, coher_out, looks_ref, values, coher_ref, sent):
    date, dates = lax.axis_index("date"), lax.axis_size("date")
    tile = lax.axis_index("az")
    cols = rows_ref.shape[-1]
    half = WIN // 2
    for gap in range(1, SPAN + 1):
        for part in range(2):
            start = tile * (GROUP * FIELDS) + part * SPAN + gap - 1
            look = rows_ref[pl.ds(start, GROUP, stride=FIELDS), :]
            looks_ref[gap - 1, part, 0] = jnp.where(date + gap < dates, look, 0.0)
    looks_sent = pltpu.make_async_copy(looks_ref, looks_out, sent.at[0])
    looks_sent.start()

    lane = lax.broadcasted_iota(jnp.int32, (FIELDS, cols), 1)
    rows = []
    for offset in range(-half, GROUP + half):
        other = tile + offset // GROUP
        start = (jnp.clip(other, 0, tiles - 1) * GROUP + offset % GROUP) * FIELDS
        row = rows_ref[pl.ds(pl.multiple_of(start, FIELDS), FIELDS), :]
        if not 0 <= offset < GROUP:
            row = jnp.where(jnp.logical_and(other >= 0, other < tiles), row, 0.0)
        rows.append(row)
    for r in range(GROUP):
        tall = rows[r]
        for shift in range(1, WIN):
            tall = tall + rows[r + shift]
        boxed = tall
        for shift in range(1, half + 1):
            boxed = boxed + jnp.where(lane >= shift, pltpu.roll(tall, shift, 1), 0.0)
            boxed = boxed + jnp.where(lane < cols - shift, pltpu.roll(tall, cols - shift, 1), 0.0)
        real = boxed[:SPAN]
        imag = boxed[SPAN : 2 * SPAN]
        own = boxed[2 * SPAN : 2 * SPAN + 1]
        later = boxed[2 * SPAN + 1 :]
        value = jnp.sqrt(real * real + imag * imag) / jnp.sqrt(own * later + 1e-06)
        values[r * GROUP : r * GROUP + SPAN, :] = value
    for gap in range(1, SPAN + 1):
        value = values[pl.ds(gap - 1, GROUP, stride=GROUP), :]
        coher_ref[gap - 1, 0] = jnp.where(date + gap < dates, value, 0.0)
    coher_sent = pltpu.make_async_copy(coher_ref, coher_out, sent.at[1])
    coher_sent.start()
    looks_sent.wait()
    coher_sent.wait()


def finish(rows, tiles):
    cols = rows.shape[-1]
    looks = (SPAN, 2, 1, GROUP, cols)
    coher = (SPAN, 1, GROUP, cols)
    return pl.pallas_call(
        functools.partial(coherence_kernel, tiles),
        out_shape=(jax.ShapeDtypeStruct(looks, jnp.float32), jax.ShapeDtypeStruct(coher, jnp.float32)),
        out_specs=(pl.BlockSpec(memory_space=pl.ANY), pl.BlockSpec(memory_space=pl.ANY)),
        scratch_shapes=[
            pltpu.VMEM(looks, jnp.float32),
            pltpu.VMEM((GROUP * GROUP, cols), jnp.float32),
            pltpu.VMEM(coher, jnp.float32),
            pltpu.SemaphoreType.DMA((2,)),
        ],
        compiler_params=pltpu.CompilerParams(vmem_limit_bytes=4 * 1024 * 1024),
        name="finish",
    )(rows)


def local(slabs):
    dates, tiles = lax.axis_size("date"), lax.axis_size("az")
    _, planes, lines, samples = slabs.shape
    cols = samples // LOOK_RG
    groups = [list(range(g, g + GROUP)) for g in range(0, dates, GROUP)]
    pieces = cut(slabs[0]).reshape(GROUP, LOOK_AZ * planes, SUB, samples // SUB)
    own = lax.all_to_all(pieces, "date", 0, 0, axis_index_groups=groups, tiled=True)
    back = [(i, i - GROUP) for i in range(GROUP, dates)]
    later = lax.ppermute(own[:SPAN], "date", back)
    fields = look_later(own, later, look_own(own, cols))
    rows = lax.all_to_all(fields, "date", 0, 0, axis_index_groups=groups, tiled=True)
    rows = lax.all_gather(rows, "az")
    return finish(rows.reshape(tiles * GROUP * FIELDS, cols), tiles)


def solution(mesh):
    in_specs = (P("date", None, "az", None),)
    out_specs = (P(None, None, "date", "az", None), P(None, "date", "az", None))
    return jax.shard_map(local, mesh=mesh, in_specs=in_specs, out_specs=out_specs, check_vma=False)
```

```python
import jax
import jax.numpy as jnp
from jax import lax
from jax.experimental import pallas as pl
from jax.experimental.pallas import tpu as pltpu
from jax.sharding import PartitionSpec as P

LOOK_AZ = 4
LOOK_RG = 16
WIN = 5
SPAN = 5
GROUP = 8
FIELDS = 3 * SPAN + 1
SUB = 16


def cut_kernel(slab_ref, out_ref, held, arrived):
    planes, lines, _ = slab_ref.shape
    width = out_ref.shape[-1]
    parts = [(plane, line) for line in range(0, lines, 8) for plane in range(planes)]
    copies = []
    for plane, line in parts:
        here = (plane, pl.ds(line, 8))
        copies.append(pltpu.make_async_copy(slab_ref.at[here], held.at[here], arrived.at[len(copies)]))
        copies[-1].start()
    for (plane, line), copy in zip(parts, copies):
        copy.wait()
        for block in range(SUB):
            part = held[plane, line : line + 8, block * width : (block + 1) * width]
            start = (line * planes + plane) * SUB + block
            out_ref[pl.ds(start, 8, stride=planes * SUB), :] = part


def cut(slab):
    planes, lines, samples = slab.shape
    rows = planes * lines * SUB
    slab = pltpu.with_memory_space_constraint(slab, pltpu.HBM)
    return pl.pallas_call(
        cut_kernel,
        in_specs=[pl.BlockSpec(memory_space=pl.ANY)],
        out_shape=jax.ShapeDtypeStruct((rows, samples // SUB), jnp.float32),
        scratch_shapes=[
            pltpu.VMEM(slab.shape, jnp.float32),
            pltpu.SemaphoreType.DMA((planes * lines // 8,)),
        ],
        compiler_params=pltpu.CompilerParams(vmem_limit_bytes=4 * 1024 * 1024),
        name="cut",
    )(slab)


def inside(index):
    return min(SPAN, GROUP - 1 - index)


def look_at(date, pairs, powers, sums, cols):
    width = sums.shape[-1]
    count = 0

    def put(terms):
        nonlocal count
        total = terms[0]
        for term in terms[1:]:
            total = total + term
        sums[count * SUB : (count + 1) * SUB, :] = total
        count += 1

    for index, gaps in pairs:
        real, imag = date(index)
        others = [date(index + gap) for gap in gaps]
        for other_real, other_imag in others:
            put([a * b for a, b in zip(real + imag, other_real + other_imag)])
        for other_real, other_imag in others:
            put([a * b - c * d for a, b, c, d in zip(imag, other_real, real, other_imag)])
    for index in powers:
        real, imag = date(index)
        put([v * v for v in real + imag])

    per_block = width // LOOK_RG
    sample = lax.broadcasted_iota(jnp.int32, (width, cols), 0)
    lane = lax.broadcasted_iota(jnp.int32, (width, cols), 1)
    weight = jnp.where(sample // LOOK_RG == lane % per_block, 1.0 / (LOOK_AZ * LOOK_RG), 0.0)
    looks = jnp.dot(
        sums[: count * SUB, :], weight, precision=lax.Precision.HIGHEST, preferred_element_type=jnp.float32
    )
    looks = looks.reshape(count, SUB, cols)
    block = lax.broadcasted_iota(jnp.int32, (1, SUB, cols), 1)
    lane = lax.broadcasted_iota(jnp.int32, (1, SUB, cols), 2)
    return jnp.sum(jnp.where(lane // per_block == block, looks, 0.0), axis=1)


def planes_of(ref, at):
    return [ref[at, 2 * k] for k in range(LOOK_AZ)], [ref[at, 2 * k + 1] for k in range(LOOK_AZ)]


OWN_PAIRS = [(d, range(1, inside(d) + 1)) for d in range(GROUP)]
LATER_PAIRS = [(d, range(inside(d) + 1, SPAN + 1)) for d in range(GROUP) if inside(d) < SPAN]
OWN_ROWS = sum(2 * len(gaps) for _, gaps in OWN_PAIRS)
LATER_ROWS = sum(2 * len(gaps) for _, gaps in LATER_PAIRS)


def own_kernel(own_ref, out_ref, sums):
    out_ref[...] = look_at(lambda d: planes_of(own_ref, d), OWN_PAIRS, range(GROUP), sums, out_ref.shape[-1])


def later_kernel(own_ref, later_ref, looks_ref, out_ref, sums, cells):
    def date(index):
        return planes_of(own_ref, index) if index < GROUP else planes_of(later_ref, index - GROUP)

    cells[...] = look_at(date, LATER_PAIRS, range(GROUP, GROUP + SPAN), sums, out_ref.shape[-1])
    own_at = later_at = 0
    for index in range(GROUP):
        near, far = inside(index), SPAN - inside(index)
        piece = out_ref.at[index]
        for part in range(2):
            if near:
                piece[part * SPAN : part * SPAN + near, :] = looks_ref[own_at : own_at + near, :]
            if far:
                piece[part * SPAN + near : (part + 1) * SPAN, :] = cells[later_at : later_at + far, :]
            own_at += near
            later_at += far
        piece[2 * SPAN : 2 * SPAN + 1 + near, :] = looks_ref[OWN_ROWS + index : OWN_ROWS + index + 1 + near, :]
        if far:
            piece[2 * SPAN + 1 + near :, :] = cells[LATER_ROWS : LATER_ROWS + far, :]


def look_own(own, cols):
    rows = OWN_ROWS + GROUP
    return pl.pallas_call(
        own_kernel,
        out_shape=jax.ShapeDtypeStruct((rows, cols), jnp.float32),
        scratch_shapes=[pltpu.VMEM((rows * SUB, own.shape[-1]), jnp.float32)],
        compiler_params=pltpu.CompilerParams(vmem_limit_bytes=8 * 1024 * 1024),
        cost_estimate=pl.CostEstimate(
            flops=12 * rows * SUB * cols * cols, bytes_accessed=own.size * 4, transcendentals=0
        ),
        name="look_own",
    )(own)


def look_later(own, later, looks):
    cols = looks.shape[-1]
    rows = LATER_ROWS + SPAN
    return pl.pallas_call(
        later_kernel,
        out_shape=jax.ShapeDtypeStruct((GROUP, FIELDS, cols), jnp.float32),
        scratch_shapes=[
            pltpu.VMEM((rows * SUB, own.shape[-1]), jnp.float32),
            pltpu.VMEM((rows, cols), jnp.float32),
        ],
        compiler_params=pltpu.CompilerParams(vmem_limit_bytes=8 * 1024 * 1024),
        name="look_later",
    )(own, later, looks)


def coherence_kernel(rows_ref, looks_out, coher_out, looks_ref, values, coher_ref, sent):
    date, dates = lax.axis_index("date"), lax.axis_size("date")
    cols = rows_ref.shape[-1]
    half = WIN // 2
    for gap in range(1, SPAN + 1):
        for part in range(2):
            look = rows_ref[pl.ds(part * SPAN + gap - 1, GROUP, stride=2 * FIELDS), :]
            looks_ref[gap - 1, part, 0] = jnp.where(date + gap < dates, look, 0.0)
    looks_sent = pltpu.make_async_copy(looks_ref, looks_out, sent.at[0])
    looks_sent.start()

    lane = lax.broadcasted_iota(jnp.int32, (FIELDS, cols), 1)
    rows = []
    for offset in range(-half, GROUP + half):
        start = (2 * (offset % GROUP) + (0 if 0 <= offset < GROUP else 1)) * FIELDS
        rows.append(rows_ref[start : start + FIELDS, :])
    for r in range(GROUP):
        tall = rows[r]
        for shift in range(1, WIN):
            tall = tall + rows[r + shift]
        boxed = tall
        for shift in range(1, half + 1):
            boxed = boxed + jnp.where(lane >= shift, pltpu.roll(tall, shift, 1), 0.0)
            boxed = boxed + jnp.where(lane < cols - shift, pltpu.roll(tall, cols - shift, 1), 0.0)
        real = boxed[:SPAN]
        imag = boxed[SPAN : 2 * SPAN]
        own = boxed[2 * SPAN : 2 * SPAN + 1]
        later = boxed[2 * SPAN + 1 :]
        value = jnp.sqrt(real * real + imag * imag) / jnp.sqrt(own * later + 1e-06)
        values[r * GROUP : r * GROUP + SPAN, :] = value
    for gap in range(1, SPAN + 1):
        value = values[pl.ds(gap - 1, GROUP, stride=GROUP), :]
        coher_ref[gap - 1, 0] = jnp.where(date + gap < dates, value, 0.0)
    coher_sent = pltpu.make_async_copy(coher_ref, coher_out, sent.at[1])
    coher_sent.start()
    looks_sent.wait()
    coher_sent.wait()


def finish(rows):
    cols = rows.shape[-1]
    looks = (SPAN, 2, 1, GROUP, cols)
    coher = (SPAN, 1, GROUP, cols)
    return pl.pallas_call(
        coherence_kernel,
        out_shape=(jax.ShapeDtypeStruct(looks, jnp.float32), jax.ShapeDtypeStruct(coher, jnp.float32)),
        out_specs=(pl.BlockSpec(memory_space=pl.ANY), pl.BlockSpec(memory_space=pl.ANY)),
        scratch_shapes=[
            pltpu.VMEM(looks, jnp.float32),
            pltpu.VMEM((GROUP * GROUP, cols), jnp.float32),
            pltpu.VMEM(coher, jnp.float32),
            pltpu.SemaphoreType.DMA((2,)),
        ],
        compiler_params=pltpu.CompilerParams(vmem_limit_bytes=4 * 1024 * 1024),
        name="finish",
    )(rows)


def to_neighbours(dates, tiles):
    half = WIN // 2
    pairs = []
    for date in range(dates):
        row = date % GROUP
        step = -1 if row < half else 1 if row >= GROUP - half else 0
        for tile in range(tiles):
            if step and 0 <= tile + step < tiles:
                pairs.append((date * tiles + tile, date * tiles + tile + step))
    return pairs


def local(slabs):
    dates, tiles = lax.axis_size("date"), lax.axis_size("az")
    _, planes, lines, samples = slabs.shape
    cols = samples // LOOK_RG
    groups = [list(range(g, g + GROUP)) for g in range(0, dates, GROUP)]
    pieces = cut(slabs[0]).reshape(GROUP, LOOK_AZ * planes, SUB, samples // SUB)
    own = lax.all_to_all(pieces, "date", 0, 0, axis_index_groups=groups, tiled=True)
    back = [(i, i - GROUP) for i in range(GROUP, dates)]
    later = lax.ppermute(own[:SPAN], "date", back)
    fields = look_later(own, later, look_own(own, cols))
    beside = lax.ppermute(fields, ("date", "az"), to_neighbours(dates, tiles))
    rows = jnp.stack([fields, beside], axis=1)
    rows = lax.all_to_all(rows, "date", 0, 0, axis_index_groups=groups, tiled=True)
    return finish(rows.reshape(GROUP * 2 * FIELDS, cols))


def solution(mesh):
    in_specs = (P("date", None, "az", None),)
    out_specs = (P(None, None, "date", "az", None), P(None, "date", "az", None))
    return jax.shard_map(local, mesh=mesh, in_specs=in_specs, out_specs=out_specs, check_vma=False)
```

```python
import functools

import jax
import jax.numpy as jnp
from jax import lax
from jax.experimental import pallas as pl
from jax.experimental.pallas import tpu as pltpu
from jax.sharding import PartitionSpec as P

LOOK_AZ = 4
LOOK_RG = 16
WIN = 5
SPAN = 5
GROUP = 8
FIELDS = 3 * SPAN + 1
SUB = 16


def cut_kernel(slab_ref, out_ref, held, arrived):
    planes, lines, _ = slab_ref.shape
    width = out_ref.shape[-1]
    blocks = SUB // 2
    parts = [(p, line, b) for line in range(0, lines, 8) for p in range(planes) for b in range(0, SUB, blocks)]
    copies = []
    for plane, line, first in parts:
        here = (plane, pl.ds(line, 8), pl.ds(first * width, blocks * width))
        copies.append(pltpu.make_async_copy(slab_ref.at[here], held.at[here], arrived.at[len(copies)]))
        copies[-1].start(priority=first // blocks)
    for (plane, line, first), copy in zip(parts, copies):
        copy.wait()
        for block in range(first, first + blocks):
            part = held[plane, line : line + 8, block * width : (block + 1) * width]
            start = (line * planes + plane) * SUB + block
            out_ref[pl.ds(start, 8, stride=planes * SUB), :] = part


def cut(slab):
    planes, lines, samples = slab.shape
    rows = planes * lines * SUB
    slab = pltpu.with_memory_space_constraint(slab, pltpu.HBM)
    return pl.pallas_call(
        cut_kernel,
        in_specs=[pl.BlockSpec(memory_space=pl.ANY)],
        out_shape=jax.ShapeDtypeStruct((rows, samples // SUB), jnp.float32),
        scratch_shapes=[
            pltpu.VMEM(slab.shape, jnp.float32),
            pltpu.SemaphoreType.DMA((planes * lines // 4,)),
        ],
        compiler_params=pltpu.CompilerParams(vmem_limit_bytes=4 * 1024 * 1024),
        name="cut",
    )(slab)


def inside(index):
    return min(SPAN, GROUP - 1 - index)


def look_at(date, pairs, powers, sums, cols):
    width = sums.shape[-1]
    count = 0

    def put(terms):
        nonlocal count
        total = terms[0]
        for term in terms[1:]:
            total = total + term
        sums[count * SUB : (count + 1) * SUB, :] = total
        count += 1

    for index, gaps in pairs:
        real, imag = date(index)
        others = [date(index + gap) for gap in gaps]
        for other_real, other_imag in others:
            put([a * b for a, b in zip(real + imag, other_real + other_imag)])
        for other_real, other_imag in others:
            put([a * b - c * d for a, b, c, d in zip(imag, other_real, real, other_imag)])
    for index in powers:
        real, imag = date(index)
        put([v * v for v in real + imag])

    per_block = width // LOOK_RG
    sample = lax.broadcasted_iota(jnp.int32, (width, cols), 0)
    lane = lax.broadcasted_iota(jnp.int32, (width, cols), 1)
    weight = jnp.where(sample // LOOK_RG == lane % per_block, 1.0 / (LOOK_AZ * LOOK_RG), 0.0)
    weight = weight.astype(jnp.bfloat16)
    total = sums[: count * SUB, :]
    high = total.astype(jnp.bfloat16)
    low = (total - high.astype(jnp.float32)).astype(jnp.bfloat16)
    looks = jnp.dot(high, weight, preferred_element_type=jnp.float32)
    looks = looks + jnp.dot(low, weight, preferred_element_type=jnp.float32)
    looks = looks.reshape(count, SUB, cols)
    block = lax.broadcasted_iota(jnp.int32, (1, SUB, cols), 1)
    lane = lax.broadcasted_iota(jnp.int32, (1, SUB, cols), 2)
    return jnp.sum(jnp.where(lane // per_block == block, looks, 0.0), axis=1)


def planes_of(ref, at):
    return [ref[at, 2 * k] for k in range(LOOK_AZ)], [ref[at, 2 * k + 1] for k in range(LOOK_AZ)]


OWN_PAIRS = [(d, range(1, inside(d) + 1)) for d in range(GROUP)]
LATER_PAIRS = [(d, range(inside(d) + 1, SPAN + 1)) for d in range(GROUP) if inside(d) < SPAN]
OWN_ROWS = sum(2 * len(gaps) for _, gaps in OWN_PAIRS)
LATER_ROWS = sum(2 * len(gaps) for _, gaps in LATER_PAIRS)


def own_kernel(own_ref, out_ref, sums):
    out_ref[...] = look_at(lambda d: planes_of(own_ref, d), OWN_PAIRS, range(GROUP), sums, out_ref.shape[-1])


def later_kernel(own_ref, later_ref, looks_ref, out_ref, sums, cells):
    def date(index):
        return planes_of(own_ref, index) if index < GROUP else planes_of(later_ref, index - GROUP)

    cells[...] = look_at(date, LATER_PAIRS, range(GROUP, GROUP + SPAN), sums, out_ref.shape[-1])
    own_at = later_at = 0
    for index in range(GROUP):
        near, far = inside(index), SPAN - inside(index)
        piece = out_ref.at[index, 0]
        for part in range(2):
            if near:
                piece[part * SPAN : part * SPAN + near, :] = looks_ref[own_at : own_at + near, :]
            if far:
                piece[part * SPAN + near : (part + 1) * SPAN, :] = cells[later_at : later_at + far, :]
            own_at += near
            later_at += far
        piece[2 * SPAN : 2 * SPAN + 1 + near, :] = looks_ref[OWN_ROWS + index : OWN_ROWS + index + 1 + near, :]
        if far:
            piece[2 * SPAN + 1 + near :, :] = cells[LATER_ROWS : LATER_ROWS + far, :]
        for tile in range(1, out_ref.shape[1]):
            out_ref[index, tile] = out_ref[index, 0]


def look_own(own, cols):
    rows = OWN_ROWS + GROUP
    return pl.pallas_call(
        own_kernel,
        out_shape=jax.ShapeDtypeStruct((rows, cols), jnp.float32),
        scratch_shapes=[pltpu.VMEM((rows * SUB, own.shape[-1]), jnp.float32)],
        compiler_params=pltpu.CompilerParams(vmem_limit_bytes=8 * 1024 * 1024),
        cost_estimate=pl.CostEstimate(
            flops=12 * rows * SUB * cols * cols, bytes_accessed=own.size * 4, transcendentals=0
        ),
        name="look_own",
    )(own)


def look_later(own, later, looks, tiles):
    cols = looks.shape[-1]
    rows = LATER_ROWS + SPAN
    return pl.pallas_call(
        later_kernel,
        out_shape=jax.ShapeDtypeStruct((GROUP, tiles, FIELDS, cols), jnp.float32),
        scratch_shapes=[
            pltpu.VMEM((rows * SUB, own.shape[-1]), jnp.float32),
            pltpu.VMEM((rows, cols), jnp.float32),
        ],
        compiler_params=pltpu.CompilerParams(vmem_limit_bytes=8 * 1024 * 1024),
        name="look_later",
    )(own, later, looks)


def coherence_kernel(tiles, rows_ref, looks_out, coher_out, looks_ref, values, coher_ref, sent):
    date, dates = lax.axis_index("date"), lax.axis_size("date")
    tile = lax.axis_index("az")
    cols = rows_ref.shape[-1]
    half = WIN // 2
    for gap in range(1, SPAN + 1):
        for part in range(2):
            start = tile * FIELDS + part * SPAN + gap - 1
            look = rows_ref[pl.ds(start, GROUP, stride=tiles * FIELDS), :]
            looks_ref[gap - 1, part, 0] = jnp.where(date + gap < dates, look, 0.0)
    looks_sent = pltpu.make_async_copy(looks_ref, looks_out, sent.at[0])
    looks_sent.start()

    lane = lax.broadcasted_iota(jnp.int32, (FIELDS, cols), 1)
    rows = []
    for offset in range(-half, GROUP + half):
        other = tile + offset // GROUP
        start = (offset % GROUP * tiles + jnp.clip(other, 0, tiles - 1)) * FIELDS
        row = rows_ref[pl.ds(pl.multiple_of(start, FIELDS), FIELDS), :]
        if not 0 <= offset < GROUP:
            row = jnp.where(jnp.logical_and(other >= 0, other < tiles), row, 0.0)
        rows.append(row)
    for r in range(GROUP):
        tall = rows[r]
        for shift in range(1, WIN):
            tall = tall + rows[r + shift]
        boxed = tall
        for shift in range(1, half + 1):
            boxed = boxed + jnp.where(lane >= shift, pltpu.roll(tall, shift, 1), 0.0)
            boxed = boxed + jnp.where(lane < cols - shift, pltpu.roll(tall, cols - shift, 1), 0.0)
        real = boxed[:SPAN]
        imag = boxed[SPAN : 2 * SPAN]
        own = boxed[2 * SPAN : 2 * SPAN + 1]
        later = boxed[2 * SPAN + 1 :]
        value = jnp.sqrt(real * real + imag * imag) / jnp.sqrt(own * later + 1e-06)
        values[r * GROUP : r * GROUP + SPAN, :] = value
    for gap in range(1, SPAN + 1):
        value = values[pl.ds(gap - 1, GROUP, stride=GROUP), :]
        coher_ref[gap - 1, 0] = jnp.where(date + gap < dates, value, 0.0)
    coher_sent = pltpu.make_async_copy(coher_ref, coher_out, sent.at[1])
    coher_sent.start()
    looks_sent.wait()
    coher_sent.wait()


def finish(rows, tiles):
    cols = rows.shape[-1]
    looks = (SPAN, 2, 1, GROUP, cols)
    coher = (SPAN, 1, GROUP, cols)
    return pl.pallas_call(
        functools.partial(coherence_kernel, tiles),
        out_shape=(jax.ShapeDtypeStruct(looks, jnp.float32), jax.ShapeDtypeStruct(coher, jnp.float32)),
        out_specs=(pl.BlockSpec(memory_space=pl.ANY), pl.BlockSpec(memory_space=pl.ANY)),
        scratch_shapes=[
            pltpu.VMEM(looks, jnp.float32),
            pltpu.VMEM((GROUP * GROUP, cols), jnp.float32),
            pltpu.VMEM(coher, jnp.float32),
            pltpu.SemaphoreType.DMA((2,)),
        ],
        compiler_params=pltpu.CompilerParams(vmem_limit_bytes=4 * 1024 * 1024),
        name="finish",
    )(rows)


def local(slabs):
    dates, tiles = lax.axis_size("date"), lax.axis_size("az")
    _, planes, lines, samples = slabs.shape
    cols = samples // LOOK_RG
    groups = [list(range(g, g + GROUP)) for g in range(0, dates, GROUP)]
    wide = [list(range(g * tiles, (g + GROUP) * tiles)) for g in range(0, dates, GROUP)]
    pieces = cut(slabs[0]).reshape(GROUP, LOOK_AZ * planes, SUB, samples // SUB)
    own = lax.all_to_all(pieces, "date", 0, 0, axis_index_groups=groups, tiled=True)
    back = [(i, i - GROUP) for i in range(GROUP, dates)]
    later = lax.ppermute(own[:SPAN], "date", back)
    fields = look_later(own, later, look_own(own, cols), tiles)
    fields = fields.reshape(GROUP * tiles, FIELDS, cols)
    rows = lax.all_to_all(fields, ("date", "az"), 0, 0, axis_index_groups=wide, tiled=True)
    return finish(rows.reshape(GROUP * tiles * FIELDS, cols), tiles)


def solution(mesh):
    in_specs = (P("date", None, "az", None),)
    out_specs = (P(None, None, "date", "az", None), P(None, "date", "az", None))
    return jax.shard_map(local, mesh=mesh, in_specs=in_specs, out_specs=out_specs, check_vma=False)
```

```python
import functools

import jax
import jax.numpy as jnp
from jax import lax
from jax.experimental import pallas as pl
from jax.experimental.pallas import tpu as pltpu
from jax.sharding import PartitionSpec as P

LOOK_AZ = 4
LOOK_RG = 16
WIN = 5
SPAN = 5
GROUP = 8
FIELDS = 3 * SPAN + 1
SUB = 16


def cut_kernel(slab_ref, out_ref, held, arrived):
    planes, lines, _ = slab_ref.shape
    width = out_ref.shape[-1]
    copies = []
    for line in range(0, lines, 8):
        here = (pl.ds(0, planes), pl.ds(line, 8))
        copies.append(pltpu.make_async_copy(slab_ref.at[here], held.at[here], arrived.at[len(copies)]))
        copies[-1].start()
    for line, copy in zip(range(0, lines, 8), copies):
        copy.wait()
        for plane in range(planes):
            for block in range(SUB):
                part = held[plane, line : line + 8, block * width : (block + 1) * width]
                start = (line * planes + plane) * SUB + block
                out_ref[pl.ds(start, 8, stride=planes * SUB), :] = part


def cut(slab):
    planes, lines, samples = slab.shape
    rows = planes * lines * SUB
    slab = pltpu.with_memory_space_constraint(slab, pltpu.HBM)
    return pl.pallas_call(
        cut_kernel,
        in_specs=[pl.BlockSpec(memory_space=pl.ANY)],
        out_shape=jax.ShapeDtypeStruct((rows, samples // SUB), jnp.float32),
        scratch_shapes=[
            pltpu.VMEM(slab.shape, jnp.float32),
            pltpu.SemaphoreType.DMA((lines // 8,)),
        ],
        compiler_params=pltpu.CompilerParams(vmem_limit_bytes=4 * 1024 * 1024),
        name="cut",
    )(slab)


def inside(index):
    return min(SPAN, GROUP - 1 - index)


def look_at(date, pairs, powers, sums, cols):
    width = sums.shape[-1]
    count = 0

    def put(terms):
        nonlocal count
        total = terms[0]
        for term in terms[1:]:
            total = total + term
        sums[count * SUB : (count + 1) * SUB, :] = total
        count += 1

    for index, gaps in pairs:
        real, imag = date(index)
        others = [date(index + gap) for gap in gaps]
        for other_real, other_imag in others:
            put([a * b for a, b in zip(real + imag, other_real + other_imag)])
        for other_real, other_imag in others:
            put([a * b - c * d for a, b, c, d in zip(imag, other_real, real, other_imag)])
    for index in powers:
        real, imag = date(index)
        put([v * v for v in real + imag])

    per_block = width // LOOK_RG
    sample = lax.broadcasted_iota(jnp.int32, (width, cols), 0)
    lane = lax.broadcasted_iota(jnp.int32, (width, cols), 1)
    weight = jnp.where(sample // LOOK_RG == lane % per_block, 1.0 / (LOOK_AZ * LOOK_RG), 0.0)
    weight = weight.astype(jnp.bfloat16)
    total = sums[: count * SUB, :]
    high = total.astype(jnp.bfloat16)
    low = (total - high.astype(jnp.float32)).astype(jnp.bfloat16)
    looks = jnp.dot(high, weight, preferred_element_type=jnp.float32)
    looks = looks + jnp.dot(low, weight, preferred_element_type=jnp.float32)
    looks = looks.reshape(count, SUB, cols)
    block = lax.broadcasted_iota(jnp.int32, (1, SUB, cols), 1)
    lane = lax.broadcasted_iota(jnp.int32, (1, SUB, cols), 2)
    return jnp.sum(jnp.where(lane // per_block == block, looks, 0.0), axis=1)


def planes_of(ref, at):
    return [ref[at, 2 * k] for k in range(LOOK_AZ)], [ref[at, 2 * k + 1] for k in range(LOOK_AZ)]


OWN_PAIRS = [(d, range(1, inside(d) + 1)) for d in range(GROUP)]
LATER_PAIRS = [(d, range(inside(d) + 1, SPAN + 1)) for d in range(GROUP) if inside(d) < SPAN]
OWN_ROWS = sum(2 * len(gaps) for _, gaps in OWN_PAIRS)
LATER_ROWS = sum(2 * len(gaps) for _, gaps in LATER_PAIRS)


def own_kernel(own_ref, out_ref, sums):
    out_ref[...] = look_at(lambda d: planes_of(own_ref, d), OWN_PAIRS, range(GROUP), sums, out_ref.shape[-1])


def later_kernel(own_ref, later_ref, looks_ref, out_ref, sums, cells):
    def date(index):
        return planes_of(own_ref, index) if index < GROUP else planes_of(later_ref, index - GROUP)

    cells[...] = look_at(date, LATER_PAIRS, range(GROUP, GROUP + SPAN), sums, out_ref.shape[-1])
    own_at = later_at = 0
    for index in range(GROUP):
        near, far = inside(index), SPAN - inside(index)
        piece = out_ref.at[index, 0]
        for part in range(2):
            if near:
                piece[part * SPAN : part * SPAN + near, :] = looks_ref[own_at : own_at + near, :]
            if far:
                piece[part * SPAN + near : (part + 1) * SPAN, :] = cells[later_at : later_at + far, :]
            own_at += near
            later_at += far
        piece[2 * SPAN : 2 * SPAN + 1 + near, :] = looks_ref[OWN_ROWS + index : OWN_ROWS + index + 1 + near, :]
        if far:
            piece[2 * SPAN + 1 + near :, :] = cells[LATER_ROWS : LATER_ROWS + far, :]
        for tile in range(1, out_ref.shape[1]):
            out_ref[index, tile] = out_ref[index, 0]


def look_own(own, cols):
    rows = OWN_ROWS + GROUP
    return pl.pallas_call(
        own_kernel,
        out_shape=jax.ShapeDtypeStruct((rows, cols), jnp.float32),
        scratch_shapes=[pltpu.VMEM((rows * SUB, own.shape[-1]), jnp.float32)],
        compiler_params=pltpu.CompilerParams(vmem_limit_bytes=8 * 1024 * 1024),
        cost_estimate=pl.CostEstimate(
            flops=12 * rows * SUB * cols * cols, bytes_accessed=own.size * 4, transcendentals=0
        ),
        name="look_own",
    )(own)


def look_later(own, later, looks, tiles):
    cols = looks.shape[-1]
    rows = LATER_ROWS + SPAN
    return pl.pallas_call(
        later_kernel,
        out_shape=jax.ShapeDtypeStruct((GROUP, tiles, FIELDS, cols), jnp.float32),
        scratch_shapes=[
            pltpu.VMEM((rows * SUB, own.shape[-1]), jnp.float32),
            pltpu.VMEM((rows, cols), jnp.float32),
        ],
        compiler_params=pltpu.CompilerParams(vmem_limit_bytes=8 * 1024 * 1024),
        name="look_later",
    )(own, later, looks)


def coherence_kernel(tiles, rows_ref, looks_out, coher_out, looks_ref, boxes, coher_ref, sent):
    date, dates = lax.axis_index("date"), lax.axis_size("date")
    tile = lax.axis_index("az")
    cols = rows_ref.shape[-1]
    half = WIN // 2
    for gap in range(1, SPAN + 1):
        for part in range(2):
            start = tile * FIELDS + part * SPAN + gap - 1
            look = rows_ref[pl.ds(start, GROUP, stride=tiles * FIELDS), :]
            looks_ref[gap - 1, part, 0] = jnp.where(date + gap < dates, look, 0.0)
    looks_sent = pltpu.make_async_copy(looks_ref, looks_out, sent.at[0])
    looks_sent.start()

    lane = lax.broadcasted_iota(jnp.int32, (FIELDS, cols), 1)
    rows = []
    for offset in range(-half, GROUP + half):
        other = tile + offset // GROUP
        start = (offset % GROUP * tiles + jnp.clip(other, 0, tiles - 1)) * FIELDS
        row = rows_ref[pl.ds(pl.multiple_of(start, FIELDS), FIELDS), :]
        if not 0 <= offset < GROUP:
            row = jnp.where(jnp.logical_and(other >= 0, other < tiles), row, 0.0)
        rows.append(row)
    for r in range(GROUP):
        tall = rows[r]
        for shift in range(1, WIN):
            tall = tall + rows[r + shift]
        boxed = tall
        for shift in range(1, half + 1):
            boxed = boxed + jnp.where(lane >= shift, pltpu.roll(tall, shift, 1), 0.0)
            boxed = boxed + jnp.where(lane < cols - shift, pltpu.roll(tall, cols - shift, 1), 0.0)
        boxes[r * FIELDS : (r + 1) * FIELDS, :] = boxed
    fields = [boxes[pl.ds(field, GROUP, stride=FIELDS), :] for field in range(FIELDS)]
    own, later = fields[2 * SPAN], fields[2 * SPAN + 1 :]
    for gap in range(1, SPAN + 1):
        real, imag = fields[gap - 1], fields[SPAN + gap - 1]
        value = jnp.sqrt(real * real + imag * imag) / jnp.sqrt(own * later[gap - 1] + 1e-06)
        coher_ref[gap - 1, 0] = jnp.where(date + gap < dates, value, 0.0)
    coher_sent = pltpu.make_async_copy(coher_ref, coher_out, sent.at[1])
    coher_sent.start()
    looks_sent.wait()
    coher_sent.wait()


def finish(rows, tiles):
    cols = rows.shape[-1]
    looks = (SPAN, 2, 1, GROUP, cols)
    coher = (SPAN, 1, GROUP, cols)
    return pl.pallas_call(
        functools.partial(coherence_kernel, tiles),
        out_shape=(jax.ShapeDtypeStruct(looks, jnp.float32), jax.ShapeDtypeStruct(coher, jnp.float32)),
        out_specs=(pl.BlockSpec(memory_space=pl.ANY), pl.BlockSpec(memory_space=pl.ANY)),
        scratch_shapes=[
            pltpu.VMEM(looks, jnp.float32),
            pltpu.VMEM((GROUP * FIELDS, cols), jnp.float32),
            pltpu.VMEM(coher, jnp.float32),
            pltpu.SemaphoreType.DMA((2,)),
        ],
        compiler_params=pltpu.CompilerParams(vmem_limit_bytes=4 * 1024 * 1024),
        name="finish",
    )(rows)


def local(slabs):
    dates, tiles = lax.axis_size("date"), lax.axis_size("az")
    _, planes, lines, samples = slabs.shape
    cols = samples // LOOK_RG
    groups = [list(range(g, g + GROUP)) for g in range(0, dates, GROUP)]
    wide = [list(range(g * tiles, (g + GROUP) * tiles)) for g in range(0, dates, GROUP)]
    pieces = cut(slabs[0]).reshape(GROUP, LOOK_AZ * planes, SUB, samples // SUB)
    own = lax.all_to_all(pieces, "date", 0, 0, axis_index_groups=groups, tiled=True)
    back = [(i, i - GROUP) for i in range(GROUP, dates)]
    later = lax.ppermute(own[:SPAN], "date", back)
    fields = look_later(own, later, look_own(own, cols), tiles)
    fields = fields.reshape(GROUP * tiles, FIELDS, cols)
    rows = lax.all_to_all(fields, ("date", "az"), 0, 0, axis_index_groups=wide, tiled=True)
    return finish(rows.reshape(GROUP * tiles * FIELDS, cols), tiles)


def solution(mesh):
    in_specs = (P("date", None, "az", None),)
    out_specs = (P(None, None, "date", "az", None), P(None, "date", "az", None))
    return jax.shard_map(local, mesh=mesh, in_specs=in_specs, out_specs=out_specs, check_vma=False)
```

```python
import functools

import jax
import jax.numpy as jnp
from jax import lax
from jax.experimental import pallas as pl
from jax.experimental.pallas import tpu as pltpu
from jax.sharding import PartitionSpec as P

LOOK_AZ = 4
LOOK_RG = 16
WIN = 5
SPAN = 5
GROUP = 8
FIELDS = 3 * SPAN + 1
SUB = 16


def cut_kernel(slab_ref, out_ref, held, arrived):
    planes, lines, _ = slab_ref.shape
    width = out_ref.shape[-1]
    copies = []
    for line in range(0, lines, 8):
        here = (pl.ds(0, planes), pl.ds(line, 8))
        copies.append(pltpu.make_async_copy(slab_ref.at[here], held.at[here], arrived.at[len(copies)]))
        copies[-1].start()
    for line, copy in zip(range(0, lines, 8), copies):
        copy.wait()
        for plane in range(planes):
            for block in range(SUB):
                part = held[plane, line : line + 8, block * width : (block + 1) * width]
                start = (line * planes + plane) * SUB + block
                out_ref[pl.ds(start, 8, stride=planes * SUB), :] = part


def cut(slab):
    planes, lines, samples = slab.shape
    rows = planes * lines * SUB
    slab = pltpu.with_memory_space_constraint(slab, pltpu.HBM)
    return pl.pallas_call(
        cut_kernel,
        in_specs=[pl.BlockSpec(memory_space=pl.ANY)],
        out_shape=jax.ShapeDtypeStruct((rows, samples // SUB), jnp.float32),
        scratch_shapes=[
            pltpu.VMEM(slab.shape, jnp.float32),
            pltpu.SemaphoreType.DMA((lines // 8,)),
        ],
        compiler_params=pltpu.CompilerParams(vmem_limit_bytes=4 * 1024 * 1024),
        name="cut",
    )(slab)


def inside(index):
    return min(SPAN, GROUP - 1 - index)


def look_at(date, pairs, powers, sums, cols):
    width = sums.shape[-1]
    count = 0

    def put(terms):
        nonlocal count
        total = terms[0]
        for term in terms[1:]:
            total = total + term
        sums[count * SUB : (count + 1) * SUB, :] = total
        count += 1

    for index, gaps in pairs:
        real, imag = date(index)
        others = [date(index + gap) for gap in gaps]
        for other_real, other_imag in others:
            put([a * b for a, b in zip(real + imag, other_real + other_imag)])
        for other_real, other_imag in others:
            put([a * b - c * d for a, b, c, d in zip(imag, other_real, real, other_imag)])
    for index in powers:
        real, imag = date(index)
        put([v * v for v in real + imag])

    per_block = width // LOOK_RG
    sample = lax.broadcasted_iota(jnp.int32, (width, cols), 0)
    lane = lax.broadcasted_iota(jnp.int32, (width, cols), 1)
    weight = jnp.where(sample // LOOK_RG == lane % per_block, 1.0 / (LOOK_AZ * LOOK_RG), 0.0)
    weight = weight.astype(jnp.bfloat16)
    total = sums[: count * SUB, :]
    high = total.astype(jnp.bfloat16)
    low = (total - high.astype(jnp.float32)).astype(jnp.bfloat16)
    looks = jnp.dot(high, weight, preferred_element_type=jnp.float32)
    looks = looks + jnp.dot(low, weight, preferred_element_type=jnp.float32)
    looks = looks.reshape(count, SUB, cols)
    block = lax.broadcasted_iota(jnp.int32, (1, SUB, cols), 1)
    lane = lax.broadcasted_iota(jnp.int32, (1, SUB, cols), 2)
    return jnp.sum(jnp.where(lane // per_block == block, looks, 0.0), axis=1)


def planes_of(ref, at):
    return [ref[at, 2 * k] for k in range(LOOK_AZ)], [ref[at, 2 * k + 1] for k in range(LOOK_AZ)]


FIRST = GROUP - SPAN


def order(tile):
    return [(d + FIRST * (tile % 2)) % GROUP for d in range(GROUP)]


def is_odd():
    return lax.rem(lax.axis_index("az"), 2) == 1


OWN_PAIRS = [(d, range(1, inside(d) + 1)) for d in range(GROUP)]
LATER_PAIRS = [(d, range(inside(d) + 1, SPAN + 1)) for d in range(GROUP) if inside(d) < SPAN]
OWN_ROWS = sum(2 * len(gaps) for _, gaps in OWN_PAIRS)
LATER_ROWS = sum(2 * len(gaps) for _, gaps in LATER_PAIRS)


def own_kernel(own_ref, out_ref, sums):
    shift = jnp.where(is_odd(), GROUP - FIRST, 0)

    def date(index):
        return planes_of(own_ref, lax.rem(index + shift, GROUP))

    out_ref[...] = look_at(date, OWN_PAIRS, range(GROUP), sums, out_ref.shape[-1])


def cross_kernel(own_ref, other_ref, out_ref, sums):
    odd = is_odd()

    def even_date(index):
        return planes_of(own_ref, index) if index < GROUP else planes_of(other_ref, index - GROUP)

    def odd_date(index):
        return planes_of(other_ref, index - FIRST) if index < GROUP else planes_of(own_ref, (index - FIRST) % GROUP)

    for date, here in ((even_date, jnp.logical_not(odd)), (odd_date, odd)):

        @pl.when(here)
        def _(date=date):
            out_ref[...] = look_at(date, LATER_PAIRS, range(GROUP, GROUP + SPAN), sums, out_ref.shape[-1])


def join_kernel(looks_ref, here_ref, back_ref, out_ref, cells):
    cells[...] = jnp.where(is_odd(), back_ref[...], here_ref[...])
    own_at = later_at = 0
    for index in range(GROUP):
        near, far = inside(index), SPAN - inside(index)
        piece = out_ref.at[0, index]
        for part in range(2):
            if near:
                piece[part * SPAN : part * SPAN + near, :] = looks_ref[own_at : own_at + near, :]
            if far:
                piece[part * SPAN + near : (part + 1) * SPAN, :] = cells[later_at : later_at + far, :]
            own_at += near
            later_at += far
        piece[2 * SPAN : 2 * SPAN + 1 + near, :] = looks_ref[OWN_ROWS + index : OWN_ROWS + index + 1 + near, :]
        if far:
            piece[2 * SPAN + 1 + near :, :] = cells[LATER_ROWS : LATER_ROWS + far, :]
    for tile in range(1, out_ref.shape[0]):
        for place, index in enumerate(order(tile)):
            out_ref[tile, place] = out_ref[0, index]


def look_own(own, cols):
    rows = OWN_ROWS + GROUP
    return pl.pallas_call(
        own_kernel,
        out_shape=jax.ShapeDtypeStruct((rows, cols), jnp.float32),
        scratch_shapes=[pltpu.VMEM((rows * SUB, own.shape[-1]), jnp.float32)],
        compiler_params=pltpu.CompilerParams(vmem_limit_bytes=8 * 1024 * 1024),
        cost_estimate=pl.CostEstimate(
            flops=12 * rows * SUB * cols * cols, bytes_accessed=own.size * 4, transcendentals=0
        ),
        name="look_own",
    )(own)


def look_across(own, other, cols):
    rows = LATER_ROWS + SPAN
    return pl.pallas_call(
        cross_kernel,
        out_shape=jax.ShapeDtypeStruct((rows, cols), jnp.float32),
        scratch_shapes=[pltpu.VMEM((rows * SUB, own.shape[-1]), jnp.float32)],
        compiler_params=pltpu.CompilerParams(vmem_limit_bytes=8 * 1024 * 1024),
        name="look_across",
    )(own, other)


def join(looks, here, back, tiles):
    return pl.pallas_call(
        join_kernel,
        out_shape=jax.ShapeDtypeStruct((tiles, GROUP, FIELDS, looks.shape[-1]), jnp.float32),
        scratch_shapes=[pltpu.VMEM(here.shape, jnp.float32)],
        compiler_params=pltpu.CompilerParams(vmem_limit_bytes=4 * 1024 * 1024),
        name="join",
    )(looks, here, back)


def coherence_kernel(tiles, rows_ref, looks_out, coher_out, looks_ref, boxes, coher_ref, sent):
    date, dates = lax.axis_index("date"), lax.axis_size("date")
    tile = lax.axis_index("az")
    cols = rows_ref.shape[-1]
    half = WIN // 2
    for gap in range(1, SPAN + 1):
        for part in range(2):
            start = tile * (GROUP * FIELDS) + part * SPAN + gap - 1
            look = rows_ref[pl.ds(start, GROUP, stride=FIELDS), :]
            looks_ref[gap - 1, part, 0] = jnp.where(date + gap < dates, look, 0.0)
    looks_sent = pltpu.make_async_copy(looks_ref, looks_out, sent.at[0])
    looks_sent.start()

    lane = lax.broadcasted_iota(jnp.int32, (FIELDS, cols), 1)
    rows = []
    for offset in range(-half, GROUP + half):
        other = tile + offset // GROUP
        start = (jnp.clip(other, 0, tiles - 1) * GROUP + offset % GROUP) * FIELDS
        row = rows_ref[pl.ds(pl.multiple_of(start, FIELDS), FIELDS), :]
        if not 0 <= offset < GROUP:
            row = jnp.where(jnp.logical_and(other >= 0, other < tiles), row, 0.0)
        rows.append(row)
    for r in range(GROUP):
        tall = rows[r]
        for shift in range(1, WIN):
            tall = tall + rows[r + shift]
        boxed = tall
        for shift in range(1, half + 1):
            boxed = boxed + jnp.where(lane >= shift, pltpu.roll(tall, shift, 1), 0.0)
            boxed = boxed + jnp.where(lane < cols - shift, pltpu.roll(tall, cols - shift, 1), 0.0)
        boxes[r * FIELDS : (r + 1) * FIELDS, :] = boxed
    fields = [boxes[pl.ds(field, GROUP, stride=FIELDS), :] for field in range(FIELDS)]
    own, later = fields[2 * SPAN], fields[2 * SPAN + 1 :]
    for gap in range(1, SPAN + 1):
        real, imag = fields[gap - 1], fields[SPAN + gap - 1]
        value = jnp.sqrt(real * real + imag * imag) / jnp.sqrt(own * later[gap - 1] + 1e-06)
        coher_ref[gap - 1, 0] = jnp.where(date + gap < dates, value, 0.0)
    coher_sent = pltpu.make_async_copy(coher_ref, coher_out, sent.at[1])
    coher_sent.start()
    looks_sent.wait()
    coher_sent.wait()


def finish(rows, tiles):
    cols = rows.shape[-1]
    looks = (SPAN, 2, 1, GROUP, cols)
    coher = (SPAN, 1, GROUP, cols)
    return pl.pallas_call(
        functools.partial(coherence_kernel, tiles),
        out_shape=(jax.ShapeDtypeStruct(looks, jnp.float32), jax.ShapeDtypeStruct(coher, jnp.float32)),
        out_specs=(pl.BlockSpec(memory_space=pl.ANY), pl.BlockSpec(memory_space=pl.ANY)),
        scratch_shapes=[
            pltpu.VMEM(looks, jnp.float32),
            pltpu.VMEM((GROUP * FIELDS, cols), jnp.float32),
            pltpu.VMEM(coher, jnp.float32),
            pltpu.SemaphoreType.DMA((2,)),
        ],
        compiler_params=pltpu.CompilerParams(vmem_limit_bytes=4 * 1024 * 1024),
        name="finish",
    )(rows)


def local(slabs):
    dates, tiles = lax.axis_size("date"), lax.axis_size("az")
    _, planes, lines, samples = slabs.shape
    cols = samples // LOOK_RG
    both = ("date", "az")
    starts = range(0, dates, GROUP)
    groups = [[(g + d) * tiles + a for d in order(a)] for g in starts for a in range(tiles)]
    wide = [[(g + d) * tiles + a for a in range(tiles) for d in order(a)] for g in starts]
    down = [((d + GROUP) * tiles + a, d * tiles + a) for d in range(dates - GROUP) for a in range(tiles)]
    across = [pair if pair[0] % tiles % 2 == 0 else pair[::-1] for pair in down]
    home = [pair for pair in down if pair[0] % tiles % 2]
    pieces = cut(slabs[0]).reshape(GROUP, LOOK_AZ * planes, SUB, samples // SUB)
    own = lax.all_to_all(pieces, both, 0, 0, axis_index_groups=groups, tiled=True)
    other = lax.ppermute(own[:SPAN], both, across)
    looks = look_own(own, cols)
    here = look_across(own, other, cols)
    fields = join(looks, here, lax.ppermute(here, both, home), tiles)
    fields = fields.reshape(GROUP * tiles, FIELDS, cols)
    rows = lax.all_to_all(fields, ("date", "az"), 0, 0, axis_index_groups=wide, tiled=True)
    return finish(rows.reshape(GROUP * tiles * FIELDS, cols), tiles)


def solution(mesh):
    in_specs = (P("date", None, "az", None),)
    out_specs = (P(None, None, "date", "az", None), P(None, "date", "az", None))
    return jax.shard_map(local, mesh=mesh, in_specs=in_specs, out_specs=out_specs, check_vma=False)
```

```python
import functools

import jax
import jax.numpy as jnp
from jax import lax
from jax.experimental import pallas as pl
from jax.experimental.pallas import tpu as pltpu
from jax.sharding import PartitionSpec as P

LOOK_AZ = 4
LOOK_RG = 16
WIN = 5
SPAN = 5
GROUP = 8
FIELDS = 3 * SPAN + 1
SUB = 16


def cut_kernel(slab_ref, out_ref, held, arrived):
    planes, lines, _ = slab_ref.shape
    width = out_ref.shape[-1]
    copies = []
    for line in range(0, lines, 8):
        here = (pl.ds(0, planes), pl.ds(line, 8))
        copies.append(pltpu.make_async_copy(slab_ref.at[here], held.at[here], arrived.at[len(copies)]))
        copies[-1].start()
    for line, copy in zip(range(0, lines, 8), copies):
        copy.wait()
        for plane in range(planes):
            for block in range(SUB):
                part = held[plane, line : line + 8, block * width : (block + 1) * width]
                start = (line * planes + plane) * SUB + block
                out_ref[pl.ds(start, 8, stride=planes * SUB), :] = part


def cut(slab):
    planes, lines, samples = slab.shape
    rows = planes * lines * SUB
    slab = pltpu.with_memory_space_constraint(slab, pltpu.HBM)
    return pl.pallas_call(
        cut_kernel,
        in_specs=[pl.BlockSpec(memory_space=pl.ANY)],
        out_shape=jax.ShapeDtypeStruct((rows, samples // SUB), jnp.float32),
        scratch_shapes=[
            pltpu.VMEM(slab.shape, jnp.float32),
            pltpu.SemaphoreType.DMA((lines // 8,)),
        ],
        compiler_params=pltpu.CompilerParams(vmem_limit_bytes=4 * 1024 * 1024),
        name="cut",
    )(slab)


def inside(index):
    return min(SPAN, GROUP - 1 - index)


def look_at(date, pairs, powers, sums, cols):
    width = sums.shape[-1]
    count = 0

    def put(terms):
        nonlocal count
        total = terms[0]
        for term in terms[1:]:
            total = total + term
        sums[count * SUB : (count + 1) * SUB, :] = total
        count += 1

    for index, gaps in pairs:
        real, imag = date(index)
        others = [date(index + gap) for gap in gaps]
        for other_real, other_imag in others:
            put([a * b for a, b in zip(real + imag, other_real + other_imag)])
        for other_real, other_imag in others:
            put([a * b - c * d for a, b, c, d in zip(imag, other_real, real, other_imag)])
    for index in powers:
        real, imag = date(index)
        put([v * v for v in real + imag])

    per_block = width // LOOK_RG
    sample = lax.broadcasted_iota(jnp.int32, (width, cols), 0)
    lane = lax.broadcasted_iota(jnp.int32, (width, cols), 1)
    weight = jnp.where(sample // LOOK_RG == lane % per_block, 1.0 / (LOOK_AZ * LOOK_RG), 0.0)
    weight = weight.astype(jnp.bfloat16)
    total = sums[: count * SUB, :]
    high = total.astype(jnp.bfloat16)
    low = (total - high.astype(jnp.float32)).astype(jnp.bfloat16)
    looks = jnp.dot(high, weight, preferred_element_type=jnp.float32)
    looks = looks + jnp.dot(low, weight, preferred_element_type=jnp.float32)
    looks = looks.reshape(count, SUB, cols)
    block = lax.broadcasted_iota(jnp.int32, (1, SUB, cols), 1)
    lane = lax.broadcasted_iota(jnp.int32, (1, SUB, cols), 2)
    return jnp.sum(jnp.where(lane // per_block == block, looks, 0.0), axis=1)


def planes_of(ref, at):
    return [ref[at, 2 * k] for k in range(LOOK_AZ)], [ref[at, 2 * k + 1] for k in range(LOOK_AZ)]


ORDERS = ((0, 1, 2, 3, 4, 5, 6, 7), (3, 4, 0, 1, 2, 6, 7, 5))


def place_of(date):
    odd = lax.rem(lax.axis_index("az"), 2) == 1
    return jnp.where(odd, ORDERS[1].index(date), ORDERS[0].index(date))


OWN_PAIRS = [(d, range(1, inside(d) + 1)) for d in range(GROUP)]
LATER_PAIRS = [(d, range(inside(d) + 1, SPAN + 1)) for d in range(GROUP) if inside(d) < SPAN]
OWN_ROWS = sum(2 * len(gaps) for _, gaps in OWN_PAIRS)
LATER_ROWS = sum(2 * len(gaps) for _, gaps in LATER_PAIRS)


def own_kernel(own_ref, out_ref, sums):
    out_ref[...] = look_at(lambda d: planes_of(own_ref, place_of(d)), OWN_PAIRS, range(GROUP), sums, out_ref.shape[-1])


def later_kernel(own_ref, later_ref, looks_ref, out_ref, sums, cells):
    def date(index):
        return planes_of(own_ref if index < GROUP else later_ref, place_of(index % GROUP))

    cells[...] = look_at(date, LATER_PAIRS, range(GROUP, GROUP + SPAN), sums, out_ref.shape[-1])
    own_at = later_at = 0
    for index in range(GROUP):
        near, far = inside(index), SPAN - inside(index)
        piece = out_ref.at[0, index]
        for part in range(2):
            if near:
                piece[part * SPAN : part * SPAN + near, :] = looks_ref[own_at : own_at + near, :]
            if far:
                piece[part * SPAN + near : (part + 1) * SPAN, :] = cells[later_at : later_at + far, :]
            own_at += near
            later_at += far
        piece[2 * SPAN : 2 * SPAN + 1 + near, :] = looks_ref[OWN_ROWS + index : OWN_ROWS + index + 1 + near, :]
        if far:
            piece[2 * SPAN + 1 + near :, :] = cells[LATER_ROWS : LATER_ROWS + far, :]
    for tile in range(1, out_ref.shape[0]):
        for place, index in enumerate(ORDERS[tile % 2]):
            out_ref[tile, place] = out_ref[0, index]


def look_own(own, cols):
    rows = OWN_ROWS + GROUP
    return pl.pallas_call(
        own_kernel,
        out_shape=jax.ShapeDtypeStruct((rows, cols), jnp.float32),
        scratch_shapes=[pltpu.VMEM((rows * SUB, own.shape[-1]), jnp.float32)],
        compiler_params=pltpu.CompilerParams(vmem_limit_bytes=8 * 1024 * 1024),
        cost_estimate=pl.CostEstimate(
            flops=12 * rows * SUB * cols * cols, bytes_accessed=own.size * 4, transcendentals=0
        ),
        name="look_own",
    )(own)


def look_later(own, later, looks, tiles):
    cols = looks.shape[-1]
    rows = LATER_ROWS + SPAN
    return pl.pallas_call(
        later_kernel,
        out_shape=jax.ShapeDtypeStruct((tiles, GROUP, FIELDS, cols), jnp.float32),
        scratch_shapes=[
            pltpu.VMEM((rows * SUB, own.shape[-1]), jnp.float32),
            pltpu.VMEM((rows, cols), jnp.float32),
        ],
        compiler_params=pltpu.CompilerParams(vmem_limit_bytes=8 * 1024 * 1024),
        name="look_later",
    )(own, later, looks)


def coherence_kernel(tiles, rows_ref, looks_out, coher_out, looks_ref, boxes, coher_ref, sent):
    date, dates = lax.axis_index("date"), lax.axis_size("date")
    tile = lax.axis_index("az")
    cols = rows_ref.shape[-1]
    half = WIN // 2
    for gap in range(1, SPAN + 1):
        for part in range(2):
            start = tile * (GROUP * FIELDS) + part * SPAN + gap - 1
            look = rows_ref[pl.ds(start, GROUP, stride=FIELDS), :]
            looks_ref[gap - 1, part, 0] = jnp.where(date + gap < dates, look, 0.0)
    looks_sent = pltpu.make_async_copy(looks_ref, looks_out, sent.at[0])
    looks_sent.start()

    lane = lax.broadcasted_iota(jnp.int32, (FIELDS, cols), 1)
    rows = []
    for offset in range(-half, GROUP + half):
        other = tile + offset // GROUP
        start = (jnp.clip(other, 0, tiles - 1) * GROUP + offset % GROUP) * FIELDS
        row = rows_ref[pl.ds(pl.multiple_of(start, FIELDS), FIELDS), :]
        if not 0 <= offset < GROUP:
            row = jnp.where(jnp.logical_and(other >= 0, other < tiles), row, 0.0)
        rows.append(row)
    for r in range(GROUP):
        tall = rows[r]
        for shift in range(1, WIN):
            tall = tall + rows[r + shift]
        boxed = tall
        for shift in range(1, half + 1):
            boxed = boxed + jnp.where(lane >= shift, pltpu.roll(tall, shift, 1), 0.0)
            boxed = boxed + jnp.where(lane < cols - shift, pltpu.roll(tall, cols - shift, 1), 0.0)
        boxes[r * FIELDS : (r + 1) * FIELDS, :] = boxed
    fields = [boxes[pl.ds(field, GROUP, stride=FIELDS), :] for field in range(FIELDS)]
    own, later = fields[2 * SPAN], fields[2 * SPAN + 1 :]
    for gap in range(1, SPAN + 1):
        real, imag = fields[gap - 1], fields[SPAN + gap - 1]
        value = jnp.sqrt(real * real + imag * imag) / jnp.sqrt(own * later[gap - 1] + 1e-06)
        coher_ref[gap - 1, 0] = jnp.where(date + gap < dates, value, 0.0)
    coher_sent = pltpu.make_async_copy(coher_ref, coher_out, sent.at[1])
    coher_sent.start()
    looks_sent.wait()
    coher_sent.wait()


def finish(rows, tiles):
    cols = rows.shape[-1]
    looks = (SPAN, 2, 1, GROUP, cols)
    coher = (SPAN, 1, GROUP, cols)
    return pl.pallas_call(
        functools.partial(coherence_kernel, tiles),
        out_shape=(jax.ShapeDtypeStruct(looks, jnp.float32), jax.ShapeDtypeStruct(coher, jnp.float32)),
        out_specs=(pl.BlockSpec(memory_space=pl.ANY), pl.BlockSpec(memory_space=pl.ANY)),
        scratch_shapes=[
            pltpu.VMEM(looks, jnp.float32),
            pltpu.VMEM((GROUP * FIELDS, cols), jnp.float32),
            pltpu.VMEM(coher, jnp.float32),
            pltpu.SemaphoreType.DMA((2,)),
        ],
        compiler_params=pltpu.CompilerParams(vmem_limit_bytes=4 * 1024 * 1024),
        name="finish",
    )(rows)


def local(slabs):
    dates, tiles = lax.axis_size("date"), lax.axis_size("az")
    _, planes, lines, samples = slabs.shape
    cols = samples // LOOK_RG
    both = ("date", "az")
    starts = range(0, dates, GROUP)
    groups = [[(g + d) * tiles + a for d in ORDERS[a % 2]] for g in starts for a in range(tiles)]
    wide = [[(g + d) * tiles + a for a in range(tiles) for d in ORDERS[a % 2]] for g in starts]
    pieces = cut(slabs[0]).reshape(GROUP, LOOK_AZ * planes, SUB, samples // SUB)
    own = lax.all_to_all(pieces, both, 0, 0, axis_index_groups=groups, tiled=True)
    back = [(i, i - GROUP) for i in range(GROUP, dates)]
    later = lax.ppermute(own[:SPAN], "date", back)
    fields = look_later(own, later, look_own(own, cols), tiles)
    fields = fields.reshape(GROUP * tiles, FIELDS, cols)
    rows = lax.all_to_all(fields, both, 0, 0, axis_index_groups=wide, tiled=True)
    return finish(rows.reshape(GROUP * tiles * FIELDS, cols), tiles)


def solution(mesh):
    in_specs = (P("date", None, "az", None),)
    out_specs = (P(None, None, "date", "az", None), P(None, "date", "az", None))
    return jax.shard_map(local, mesh=mesh, in_specs=in_specs, out_specs=out_specs, check_vma=False)
```

```python
import functools

import jax
import jax.numpy as jnp
from jax import lax
from jax.experimental import pallas as pl
from jax.experimental.pallas import tpu as pltpu
from jax.sharding import PartitionSpec as P

LOOK_AZ = 4
LOOK_RG = 16
WIN = 5
SPAN = 5
GROUP = 8
FIELDS = 3 * SPAN + 1
SUB = 16


def cut_kernel(slab_ref, out_ref, held, arrived):
    planes, lines, _ = slab_ref.shape
    width = out_ref.shape[-1]
    copies = []
    for line in range(0, lines, 8):
        here = (pl.ds(0, planes), pl.ds(line, 8))
        copies.append(pltpu.make_async_copy(slab_ref.at[here], held.at[here], arrived.at[len(copies)]))
        copies[-1].start()
    for line, copy in zip(range(0, lines, 8), copies):
        copy.wait()
        for plane in range(planes):
            for block in range(SUB):
                part = held[plane, line : line + 8, block * width : (block + 1) * width]
                start = (line * planes + plane) * SUB + block
                out_ref[pl.ds(start, 8, stride=planes * SUB), :] = part


def cut(slab):
    planes, lines, samples = slab.shape
    rows = planes * lines * SUB
    slab = pltpu.with_memory_space_constraint(slab, pltpu.HBM)
    return pl.pallas_call(
        cut_kernel,
        in_specs=[pl.BlockSpec(memory_space=pl.ANY)],
        out_shape=jax.ShapeDtypeStruct((rows, samples // SUB), jnp.float32),
        scratch_shapes=[
            pltpu.VMEM(slab.shape, jnp.float32),
            pltpu.SemaphoreType.DMA((lines // 8,)),
        ],
        compiler_params=pltpu.CompilerParams(vmem_limit_bytes=4 * 1024 * 1024),
        name="cut",
    )(slab)


def inside(index):
    return min(SPAN, GROUP - 1 - index)


def look_at(date, pairs, powers, sums, cols):
    width = sums.shape[-1]
    count = 0

    def put(terms):
        nonlocal count
        total = terms[0]
        for term in terms[1:]:
            total = total + term
        sums[count * SUB : (count + 1) * SUB, :] = total
        count += 1

    for index, gaps in pairs:
        real, imag = date(index)
        others = [date(index + gap) for gap in gaps]
        for other_real, other_imag in others:
            put([a * b for a, b in zip(real + imag, other_real + other_imag)])
        for other_real, other_imag in others:
            put([a * b - c * d for a, b, c, d in zip(imag, other_real, real, other_imag)])
    for index in powers:
        real, imag = date(index)
        put([v * v for v in real + imag])

    per_block = width // LOOK_RG
    sample = lax.broadcasted_iota(jnp.int32, (width, cols), 0)
    lane = lax.broadcasted_iota(jnp.int32, (width, cols), 1)
    weight = jnp.where(sample // LOOK_RG == lane % per_block, 1.0 / (LOOK_AZ * LOOK_RG), 0.0)
    weight = weight.astype(jnp.bfloat16)
    total = sums[: count * SUB, :]
    high = total.astype(jnp.bfloat16)
    low = (total - high.astype(jnp.float32)).astype(jnp.bfloat16)
    looks = jnp.dot(high, weight, preferred_element_type=jnp.float32)
    looks = looks + jnp.dot(low, weight, preferred_element_type=jnp.float32)
    looks = looks.reshape(count, SUB, cols)
    block = lax.broadcasted_iota(jnp.int32, (1, SUB, cols), 1)
    lane = lax.broadcasted_iota(jnp.int32, (1, SUB, cols), 2)
    return jnp.sum(jnp.where(lane // per_block == block, looks, 0.0), axis=1)


def planes_of(ref, at):
    return [ref[at, 2 * k] for k in range(LOOK_AZ)], [ref[at, 2 * k + 1] for k in range(LOOK_AZ)]


OWN_PAIRS = [(d, range(1, inside(d) + 1)) for d in range(GROUP)]
LATER_PAIRS = [(d, range(inside(d) + 1, SPAN + 1)) for d in range(GROUP) if inside(d) < SPAN]
OWN_ROWS = sum(2 * len(gaps) for _, gaps in OWN_PAIRS)
LATER_ROWS = sum(2 * len(gaps) for _, gaps in LATER_PAIRS)


def own_kernel(own_ref, out_ref, sums):
    out_ref[...] = look_at(lambda d: planes_of(own_ref, GROUP - 1 - d), OWN_PAIRS, range(GROUP), sums, out_ref.shape[-1])


def later_kernel(own_ref, later_ref, looks_ref, out_ref, sums, cells):
    def date(index):
        if index < GROUP:
            return planes_of(own_ref, GROUP - 1 - index)
        return planes_of(later_ref, GROUP + SPAN - 1 - index)

    cells[...] = look_at(date, LATER_PAIRS, range(GROUP, GROUP + SPAN), sums, out_ref.shape[-1])
    own_at = later_at = 0
    for index in range(GROUP):
        near, far = inside(index), SPAN - inside(index)
        place = GROUP - 1 - index
        piece = out_ref.at[place, 0]
        for part in range(2):
            if near:
                piece[part * SPAN : part * SPAN + near, :] = looks_ref[own_at : own_at + near, :]
            if far:
                piece[part * SPAN + near : (part + 1) * SPAN, :] = cells[later_at : later_at + far, :]
            own_at += near
            later_at += far
        piece[2 * SPAN : 2 * SPAN + 1 + near, :] = looks_ref[OWN_ROWS + index : OWN_ROWS + index + 1 + near, :]
        if far:
            piece[2 * SPAN + 1 + near :, :] = cells[LATER_ROWS : LATER_ROWS + far, :]
        for tile in range(1, out_ref.shape[1]):
            out_ref[place, tile] = out_ref[place, 0]


def look_own(own, cols):
    rows = OWN_ROWS + GROUP
    return pl.pallas_call(
        own_kernel,
        out_shape=jax.ShapeDtypeStruct((rows, cols), jnp.float32),
        scratch_shapes=[pltpu.VMEM((rows * SUB, own.shape[-1]), jnp.float32)],
        compiler_params=pltpu.CompilerParams(vmem_limit_bytes=8 * 1024 * 1024),
        cost_estimate=pl.CostEstimate(
            flops=12 * rows * SUB * cols * cols, bytes_accessed=own.size * 4, transcendentals=0
        ),
        name="look_own",
    )(own)


def look_later(own, later, looks, tiles):
    cols = looks.shape[-1]
    rows = LATER_ROWS + SPAN
    return pl.pallas_call(
        later_kernel,
        out_shape=jax.ShapeDtypeStruct((GROUP, tiles, FIELDS, cols), jnp.float32),
        scratch_shapes=[
            pltpu.VMEM((rows * SUB, own.shape[-1]), jnp.float32),
            pltpu.VMEM((rows, cols), jnp.float32),
        ],
        compiler_params=pltpu.CompilerParams(vmem_limit_bytes=8 * 1024 * 1024),
        name="look_later",
    )(own, later, looks)


def coherence_kernel(tiles, rows_ref, looks_out, coher_out, looks_ref, boxes, coher_ref, sent):
    date, dates = lax.axis_index("date"), lax.axis_size("date")
    tile = lax.axis_index("az")
    cols = rows_ref.shape[-1]
    half = WIN // 2
    for gap in range(1, SPAN + 1):
        for part in range(2):
            start = tile * FIELDS + part * SPAN + gap - 1
            look = rows_ref[pl.ds(start, GROUP, stride=tiles * FIELDS), :]
            looks_ref[gap - 1, part, 0] = jnp.where(date + gap < dates, look, 0.0)
    looks_sent = pltpu.make_async_copy(looks_ref, looks_out, sent.at[0])
    looks_sent.start()

    lane = lax.broadcasted_iota(jnp.int32, (FIELDS, cols), 1)
    rows = []
    for offset in range(-half, GROUP + half):
        other = tile + offset // GROUP
        start = (offset % GROUP * tiles + jnp.clip(other, 0, tiles - 1)) * FIELDS
        row = rows_ref[pl.ds(pl.multiple_of(start, FIELDS), FIELDS), :]
        if not 0 <= offset < GROUP:
            row = jnp.where(jnp.logical_and(other >= 0, other < tiles), row, 0.0)
        rows.append(row)
    for r in range(GROUP):
        tall = rows[r]
        for shift in range(1, WIN):
            tall = tall + rows[r + shift]
        boxed = tall
        for shift in range(1, half + 1):
            boxed = boxed + jnp.where(lane >= shift, pltpu.roll(tall, shift, 1), 0.0)
            boxed = boxed + jnp.where(lane < cols - shift, pltpu.roll(tall, cols - shift, 1), 0.0)
        boxes[r * FIELDS : (r + 1) * FIELDS, :] = boxed
    fields = [boxes[pl.ds(field, GROUP, stride=FIELDS), :] for field in range(FIELDS)]
    own, later = fields[2 * SPAN], fields[2 * SPAN + 1 :]
    for gap in range(1, SPAN + 1):
        real, imag = fields[gap - 1], fields[SPAN + gap - 1]
        value = jnp.sqrt(real * real + imag * imag) / jnp.sqrt(own * later[gap - 1] + 1e-06)
        coher_ref[gap - 1, 0] = jnp.where(date + gap < dates, value, 0.0)
    coher_sent = pltpu.make_async_copy(coher_ref, coher_out, sent.at[1])
    coher_sent.start()
    looks_sent.wait()
    coher_sent.wait()


def finish(rows, tiles):
    cols = rows.shape[-1]
    looks = (SPAN, 2, 1, GROUP, cols)
    coher = (SPAN, 1, GROUP, cols)
    return pl.pallas_call(
        functools.partial(coherence_kernel, tiles),
        out_shape=(jax.ShapeDtypeStruct(looks, jnp.float32), jax.ShapeDtypeStruct(coher, jnp.float32)),
        out_specs=(pl.BlockSpec(memory_space=pl.ANY), pl.BlockSpec(memory_space=pl.ANY)),
        scratch_shapes=[
            pltpu.VMEM(looks, jnp.float32),
            pltpu.VMEM((GROUP * FIELDS, cols), jnp.float32),
            pltpu.VMEM(coher, jnp.float32),
            pltpu.SemaphoreType.DMA((2,)),
        ],
        compiler_params=pltpu.CompilerParams(vmem_limit_bytes=4 * 1024 * 1024),
        name="finish",
    )(rows)


def local(slabs):
    dates, tiles = lax.axis_size("date"), lax.axis_size("az")
    _, planes, lines, samples = slabs.shape
    cols = samples // LOOK_RG
    groups = [list(range(g, g + GROUP))[::-1] for g in range(0, dates, GROUP)]
    wide = [[d * tiles + a for d in group for a in range(tiles)] for group in groups]
    pieces = cut(slabs[0]).reshape(GROUP, LOOK_AZ * planes, SUB, samples // SUB)
    own = lax.all_to_all(pieces, "date", 0, 0, axis_index_groups=groups, tiled=True)
    back = [(i, i - GROUP) for i in range(GROUP, dates)]
    later = lax.ppermute(own[GROUP - SPAN :], "date", back)
    fields = look_later(own, later, look_own(own, cols), tiles)
    fields = fields.reshape(GROUP * tiles, FIELDS, cols)
    rows = lax.all_to_all(fields, ("date", "az"), 0, 0, axis_index_groups=wide, tiled=True)
    return finish(rows.reshape(GROUP * tiles * FIELDS, cols), tiles)


def solution(mesh):
    in_specs = (P("date", None, "az", None),)
    out_specs = (P(None, None, "date", "az", None), P(None, "date", "az", None))
    return jax.shard_map(local, mesh=mesh, in_specs=in_specs, out_specs=out_specs, check_vma=False)
```

```python
import functools

import jax
import jax.numpy as jnp
from jax import lax
from jax.experimental import pallas as pl
from jax.experimental.pallas import tpu as pltpu
from jax.sharding import PartitionSpec as P

LOOK_AZ = 4
LOOK_RG = 16
WIN = 5
SPAN = 5
GROUP = 8
FIELDS = 3 * SPAN + 1
SUB = 16


def cut_kernel(slab_ref, out_ref, held, arrived):
    planes, lines, _ = slab_ref.shape
    width = out_ref.shape[-1]
    copies = []
    for line in range(0, lines, 8):
        here = (pl.ds(0, planes), pl.ds(line, 8))
        copies.append(pltpu.make_async_copy(slab_ref.at[here], held.at[here], arrived.at[len(copies)]))
        copies[-1].start()
    for line, copy in zip(range(0, lines, 8), copies):
        copy.wait()
        for plane in range(planes):
            for block in range(SUB):
                part = held[plane, line : line + 8, block * width : (block + 1) * width]
                start = (line * planes + plane) * SUB + block
                out_ref[pl.ds(start, 8, stride=planes * SUB), :] = part


def cut(slab):
    planes, lines, samples = slab.shape
    rows = planes * lines * SUB
    slab = pltpu.with_memory_space_constraint(slab, pltpu.HBM)
    return pl.pallas_call(
        cut_kernel,
        in_specs=[pl.BlockSpec(memory_space=pl.ANY)],
        out_shape=jax.ShapeDtypeStruct((rows, samples // SUB), jnp.float32),
        scratch_shapes=[
            pltpu.VMEM(slab.shape, jnp.float32),
            pltpu.SemaphoreType.DMA((lines // 8,)),
        ],
        compiler_params=pltpu.CompilerParams(vmem_limit_bytes=4 * 1024 * 1024),
        name="cut",
    )(slab)


def inside(index):
    return min(SPAN, GROUP - 1 - index)


def look_at(date, pairs, powers, sums, cols):
    width = sums.shape[-1]
    count = 0

    def put(terms):
        nonlocal count
        total = terms[0]
        for term in terms[1:]:
            total = total + term
        sums[count * SUB : (count + 1) * SUB, :] = total
        count += 1

    for index, gaps in pairs:
        real, imag = date(index)
        others = [date(index + gap) for gap in gaps]
        for other_real, other_imag in others:
            put([a * b for a, b in zip(real + imag, other_real + other_imag)])
        for other_real, other_imag in others:
            put([a * b - c * d for a, b, c, d in zip(imag, other_real, real, other_imag)])
    for index in powers:
        real, imag = date(index)
        put([v * v for v in real + imag])

    per_block = width // LOOK_RG
    sample = lax.broadcasted_iota(jnp.int32, (width, cols), 0)
    lane = lax.broadcasted_iota(jnp.int32, (width, cols), 1)
    weight = jnp.where(sample // LOOK_RG == lane % per_block, 1.0 / (LOOK_AZ * LOOK_RG), 0.0)
    weight = weight.astype(jnp.bfloat16)
    total = sums[: count * SUB, :]
    high = total.astype(jnp.bfloat16)
    low = (total - high.astype(jnp.float32)).astype(jnp.bfloat16)
    looks = jnp.dot(high, weight, preferred_element_type=jnp.float32)
    looks = looks + jnp.dot(low, weight, preferred_element_type=jnp.float32)
    looks = looks.reshape(count, SUB, cols)
    block = lax.broadcasted_iota(jnp.int32, (1, SUB, cols), 1)
    lane = lax.broadcasted_iota(jnp.int32, (1, SUB, cols), 2)
    return jnp.sum(jnp.where(lane // per_block == block, looks, 0.0), axis=1)


def planes_of(ref, at):
    return [ref[at, 2 * k] for k in range(LOOK_AZ)], [ref[at, 2 * k + 1] for k in range(LOOK_AZ)]


OWN_PAIRS = [(d, range(1, inside(d) + 1)) for d in range(GROUP)]
LATER_PAIRS = [(d, range(inside(d) + 1, SPAN + 1)) for d in range(GROUP) if inside(d) < SPAN]
OWN_ROWS = sum(2 * len(gaps) for _, gaps in OWN_PAIRS)
LATER_ROWS = sum(2 * len(gaps) for _, gaps in LATER_PAIRS)


def own_kernel(own_ref, out_ref, sums):
    out_ref[...] = look_at(lambda d: planes_of(own_ref, GROUP - 1 - d), OWN_PAIRS, range(GROUP), sums, out_ref.shape[-1])


def later_kernel(own_ref, later_ref, looks_ref, out_ref, sums, cells):
    def date(index):
        if index < GROUP:
            return planes_of(own_ref, GROUP - 1 - index)
        return planes_of(later_ref, GROUP + SPAN - 1 - index)

    cells[...] = look_at(date, LATER_PAIRS, range(GROUP, GROUP + SPAN), sums, out_ref.shape[-1])
    own_at = later_at = 0
    for index in range(GROUP):
        near, far = inside(index), SPAN - inside(index)
        place = GROUP - 1 - index
        piece = out_ref.at[place, 0]
        for part in range(2):
            if near:
                piece[part * SPAN : part * SPAN + near, :] = looks_ref[own_at : own_at + near, :]
            if far:
                piece[part * SPAN + near : (part + 1) * SPAN, :] = cells[later_at : later_at + far, :]
            own_at += near
            later_at += far
        piece[2 * SPAN : 2 * SPAN + 1 + near, :] = looks_ref[OWN_ROWS + index : OWN_ROWS + index + 1 + near, :]
        if far:
            piece[2 * SPAN + 1 + near :, :] = cells[LATER_ROWS : LATER_ROWS + far, :]
        for tile in range(1, out_ref.shape[1]):
            out_ref[place, tile] = out_ref[place, 0]


def look_own(own, cols):
    rows = OWN_ROWS + GROUP
    return pl.pallas_call(
        own_kernel,
        out_shape=jax.ShapeDtypeStruct((rows, cols), jnp.float32),
        scratch_shapes=[pltpu.VMEM((rows * SUB, own.shape[-1]), jnp.float32)],
        compiler_params=pltpu.CompilerParams(vmem_limit_bytes=8 * 1024 * 1024),
        cost_estimate=pl.CostEstimate(
            flops=12 * rows * SUB * cols * cols, bytes_accessed=own.size * 4, transcendentals=0
        ),
        name="look_own",
    )(own)


def look_later(own, later, looks, tiles):
    cols = looks.shape[-1]
    rows = LATER_ROWS + SPAN
    return pl.pallas_call(
        later_kernel,
        out_shape=jax.ShapeDtypeStruct((GROUP, tiles, FIELDS, cols), jnp.float32),
        scratch_shapes=[
            pltpu.VMEM((rows * SUB, own.shape[-1]), jnp.float32),
            pltpu.VMEM((rows, cols), jnp.float32),
        ],
        compiler_params=pltpu.CompilerParams(vmem_limit_bytes=8 * 1024 * 1024),
        name="look_later",
    )(own, later, looks)


def coherence_kernel(tiles, rows_ref, looks_out, coher_out, looks_ref, boxes, coher_ref, sent):
    date, dates = lax.axis_index("date"), lax.axis_size("date")
    tile = lax.axis_index("az")
    cols = rows_ref.shape[-1]
    half = WIN // 2
    for gap in range(1, SPAN + 1):
        for part in range(2):
            start = (tiles - 1 - tile) * FIELDS + part * SPAN + gap - 1
            look = rows_ref[pl.ds(start, GROUP, stride=tiles * FIELDS), :]
            looks_ref[gap - 1, part, 0] = jnp.where(date + gap < dates, look, 0.0)
    looks_sent = pltpu.make_async_copy(looks_ref, looks_out, sent.at[0])
    looks_sent.start()

    lane = lax.broadcasted_iota(jnp.int32, (FIELDS, cols), 1)
    rows = []
    for offset in range(-half, GROUP + half):
        other = tile + offset // GROUP
        start = (offset % GROUP * tiles + tiles - 1 - jnp.clip(other, 0, tiles - 1)) * FIELDS
        row = rows_ref[pl.ds(pl.multiple_of(start, FIELDS), FIELDS), :]
        if not 0 <= offset < GROUP:
            row = jnp.where(jnp.logical_and(other >= 0, other < tiles), row, 0.0)
        rows.append(row)
    for r in range(GROUP):
        tall = rows[r]
        for shift in range(1, WIN):
            tall = tall + rows[r + shift]
        boxed = tall
        for shift in range(1, half + 1):
            boxed = boxed + jnp.where(lane >= shift, pltpu.roll(tall, shift, 1), 0.0)
            boxed = boxed + jnp.where(lane < cols - shift, pltpu.roll(tall, cols - shift, 1), 0.0)
        boxes[r * FIELDS : (r + 1) * FIELDS, :] = boxed
    fields = [boxes[pl.ds(field, GROUP, stride=FIELDS), :] for field in range(FIELDS)]
    own, later = fields[2 * SPAN], fields[2 * SPAN + 1 :]
    for gap in range(1, SPAN + 1):
        real, imag = fields[gap - 1], fields[SPAN + gap - 1]
        value = jnp.sqrt(real * real + imag * imag) / jnp.sqrt(own * later[gap - 1] + 1e-06)
        coher_ref[gap - 1, 0] = jnp.where(date + gap < dates, value, 0.0)
    coher_sent = pltpu.make_async_copy(coher_ref, coher_out, sent.at[1])
    coher_sent.start()
    looks_sent.wait()
    coher_sent.wait()


def finish(rows, tiles):
    cols = rows.shape[-1]
    looks = (SPAN, 2, 1, GROUP, cols)
    coher = (SPAN, 1, GROUP, cols)
    return pl.pallas_call(
        functools.partial(coherence_kernel, tiles),
        out_shape=(jax.ShapeDtypeStruct(looks, jnp.float32), jax.ShapeDtypeStruct(coher, jnp.float32)),
        out_specs=(pl.BlockSpec(memory_space=pl.ANY), pl.BlockSpec(memory_space=pl.ANY)),
        scratch_shapes=[
            pltpu.VMEM(looks, jnp.float32),
            pltpu.VMEM((GROUP * FIELDS, cols), jnp.float32),
            pltpu.VMEM(coher, jnp.float32),
            pltpu.SemaphoreType.DMA((2,)),
        ],
        compiler_params=pltpu.CompilerParams(vmem_limit_bytes=4 * 1024 * 1024),
        name="finish",
    )(rows)


def local(slabs):
    dates, tiles = lax.axis_size("date"), lax.axis_size("az")
    _, planes, lines, samples = slabs.shape
    cols = samples // LOOK_RG
    groups = [list(range(g, g + GROUP))[::-1] for g in range(0, dates, GROUP)]
    wide = [[d * tiles + a for d in group for a in range(tiles)[::-1]] for group in groups]
    pieces = cut(slabs[0]).reshape(GROUP, LOOK_AZ * planes, SUB, samples // SUB)
    own = lax.all_to_all(pieces, "date", 0, 0, axis_index_groups=groups, tiled=True)
    back = [(i, i - GROUP) for i in range(GROUP, dates)]
    later = lax.ppermute(own[GROUP - SPAN :], "date", back)
    fields = look_later(own, later, look_own(own, cols), tiles)
    fields = fields.reshape(GROUP * tiles, FIELDS, cols)
    rows = lax.all_to_all(fields, ("date", "az"), 0, 0, axis_index_groups=wide, tiled=True)
    return finish(rows.reshape(GROUP * tiles * FIELDS, cols), tiles)


def solution(mesh):
    in_specs = (P("date", None, "az", None),)
    out_specs = (P(None, None, "date", "az", None), P(None, "date", "az", None))
    return jax.shard_map(local, mesh=mesh, in_specs=in_specs, out_specs=out_specs, check_vma=False)
```

```python
import functools

import jax
import jax.numpy as jnp
from jax import lax
from jax.experimental import pallas as pl
from jax.experimental.pallas import tpu as pltpu
from jax.sharding import PartitionSpec as P

LOOK_AZ = 4
LOOK_RG = 16
WIN = 5
SPAN = 5
GROUP = 8
FIELDS = 3 * SPAN + 1
SUB = 16


def cut_kernel(slab_ref, out_ref, held, arrived):
    planes, lines, _ = slab_ref.shape
    width = out_ref.shape[-1]
    copies = []
    for line in range(0, lines, 8):
        here = (pl.ds(0, planes), pl.ds(line, 8))
        copies.append(pltpu.make_async_copy(slab_ref.at[here], held.at[here], arrived.at[len(copies)]))
        copies[-1].start()
    for line, copy in zip(range(0, lines, 8), copies):
        copy.wait()
        for plane in range(planes):
            for block in range(SUB):
                part = held[plane, line : line + 8, block * width : (block + 1) * width]
                start = (line * planes + plane) * SUB + block
                out_ref[pl.ds(start, 8, stride=planes * SUB), :] = part


def cut(slab):
    planes, lines, samples = slab.shape
    rows = planes * lines * SUB
    slab = pltpu.with_memory_space_constraint(slab, pltpu.HBM)
    return pl.pallas_call(
        cut_kernel,
        in_specs=[pl.BlockSpec(memory_space=pl.ANY)],
        out_shape=jax.ShapeDtypeStruct((rows, samples // SUB), jnp.float32),
        scratch_shapes=[
            pltpu.VMEM(slab.shape, jnp.float32),
            pltpu.SemaphoreType.DMA((lines // 8,)),
        ],
        compiler_params=pltpu.CompilerParams(vmem_limit_bytes=4 * 1024 * 1024),
        name="cut",
    )(slab)


def inside(index):
    return min(SPAN, GROUP - 1 - index)


def at(tile, row, tiles):
    return (tile % 2 * GROUP + row) * (tiles // 2) + tiles // 2 - 1 - tile // 2


def look_at(date, pairs, powers, sums, cols):
    width = sums.shape[-1]
    count = 0

    def put(terms):
        nonlocal count
        total = terms[0]
        for term in terms[1:]:
            total = total + term
        sums[count * SUB : (count + 1) * SUB, :] = total
        count += 1

    for index, gaps in pairs:
        real, imag = date(index)
        others = [date(index + gap) for gap in gaps]
        for other_real, other_imag in others:
            put([a * b for a, b in zip(real + imag, other_real + other_imag)])
        for other_real, other_imag in others:
            put([a * b - c * d for a, b, c, d in zip(imag, other_real, real, other_imag)])
    for index in powers:
        real, imag = date(index)
        put([v * v for v in real + imag])

    per_block = width // LOOK_RG
    sample = lax.broadcasted_iota(jnp.int32, (width, cols), 0)
    lane = lax.broadcasted_iota(jnp.int32, (width, cols), 1)
    weight = jnp.where(sample // LOOK_RG == lane % per_block, 1.0 / (LOOK_AZ * LOOK_RG), 0.0)
    weight = weight.astype(jnp.bfloat16)
    total = sums[: count * SUB, :]
    high = total.astype(jnp.bfloat16)
    low = (total - high.astype(jnp.float32)).astype(jnp.bfloat16)
    looks = jnp.dot(high, weight, preferred_element_type=jnp.float32)
    looks = looks + jnp.dot(low, weight, preferred_element_type=jnp.float32)
    looks = looks.reshape(count, SUB, cols)
    block = lax.broadcasted_iota(jnp.int32, (1, SUB, cols), 1)
    lane = lax.broadcasted_iota(jnp.int32, (1, SUB, cols), 2)
    return jnp.sum(jnp.where(lane // per_block == block, looks, 0.0), axis=1)


def planes_of(ref, at):
    return [ref[at, 2 * k] for k in range(LOOK_AZ)], [ref[at, 2 * k + 1] for k in range(LOOK_AZ)]


OWN_PAIRS = [(d, range(1, inside(d) + 1)) for d in range(GROUP)]
LATER_PAIRS = [(d, range(inside(d) + 1, SPAN + 1)) for d in range(GROUP) if inside(d) < SPAN]
OWN_ROWS = sum(2 * len(gaps) for _, gaps in OWN_PAIRS)
LATER_ROWS = sum(2 * len(gaps) for _, gaps in LATER_PAIRS)


def own_kernel(own_ref, out_ref, sums):
    out_ref[...] = look_at(lambda d: planes_of(own_ref, GROUP - 1 - d), OWN_PAIRS, range(GROUP), sums, out_ref.shape[-1])


def later_kernel(own_ref, later_ref, looks_ref, out_ref, sums, cells):
    def date(index):
        if index < GROUP:
            return planes_of(own_ref, GROUP - 1 - index)
        return planes_of(later_ref, GROUP + SPAN - 1 - index)

    cells[...] = look_at(date, LATER_PAIRS, range(GROUP, GROUP + SPAN), sums, out_ref.shape[-1])
    tiles = out_ref.shape[0] // GROUP
    own_at = later_at = 0
    for index in range(GROUP):
        near, far = inside(index), SPAN - inside(index)
        place = GROUP - 1 - index
        piece = out_ref.at[at(0, place, tiles)]
        for part in range(2):
            if near:
                piece[part * SPAN : part * SPAN + near, :] = looks_ref[own_at : own_at + near, :]
            if far:
                piece[part * SPAN + near : (part + 1) * SPAN, :] = cells[later_at : later_at + far, :]
            own_at += near
            later_at += far
        piece[2 * SPAN : 2 * SPAN + 1 + near, :] = looks_ref[OWN_ROWS + index : OWN_ROWS + index + 1 + near, :]
        if far:
            piece[2 * SPAN + 1 + near :, :] = cells[LATER_ROWS : LATER_ROWS + far, :]
        for tile in range(1, tiles):
            out_ref[at(tile, place, tiles)] = out_ref[at(0, place, tiles)]


def look_own(own, cols):
    rows = OWN_ROWS + GROUP
    return pl.pallas_call(
        own_kernel,
        out_shape=jax.ShapeDtypeStruct((rows, cols), jnp.float32),
        scratch_shapes=[pltpu.VMEM((rows * SUB, own.shape[-1]), jnp.float32)],
        compiler_params=pltpu.CompilerParams(vmem_limit_bytes=8 * 1024 * 1024),
        cost_estimate=pl.CostEstimate(
            flops=12 * rows * SUB * cols * cols, bytes_accessed=own.size * 4, transcendentals=0
        ),
        name="look_own",
    )(own)


def look_later(own, later, looks, tiles):
    cols = looks.shape[-1]
    rows = LATER_ROWS + SPAN
    return pl.pallas_call(
        later_kernel,
        out_shape=jax.ShapeDtypeStruct((GROUP * tiles, FIELDS, cols), jnp.float32),
        scratch_shapes=[
            pltpu.VMEM((rows * SUB, own.shape[-1]), jnp.float32),
            pltpu.VMEM((rows, cols), jnp.float32),
        ],
        compiler_params=pltpu.CompilerParams(vmem_limit_bytes=8 * 1024 * 1024),
        name="look_later",
    )(own, later, looks)


def coherence_kernel(tiles, rows_ref, looks_out, coher_out, looks_ref, boxes, coher_ref, sent):
    date, dates = lax.axis_index("date"), lax.axis_size("date")
    tile = lax.axis_index("az")
    cols = rows_ref.shape[-1]
    half = WIN // 2
    for gap in range(1, SPAN + 1):
        for part in range(2):
            start = at(tile, 0, tiles) * FIELDS + part * SPAN + gap - 1
            look = rows_ref[pl.ds(start, GROUP, stride=tiles // 2 * FIELDS), :]
            looks_ref[gap - 1, part, 0] = jnp.where(date + gap < dates, look, 0.0)
    looks_sent = pltpu.make_async_copy(looks_ref, looks_out, sent.at[0])
    looks_sent.start()

    lane = lax.broadcasted_iota(jnp.int32, (FIELDS, cols), 1)
    rows = []
    for offset in range(-half, GROUP + half):
        other = tile + offset // GROUP
        start = at(jnp.clip(other, 0, tiles - 1), offset % GROUP, tiles) * FIELDS
        row = rows_ref[pl.ds(pl.multiple_of(start, FIELDS), FIELDS), :]
        if not 0 <= offset < GROUP:
            row = jnp.where(jnp.logical_and(other >= 0, other < tiles), row, 0.0)
        rows.append(row)
    for r in range(GROUP):
        tall = rows[r]
        for shift in range(1, WIN):
            tall = tall + rows[r + shift]
        boxed = tall
        for shift in range(1, half + 1):
            boxed = boxed + jnp.where(lane >= shift, pltpu.roll(tall, shift, 1), 0.0)
            boxed = boxed + jnp.where(lane < cols - shift, pltpu.roll(tall, cols - shift, 1), 0.0)
        boxes[r * FIELDS : (r + 1) * FIELDS, :] = boxed
    fields = [boxes[pl.ds(field, GROUP, stride=FIELDS), :] for field in range(FIELDS)]
    own, later = fields[2 * SPAN], fields[2 * SPAN + 1 :]
    for gap in range(1, SPAN + 1):
        real, imag = fields[gap - 1], fields[SPAN + gap - 1]
        value = jnp.sqrt(real * real + imag * imag) / jnp.sqrt(own * later[gap - 1] + 1e-06)
        coher_ref[gap - 1, 0] = jnp.where(date + gap < dates, value, 0.0)
    coher_sent = pltpu.make_async_copy(coher_ref, coher_out, sent.at[1])
    coher_sent.start()
    looks_sent.wait()
    coher_sent.wait()


def finish(rows, tiles):
    cols = rows.shape[-1]
    looks = (SPAN, 2, 1, GROUP, cols)
    coher = (SPAN, 1, GROUP, cols)
    return pl.pallas_call(
        functools.partial(coherence_kernel, tiles),
        out_shape=(jax.ShapeDtypeStruct(looks, jnp.float32), jax.ShapeDtypeStruct(coher, jnp.float32)),
        out_specs=(pl.BlockSpec(memory_space=pl.ANY), pl.BlockSpec(memory_space=pl.ANY)),
        scratch_shapes=[
            pltpu.VMEM(looks, jnp.float32),
            pltpu.VMEM((GROUP * FIELDS, cols), jnp.float32),
            pltpu.VMEM(coher, jnp.float32),
            pltpu.SemaphoreType.DMA((2,)),
        ],
        compiler_params=pltpu.CompilerParams(vmem_limit_bytes=4 * 1024 * 1024),
        name="finish",
    )(rows)


def local(slabs):
    dates, tiles = lax.axis_size("date"), lax.axis_size("az")
    _, planes, lines, samples = slabs.shape
    cols = samples // LOOK_RG
    groups = [list(range(g, g + GROUP))[::-1] for g in range(0, dates, GROUP)]
    places = sorted((at(a, row, tiles), row, a) for row in range(GROUP) for a in range(tiles))
    wide = [[group[row] * tiles + a for _, row, a in places] for group in groups]
    pieces = cut(slabs[0]).reshape(GROUP, LOOK_AZ * planes, SUB, samples // SUB)
    own = lax.all_to_all(pieces, "date", 0, 0, axis_index_groups=groups, tiled=True)
    back = [(i, i - GROUP) for i in range(GROUP, dates)]
    later = lax.ppermute(own[GROUP - SPAN :], "date", back)
    fields = look_later(own, later, look_own(own, cols), tiles)
    rows = lax.all_to_all(fields, ("date", "az"), 0, 0, axis_index_groups=wide, tiled=True)
    return finish(rows.reshape(GROUP * tiles * FIELDS, cols), tiles)


def solution(mesh):
    in_specs = (P("date", None, "az", None),)
    out_specs = (P(None, None, "date", "az", None), P(None, "date", "az", None))
    return jax.shard_map(local, mesh=mesh, in_specs=in_specs, out_specs=out_specs, check_vma=False)
```

```python
import functools

import jax
import jax.numpy as jnp
from jax import lax
from jax.experimental import pallas as pl
from jax.experimental.pallas import tpu as pltpu
from jax.sharding import PartitionSpec as P

LOOK_AZ = 4
LOOK_RG = 16
WIN = 5
SPAN = 5
GROUP = 8
FIELDS = 3 * SPAN + 1
ORDER = (5, 7, 6, 4, 3, 2, 1, 0)
SUB = 16


def cut_kernel(slab_ref, out_ref, held, arrived):
    planes, lines, _ = slab_ref.shape
    width = out_ref.shape[-1]
    copies = []
    for line in range(0, lines, 8):
        here = (pl.ds(0, planes), pl.ds(line, 8))
        copies.append(pltpu.make_async_copy(slab_ref.at[here], held.at[here], arrived.at[len(copies)]))
        copies[-1].start()
    for line, copy in zip(range(0, lines, 8), copies):
        copy.wait()
        for plane in range(planes):
            for block in range(SUB):
                part = held[plane, line : line + 8, block * width : (block + 1) * width]
                start = (line * planes + plane) * SUB + block
                out_ref[pl.ds(start, 8, stride=planes * SUB), :] = part


def cut(slab):
    planes, lines, samples = slab.shape
    rows = planes * lines * SUB
    slab = pltpu.with_memory_space_constraint(slab, pltpu.HBM)
    return pl.pallas_call(
        cut_kernel,
        in_specs=[pl.BlockSpec(memory_space=pl.ANY)],
        out_shape=jax.ShapeDtypeStruct((rows, samples // SUB), jnp.float32),
        scratch_shapes=[
            pltpu.VMEM(slab.shape, jnp.float32),
            pltpu.SemaphoreType.DMA((lines // 8,)),
        ],
        compiler_params=pltpu.CompilerParams(vmem_limit_bytes=4 * 1024 * 1024),
        name="cut",
    )(slab)


def inside(index):
    return min(SPAN, GROUP - 1 - index)


def at(tile, row, tiles):
    return (tile % 2 * GROUP + row) * (tiles // 2) + tiles // 2 - 1 - tile // 2


def look_at(date, pairs, powers, sums, cols):
    width = sums.shape[-1]
    count = 0

    def put(terms):
        nonlocal count
        total = terms[0]
        for term in terms[1:]:
            total = total + term
        sums[count * SUB : (count + 1) * SUB, :] = total
        count += 1

    for index, gaps in pairs:
        real, imag = date(index)
        others = [date(index + gap) for gap in gaps]
        for other_real, other_imag in others:
            put([a * b for a, b in zip(real + imag, other_real + other_imag)])
        for other_real, other_imag in others:
            put([a * b - c * d for a, b, c, d in zip(imag, other_real, real, other_imag)])
    for index in powers:
        real, imag = date(index)
        put([v * v for v in real + imag])

    per_block = width // LOOK_RG
    sample = lax.broadcasted_iota(jnp.int32, (width, cols), 0)
    lane = lax.broadcasted_iota(jnp.int32, (width, cols), 1)
    weight = jnp.where(sample // LOOK_RG == lane % per_block, 1.0 / (LOOK_AZ * LOOK_RG), 0.0)
    weight = weight.astype(jnp.bfloat16)
    total = sums[: count * SUB, :]
    high = total.astype(jnp.bfloat16)
    low = (total - high.astype(jnp.float32)).astype(jnp.bfloat16)
    looks = jnp.dot(high, weight, preferred_element_type=jnp.float32)
    looks = looks + jnp.dot(low, weight, preferred_element_type=jnp.float32)
    looks = looks.reshape(count, SUB, cols)
    block = lax.broadcasted_iota(jnp.int32, (1, SUB, cols), 1)
    lane = lax.broadcasted_iota(jnp.int32, (1, SUB, cols), 2)
    return jnp.sum(jnp.where(lane // per_block == block, looks, 0.0), axis=1)


def planes_of(ref, at):
    return [ref[at, 2 * k] for k in range(LOOK_AZ)], [ref[at, 2 * k + 1] for k in range(LOOK_AZ)]


OWN_PAIRS = [(d, range(1, inside(d) + 1)) for d in range(GROUP)]
LATER_PAIRS = [(d, range(inside(d) + 1, SPAN + 1)) for d in range(GROUP) if inside(d) < SPAN]
OWN_ROWS = sum(2 * len(gaps) for _, gaps in OWN_PAIRS)
LATER_ROWS = sum(2 * len(gaps) for _, gaps in LATER_PAIRS)


def own_kernel(own_ref, out_ref, sums):
    out_ref[...] = look_at(lambda d: planes_of(own_ref, ORDER.index(d)), OWN_PAIRS, range(GROUP), sums, out_ref.shape[-1])


def later_kernel(own_ref, later_ref, looks_ref, out_ref, sums, cells):
    def date(index):
        if index < GROUP:
            return planes_of(own_ref, ORDER.index(index))
        return planes_of(later_ref, ORDER.index(index - GROUP) - (GROUP - SPAN))

    cells[...] = look_at(date, LATER_PAIRS, range(GROUP, GROUP + SPAN), sums, out_ref.shape[-1])
    tiles = out_ref.shape[0] // GROUP
    own_at = later_at = 0
    for index in range(GROUP):
        near, far = inside(index), SPAN - inside(index)
        place = ORDER.index(index)
        piece = out_ref.at[at(0, place, tiles)]
        for part in range(2):
            if near:
                piece[part * SPAN : part * SPAN + near, :] = looks_ref[own_at : own_at + near, :]
            if far:
                piece[part * SPAN + near : (part + 1) * SPAN, :] = cells[later_at : later_at + far, :]
            own_at += near
            later_at += far
        piece[2 * SPAN : 2 * SPAN + 1 + near, :] = looks_ref[OWN_ROWS + index : OWN_ROWS + index + 1 + near, :]
        if far:
            piece[2 * SPAN + 1 + near :, :] = cells[LATER_ROWS : LATER_ROWS + far, :]
        for tile in range(1, tiles):
            out_ref[at(tile, place, tiles)] = out_ref[at(0, place, tiles)]


def look_own(own, cols):
    rows = OWN_ROWS + GROUP
    return pl.pallas_call(
        own_kernel,
        out_shape=jax.ShapeDtypeStruct((rows, cols), jnp.float32),
        scratch_shapes=[pltpu.VMEM((rows * SUB, own.shape[-1]), jnp.float32)],
        compiler_params=pltpu.CompilerParams(vmem_limit_bytes=8 * 1024 * 1024),
        cost_estimate=pl.CostEstimate(
            flops=12 * rows * SUB * cols * cols, bytes_accessed=own.size * 4, transcendentals=0
        ),
        name="look_own",
    )(own)


def look_later(own, later, looks, tiles):
    cols = looks.shape[-1]
    rows = LATER_ROWS + SPAN
    return pl.pallas_call(
        later_kernel,
        out_shape=jax.ShapeDtypeStruct((GROUP * tiles, FIELDS, cols), jnp.float32),
        scratch_shapes=[
            pltpu.VMEM((rows * SUB, own.shape[-1]), jnp.float32),
            pltpu.VMEM((rows, cols), jnp.float32),
        ],
        compiler_params=pltpu.CompilerParams(vmem_limit_bytes=8 * 1024 * 1024),
        name="look_later",
    )(own, later, looks)


def coherence_kernel(tiles, rows_ref, looks_out, coher_out, looks_ref, boxes, coher_ref, sent):
    date, dates = lax.axis_index("date"), lax.axis_size("date")
    tile = lax.axis_index("az")
    cols = rows_ref.shape[-1]
    half = WIN // 2
    for gap in range(1, SPAN + 1):
        for part in range(2):
            start = at(tile, 0, tiles) * FIELDS + part * SPAN + gap - 1
            look = rows_ref[pl.ds(start, GROUP, stride=tiles // 2 * FIELDS), :]
            looks_ref[gap - 1, part, 0] = jnp.where(date + gap < dates, look, 0.0)
    looks_sent = pltpu.make_async_copy(looks_ref, looks_out, sent.at[0])
    looks_sent.start()

    lane = lax.broadcasted_iota(jnp.int32, (FIELDS, cols), 1)
    rows = []
    for offset in range(-half, GROUP + half):
        other = tile + offset // GROUP
        start = at(jnp.clip(other, 0, tiles - 1), offset % GROUP, tiles) * FIELDS
        row = rows_ref[pl.ds(pl.multiple_of(start, FIELDS), FIELDS), :]
        if not 0 <= offset < GROUP:
            row = jnp.where(jnp.logical_and(other >= 0, other < tiles), row, 0.0)
        rows.append(row)
    for r in range(GROUP):
        tall = rows[r]
        for shift in range(1, WIN):
            tall = tall + rows[r + shift]
        boxed = tall
        for shift in range(1, half + 1):
            boxed = boxed + jnp.where(lane >= shift, pltpu.roll(tall, shift, 1), 0.0)
            boxed = boxed + jnp.where(lane < cols - shift, pltpu.roll(tall, cols - shift, 1), 0.0)
        boxes[r * FIELDS : (r + 1) * FIELDS, :] = boxed
    fields = [boxes[pl.ds(field, GROUP, stride=FIELDS), :] for field in range(FIELDS)]
    own, later = fields[2 * SPAN], fields[2 * SPAN + 1 :]
    for gap in range(1, SPAN + 1):
        real, imag = fields[gap - 1], fields[SPAN + gap - 1]
        value = jnp.sqrt(real * real + imag * imag) / jnp.sqrt(own * later[gap - 1] + 1e-06)
        coher_ref[gap - 1, 0] = jnp.where(date + gap < dates, value, 0.0)
    coher_sent = pltpu.make_async_copy(coher_ref, coher_out, sent.at[1])
    coher_sent.start()
    looks_sent.wait()
    coher_sent.wait()


def finish(rows, tiles):
    cols = rows.shape[-1]
    looks = (SPAN, 2, 1, GROUP, cols)
    coher = (SPAN, 1, GROUP, cols)
    return pl.pallas_call(
        functools.partial(coherence_kernel, tiles),
        out_shape=(jax.ShapeDtypeStruct(looks, jnp.float32), jax.ShapeDtypeStruct(coher, jnp.float32)),
        out_specs=(pl.BlockSpec(memory_space=pl.ANY), pl.BlockSpec(memory_space=pl.ANY)),
        scratch_shapes=[
            pltpu.VMEM(looks, jnp.float32),
            pltpu.VMEM((GROUP * FIELDS, cols), jnp.float32),
            pltpu.VMEM(coher, jnp.float32),
            pltpu.SemaphoreType.DMA((2,)),
        ],
        compiler_params=pltpu.CompilerParams(vmem_limit_bytes=4 * 1024 * 1024),
        name="finish",
    )(rows)


def local(slabs):
    dates, tiles = lax.axis_size("date"), lax.axis_size("az")
    _, planes, lines, samples = slabs.shape
    cols = samples // LOOK_RG
    groups = [[g + d for d in ORDER] for g in range(0, dates, GROUP)]
    places = sorted((at(a, row, tiles), row, a) for row in range(GROUP) for a in range(tiles))
    wide = [[group[row] * tiles + a for _, row, a in places] for group in groups]
    pieces = cut(slabs[0]).reshape(GROUP, LOOK_AZ * planes, SUB, samples // SUB)
    own = lax.all_to_all(pieces, "date", 0, 0, axis_index_groups=groups, tiled=True)
    back = [(i, i - GROUP) for i in range(GROUP, dates)]
    later = lax.ppermute(own[GROUP - SPAN :], "date", back)
    fields = look_later(own, later, look_own(own, cols), tiles)
    rows = lax.all_to_all(fields, ("date", "az"), 0, 0, axis_index_groups=wide, tiled=True)
    return finish(rows.reshape(GROUP * tiles * FIELDS, cols), tiles)


def solution(mesh):
    in_specs = (P("date", None, "az", None),)
    out_specs = (P(None, None, "date", "az", None), P(None, "date", "az", None))
    return jax.shard_map(local, mesh=mesh, in_specs=in_specs, out_specs=out_specs, check_vma=False)
```

```python
import functools

import jax
import jax.numpy as jnp
from jax import lax
from jax.experimental import pallas as pl
from jax.experimental.pallas import tpu as pltpu
from jax.sharding import PartitionSpec as P

LOOK_AZ = 4
LOOK_RG = 16
WIN = 5
SPAN = 5
GROUP = 8
FIELDS = 3 * SPAN + 1
ORDERS = ((5, 7, 6, 4, 3, 2, 1, 0), (7, 6, 5, 3, 4, 1, 0, 2))
SUB = 16


def cut_kernel(slab_ref, out_ref, held, arrived):
    planes, lines, _ = slab_ref.shape
    width = out_ref.shape[-1]
    copies = []
    for line in range(0, lines, 8):
        here = (pl.ds(0, planes), pl.ds(line, 8))
        copies.append(pltpu.make_async_copy(slab_ref.at[here], held.at[here], arrived.at[len(copies)]))
        copies[-1].start()
    for line, copy in zip(range(0, lines, 8), copies):
        copy.wait()
        for plane in range(planes):
            for block in range(SUB):
                part = held[plane, line : line + 8, block * width : (block + 1) * width]
                start = (line * planes + plane) * SUB + block
                out_ref[pl.ds(start, 8, stride=planes * SUB), :] = part


def cut(slab):
    planes, lines, samples = slab.shape
    rows = planes * lines * SUB
    slab = pltpu.with_memory_space_constraint(slab, pltpu.HBM)
    return pl.pallas_call(
        cut_kernel,
        in_specs=[pl.BlockSpec(memory_space=pl.ANY)],
        out_shape=jax.ShapeDtypeStruct((rows, samples // SUB), jnp.float32),
        scratch_shapes=[
            pltpu.VMEM(slab.shape, jnp.float32),
            pltpu.SemaphoreType.DMA((lines // 8,)),
        ],
        compiler_params=pltpu.CompilerParams(vmem_limit_bytes=4 * 1024 * 1024),
        name="cut",
    )(slab)


def inside(index):
    return min(SPAN, GROUP - 1 - index)


def at(tile, row, tiles):
    return (tile % 2 * GROUP + row) * (tiles // 2) + tiles // 2 - 1 - tile // 2


def place_of(date):
    odd = lax.rem(lax.axis_index("az"), 2) == 1
    return jnp.where(odd, ORDERS[1].index(date), ORDERS[0].index(date))


def look_at(date, pairs, powers, sums, cols):
    width = sums.shape[-1]
    count = 0

    def put(terms):
        nonlocal count
        total = terms[0]
        for term in terms[1:]:
            total = total + term
        sums[count * SUB : (count + 1) * SUB, :] = total
        count += 1

    for index, gaps in pairs:
        real, imag = date(index)
        others = [date(index + gap) for gap in gaps]
        for other_real, other_imag in others:
            put([a * b for a, b in zip(real + imag, other_real + other_imag)])
        for other_real, other_imag in others:
            put([a * b - c * d for a, b, c, d in zip(imag, other_real, real, other_imag)])
    for index in powers:
        real, imag = date(index)
        put([v * v for v in real + imag])

    per_block = width // LOOK_RG
    sample = lax.broadcasted_iota(jnp.int32, (width, cols), 0)
    lane = lax.broadcasted_iota(jnp.int32, (width, cols), 1)
    weight = jnp.where(sample // LOOK_RG == lane % per_block, 1.0 / (LOOK_AZ * LOOK_RG), 0.0)
    weight = weight.astype(jnp.bfloat16)
    total = sums[: count * SUB, :]
    high = total.astype(jnp.bfloat16)
    low = (total - high.astype(jnp.float32)).astype(jnp.bfloat16)
    looks = jnp.dot(high, weight, preferred_element_type=jnp.float32)
    looks = looks + jnp.dot(low, weight, preferred_element_type=jnp.float32)
    looks = looks.reshape(count, SUB, cols)
    block = lax.broadcasted_iota(jnp.int32, (1, SUB, cols), 1)
    lane = lax.broadcasted_iota(jnp.int32, (1, SUB, cols), 2)
    return jnp.sum(jnp.where(lane // per_block == block, looks, 0.0), axis=1)


def planes_of(ref, at):
    return [ref[at, 2 * k] for k in range(LOOK_AZ)], [ref[at, 2 * k + 1] for k in range(LOOK_AZ)]


OWN_PAIRS = [(d, range(1, inside(d) + 1)) for d in range(GROUP)]
LATER_PAIRS = [(d, range(inside(d) + 1, SPAN + 1)) for d in range(GROUP) if inside(d) < SPAN]
OWN_ROWS = sum(2 * len(gaps) for _, gaps in OWN_PAIRS)
LATER_ROWS = sum(2 * len(gaps) for _, gaps in LATER_PAIRS)


def own_kernel(own_ref, out_ref, sums):
    out_ref[...] = look_at(lambda d: planes_of(own_ref, place_of(d)), OWN_PAIRS, range(GROUP), sums, out_ref.shape[-1])


def later_kernel(own_ref, later_ref, looks_ref, out_ref, sums, cells):
    def date(index):
        if index < GROUP:
            return planes_of(own_ref, place_of(index))
        return planes_of(later_ref, place_of(index - GROUP) - (GROUP - SPAN))

    cells[...] = look_at(date, LATER_PAIRS, range(GROUP, GROUP + SPAN), sums, out_ref.shape[-1])
    tiles = out_ref.shape[0] // GROUP
    own_at = later_at = 0
    for index in range(GROUP):
        near, far = inside(index), SPAN - inside(index)
        place = ORDERS[0].index(index)
        piece = out_ref.at[at(0, place, tiles)]
        for part in range(2):
            if near:
                piece[part * SPAN : part * SPAN + near, :] = looks_ref[own_at : own_at + near, :]
            if far:
                piece[part * SPAN + near : (part + 1) * SPAN, :] = cells[later_at : later_at + far, :]
            own_at += near
            later_at += far
        piece[2 * SPAN : 2 * SPAN + 1 + near, :] = looks_ref[OWN_ROWS + index : OWN_ROWS + index + 1 + near, :]
        if far:
            piece[2 * SPAN + 1 + near :, :] = cells[LATER_ROWS : LATER_ROWS + far, :]
        for tile in range(1, tiles):
            out_ref[at(tile, ORDERS[tile % 2].index(index), tiles)] = out_ref[at(0, place, tiles)]


def look_own(own, cols):
    rows = OWN_ROWS + GROUP
    return pl.pallas_call(
        own_kernel,
        out_shape=jax.ShapeDtypeStruct((rows, cols), jnp.float32),
        scratch_shapes=[pltpu.VMEM((rows * SUB, own.shape[-1]), jnp.float32)],
        compiler_params=pltpu.CompilerParams(vmem_limit_bytes=8 * 1024 * 1024),
        cost_estimate=pl.CostEstimate(
            flops=12 * rows * SUB * cols * cols, bytes_accessed=own.size * 4, transcendentals=0
        ),
        name="look_own",
    )(own)


def look_later(own, later, looks, tiles):
    cols = looks.shape[-1]
    rows = LATER_ROWS + SPAN
    return pl.pallas_call(
        later_kernel,
        out_shape=jax.ShapeDtypeStruct((GROUP * tiles, FIELDS, cols), jnp.float32),
        scratch_shapes=[
            pltpu.VMEM((rows * SUB, own.shape[-1]), jnp.float32),
            pltpu.VMEM((rows, cols), jnp.float32),
        ],
        compiler_params=pltpu.CompilerParams(vmem_limit_bytes=8 * 1024 * 1024),
        name="look_later",
    )(own, later, looks)


def coherence_kernel(tiles, rows_ref, looks_out, coher_out, looks_ref, boxes, coher_ref, sent):
    date, dates = lax.axis_index("date"), lax.axis_size("date")
    tile = lax.axis_index("az")
    cols = rows_ref.shape[-1]
    half = WIN // 2
    for gap in range(1, SPAN + 1):
        for part in range(2):
            start = at(tile, 0, tiles) * FIELDS + part * SPAN + gap - 1
            look = rows_ref[pl.ds(start, GROUP, stride=tiles // 2 * FIELDS), :]
            looks_ref[gap - 1, part, 0] = jnp.where(date + gap < dates, look, 0.0)
    looks_sent = pltpu.make_async_copy(looks_ref, looks_out, sent.at[0])
    looks_sent.start()

    lane = lax.broadcasted_iota(jnp.int32, (FIELDS, cols), 1)
    rows = []
    for offset in range(-half, GROUP + half):
        other = tile + offset // GROUP
        start = at(jnp.clip(other, 0, tiles - 1), offset % GROUP, tiles) * FIELDS
        row = rows_ref[pl.ds(pl.multiple_of(start, FIELDS), FIELDS), :]
        if not 0 <= offset < GROUP:
            row = jnp.where(jnp.logical_and(other >= 0, other < tiles), row, 0.0)
        rows.append(row)
    for r in range(GROUP):
        tall = rows[r]
        for shift in range(1, WIN):
            tall = tall + rows[r + shift]
        boxed = tall
        for shift in range(1, half + 1):
            boxed = boxed + jnp.where(lane >= shift, pltpu.roll(tall, shift, 1), 0.0)
            boxed = boxed + jnp.where(lane < cols - shift, pltpu.roll(tall, cols - shift, 1), 0.0)
        boxes[r * FIELDS : (r + 1) * FIELDS, :] = boxed
    fields = [boxes[pl.ds(field, GROUP, stride=FIELDS), :] for field in range(FIELDS)]
    own, later = fields[2 * SPAN], fields[2 * SPAN + 1 :]
    for gap in range(1, SPAN + 1):
        real, imag = fields[gap - 1], fields[SPAN + gap - 1]
        value = jnp.sqrt(real * real + imag * imag) / jnp.sqrt(own * later[gap - 1] + 1e-06)
        coher_ref[gap - 1, 0] = jnp.where(date + gap < dates, value, 0.0)
    coher_sent = pltpu.make_async_copy(coher_ref, coher_out, sent.at[1])
    coher_sent.start()
    looks_sent.wait()
    coher_sent.wait()


def finish(rows, tiles):
    cols = rows.shape[-1]
    looks = (SPAN, 2, 1, GROUP, cols)
    coher = (SPAN, 1, GROUP, cols)
    return pl.pallas_call(
        functools.partial(coherence_kernel, tiles),
        out_shape=(jax.ShapeDtypeStruct(looks, jnp.float32), jax.ShapeDtypeStruct(coher, jnp.float32)),
        out_specs=(pl.BlockSpec(memory_space=pl.ANY), pl.BlockSpec(memory_space=pl.ANY)),
        scratch_shapes=[
            pltpu.VMEM(looks, jnp.float32),
            pltpu.VMEM((GROUP * FIELDS, cols), jnp.float32),
            pltpu.VMEM(coher, jnp.float32),
            pltpu.SemaphoreType.DMA((2,)),
        ],
        compiler_params=pltpu.CompilerParams(vmem_limit_bytes=4 * 1024 * 1024),
        name="finish",
    )(rows)


def local(slabs):
    dates, tiles = lax.axis_size("date"), lax.axis_size("az")
    _, planes, lines, samples = slabs.shape
    cols = samples // LOOK_RG
    both = ("date", "az")
    starts = range(0, dates, GROUP)
    groups = [[(g + d) * tiles + a for d in ORDERS[a % 2]] for g in starts for a in range(tiles)]
    places = sorted((at(a, row, tiles), row, a) for row in range(GROUP) for a in range(tiles))
    wide = [[(g + ORDERS[a % 2][row]) * tiles + a for _, row, a in places] for g in starts]
    pieces = cut(slabs[0]).reshape(GROUP, LOOK_AZ * planes, SUB, samples // SUB)
    own = lax.all_to_all(pieces, both, 0, 0, axis_index_groups=groups, tiled=True)
    back = [(i, i - GROUP) for i in range(GROUP, dates)]
    later = lax.ppermute(own[GROUP - SPAN :], "date", back)
    fields = look_later(own, later, look_own(own, cols), tiles)
    rows = lax.all_to_all(fields, ("date", "az"), 0, 0, axis_index_groups=wide, tiled=True)
    return finish(rows.reshape(GROUP * tiles * FIELDS, cols), tiles)


def solution(mesh):
    in_specs = (P("date", None, "az", None),)
    out_specs = (P(None, None, "date", "az", None), P(None, "date", "az", None))
    return jax.shard_map(local, mesh=mesh, in_specs=in_specs, out_specs=out_specs, check_vma=False)
```

```python
import functools

import jax
import jax.numpy as jnp
from jax import lax
from jax.experimental import pallas as pl
from jax.experimental.pallas import tpu as pltpu
from jax.sharding import PartitionSpec as P

LOOK_AZ = 4
LOOK_RG = 16
WIN = 5
SPAN = 5
GROUP = 8
FIELDS = 3 * SPAN + 1
ORDER = (6, 7, 5, 4, 2, 3, 0, 1)
SUB = 16


def cut_kernel(slab_ref, out_ref, held, arrived):
    planes, lines, _ = slab_ref.shape
    width = out_ref.shape[-1]
    copies = []
    for line in range(0, lines, 8):
        here = (pl.ds(0, planes), pl.ds(line, 8))
        copies.append(pltpu.make_async_copy(slab_ref.at[here], held.at[here], arrived.at[len(copies)]))
        copies[-1].start()
    for line, copy in zip(range(0, lines, 8), copies):
        copy.wait()
        for plane in range(planes):
            for block in range(SUB):
                part = held[plane, line : line + 8, block * width : (block + 1) * width]
                start = (line * planes + plane) * SUB + block
                out_ref[pl.ds(start, 8, stride=planes * SUB), :] = part


def cut(slab):
    planes, lines, samples = slab.shape
    rows = planes * lines * SUB
    slab = pltpu.with_memory_space_constraint(slab, pltpu.HBM)
    return pl.pallas_call(
        cut_kernel,
        in_specs=[pl.BlockSpec(memory_space=pl.ANY)],
        out_shape=jax.ShapeDtypeStruct((rows, samples // SUB), jnp.float32),
        scratch_shapes=[
            pltpu.VMEM(slab.shape, jnp.float32),
            pltpu.SemaphoreType.DMA((lines // 8,)),
        ],
        compiler_params=pltpu.CompilerParams(vmem_limit_bytes=4 * 1024 * 1024),
        name="cut",
    )(slab)


def inside(index):
    return min(SPAN, GROUP - 1 - index)


def at(tile, row, tiles):
    return (tile % 2 * GROUP + row) * (tiles // 2) + tiles // 2 - 1 - tile // 2


def look_at(date, pairs, powers, sums, cols):
    width = sums.shape[-1]
    count = 0

    def put(terms):
        nonlocal count
        total = terms[0]
        for term in terms[1:]:
            total = total + term
        sums[count * SUB : (count + 1) * SUB, :] = total
        count += 1

    for index, gaps in pairs:
        real, imag = date(index)
        others = [date(index + gap) for gap in gaps]
        for other_real, other_imag in others:
            put([a * b for a, b in zip(real + imag, other_real + other_imag)])
        for other_real, other_imag in others:
            put([a * b - c * d for a, b, c, d in zip(imag, other_real, real, other_imag)])
    for index in powers:
        real, imag = date(index)
        put([v * v for v in real + imag])

    per_block = width // LOOK_RG
    sample = lax.broadcasted_iota(jnp.int32, (width, cols), 0)
    lane = lax.broadcasted_iota(jnp.int32, (width, cols), 1)
    weight = jnp.where(sample // LOOK_RG == lane % per_block, 1.0 / (LOOK_AZ * LOOK_RG), 0.0)
    weight = weight.astype(jnp.bfloat16)
    total = sums[: count * SUB, :]
    high = total.astype(jnp.bfloat16)
    low = (total - high.astype(jnp.float32)).astype(jnp.bfloat16)
    looks = jnp.dot(high, weight, preferred_element_type=jnp.float32)
    looks = looks + jnp.dot(low, weight, preferred_element_type=jnp.float32)
    looks = looks.reshape(count, SUB, cols)
    block = lax.broadcasted_iota(jnp.int32, (1, SUB, cols), 1)
    lane = lax.broadcasted_iota(jnp.int32, (1, SUB, cols), 2)
    return jnp.sum(jnp.where(lane // per_block == block, looks, 0.0), axis=1)


def planes_of(ref, at):
    return [ref[at, 2 * k] for k in range(LOOK_AZ)], [ref[at, 2 * k + 1] for k in range(LOOK_AZ)]


OWN_PAIRS = [(d, range(1, inside(d) + 1)) for d in range(GROUP)]
LATER_PAIRS = [(d, range(inside(d) + 1, SPAN + 1)) for d in range(GROUP) if inside(d) < SPAN]
OWN_ROWS = sum(2 * len(gaps) for _, gaps in OWN_PAIRS)
LATER_ROWS = sum(2 * len(gaps) for _, gaps in LATER_PAIRS)


def own_kernel(own_ref, out_ref, sums):
    out_ref[...] = look_at(lambda d: planes_of(own_ref, ORDER.index(d)), OWN_PAIRS, range(GROUP), sums, out_ref.shape[-1])


def later_kernel(own_ref, later_ref, looks_ref, out_ref, sums, cells):
    def date(index):
        if index < GROUP:
            return planes_of(own_ref, ORDER.index(index))
        return planes_of(later_ref, ORDER.index(index - GROUP) - (GROUP - SPAN))

    cells[...] = look_at(date, LATER_PAIRS, range(GROUP, GROUP + SPAN), sums, out_ref.shape[-1])
    tiles = out_ref.shape[0] // GROUP
    own_at = later_at = 0
    for index in range(GROUP):
        near, far = inside(index), SPAN - inside(index)
        place = ORDER.index(index)
        piece = out_ref.at[at(0, place, tiles)]
        for part in range(2):
            if near:
                piece[part * SPAN : part * SPAN + near, :] = looks_ref[own_at : own_at + near, :]
            if far:
                piece[part * SPAN + near : (part + 1) * SPAN, :] = cells[later_at : later_at + far, :]
            own_at += near
            later_at += far
        piece[2 * SPAN : 2 * SPAN + 1 + near, :] = looks_ref[OWN_ROWS + index : OWN_ROWS + index + 1 + near, :]
        if far:
            piece[2 * SPAN + 1 + near :, :] = cells[LATER_ROWS : LATER_ROWS + far, :]
        for tile in range(1, tiles):
            out_ref[at(tile, place, tiles)] = out_ref[at(0, place, tiles)]


def look_own(own, cols):
    rows = OWN_ROWS + GROUP
    return pl.pallas_call(
        own_kernel,
        out_shape=jax.ShapeDtypeStruct((rows, cols), jnp.float32),
        scratch_shapes=[pltpu.VMEM((rows * SUB, own.shape[-1]), jnp.float32)],
        compiler_params=pltpu.CompilerParams(vmem_limit_bytes=8 * 1024 * 1024),
        cost_estimate=pl.CostEstimate(
            flops=12 * rows * SUB * cols * cols, bytes_accessed=own.size * 4, transcendentals=0
        ),
        name="look_own",
    )(own)


def look_later(own, later, looks, tiles):
    cols = looks.shape[-1]
    rows = LATER_ROWS + SPAN
    return pl.pallas_call(
        later_kernel,
        out_shape=jax.ShapeDtypeStruct((GROUP * tiles, FIELDS, cols), jnp.float32),
        scratch_shapes=[
            pltpu.VMEM((rows * SUB, own.shape[-1]), jnp.float32),
            pltpu.VMEM((rows, cols), jnp.float32),
        ],
        compiler_params=pltpu.CompilerParams(vmem_limit_bytes=8 * 1024 * 1024),
        name="look_later",
    )(own, later, looks)


def coherence_kernel(tiles, rows_ref, looks_out, coher_out, looks_ref, boxes, coher_ref, sent):
    date, dates = lax.axis_index("date"), lax.axis_size("date")
    tile = lax.axis_index("az")
    cols = rows_ref.shape[-1]
    half = WIN // 2
    for gap in range(1, SPAN + 1):
        for part in range(2):
            start = at(tile, 0, tiles) * FIELDS + part * SPAN + gap - 1
            look = rows_ref[pl.ds(start, GROUP, stride=tiles // 2 * FIELDS), :]
            looks_ref[gap - 1, part, 0] = jnp.where(date + gap < dates, look, 0.0)
    looks_sent = pltpu.make_async_copy(looks_ref, looks_out, sent.at[0])
    looks_sent.start()

    lane = lax.broadcasted_iota(jnp.int32, (FIELDS, cols), 1)
    rows = []
    for offset in range(-half, GROUP + half):
        other = tile + offset // GROUP
        start = at(jnp.clip(other, 0, tiles - 1), offset % GROUP, tiles) * FIELDS
        row = rows_ref[pl.ds(pl.multiple_of(start, FIELDS), FIELDS), :]
        if not 0 <= offset < GROUP:
            row = jnp.where(jnp.logical_and(other >= 0, other < tiles), row, 0.0)
        rows.append(row)
    for r in range(GROUP):
        tall = rows[r]
        for shift in range(1, WIN):
            tall = tall + rows[r + shift]
        boxed = tall
        for shift in range(1, half + 1):
            boxed = boxed + jnp.where(lane >= shift, pltpu.roll(tall, shift, 1), 0.0)
            boxed = boxed + jnp.where(lane < cols - shift, pltpu.roll(tall, cols - shift, 1), 0.0)
        boxes[r * FIELDS : (r + 1) * FIELDS, :] = boxed
    fields = [boxes[pl.ds(field, GROUP, stride=FIELDS), :] for field in range(FIELDS)]
    own, later = fields[2 * SPAN], fields[2 * SPAN + 1 :]
    for gap in range(1, SPAN + 1):
        real, imag = fields[gap - 1], fields[SPAN + gap - 1]
        value = jnp.sqrt(real * real + imag * imag) / jnp.sqrt(own * later[gap - 1] + 1e-06)
        coher_ref[gap - 1, 0] = jnp.where(date + gap < dates, value, 0.0)
    coher_sent = pltpu.make_async_copy(coher_ref, coher_out, sent.at[1])
    coher_sent.start()
    looks_sent.wait()
    coher_sent.wait()


def finish(rows, tiles):
    cols = rows.shape[-1]
    looks = (SPAN, 2, 1, GROUP, cols)
    coher = (SPAN, 1, GROUP, cols)
    return pl.pallas_call(
        functools.partial(coherence_kernel, tiles),
        out_shape=(jax.ShapeDtypeStruct(looks, jnp.float32), jax.ShapeDtypeStruct(coher, jnp.float32)),
        out_specs=(pl.BlockSpec(memory_space=pl.ANY), pl.BlockSpec(memory_space=pl.ANY)),
        scratch_shapes=[
            pltpu.VMEM(looks, jnp.float32),
            pltpu.VMEM((GROUP * FIELDS, cols), jnp.float32),
            pltpu.VMEM(coher, jnp.float32),
            pltpu.SemaphoreType.DMA((2,)),
        ],
        compiler_params=pltpu.CompilerParams(vmem_limit_bytes=4 * 1024 * 1024),
        name="finish",
    )(rows)


def local(slabs):
    dates, tiles = lax.axis_size("date"), lax.axis_size("az")
    _, planes, lines, samples = slabs.shape
    cols = samples // LOOK_RG
    groups = [[g + d for d in ORDER] for g in range(0, dates, GROUP)]
    places = sorted((at(a, row, tiles), row, a) for row in range(GROUP) for a in range(tiles))
    wide = [[group[row] * tiles + a for _, row, a in places] for group in groups]
    pieces = cut(slabs[0]).reshape(GROUP, LOOK_AZ * planes, SUB, samples // SUB)
    own = lax.all_to_all(pieces, "date", 0, 0, axis_index_groups=groups, tiled=True)
    back = [(i, i - GROUP) for i in range(GROUP, dates)]
    later = lax.ppermute(own[GROUP - SPAN :], "date", back)
    fields = look_later(own, later, look_own(own, cols), tiles)
    rows = lax.all_to_all(fields, ("date", "az"), 0, 0, axis_index_groups=wide, tiled=True)
    return finish(rows.reshape(GROUP * tiles * FIELDS, cols), tiles)


def solution(mesh):
    in_specs = (P("date", None, "az", None),)
    out_specs = (P(None, None, "date", "az", None), P(None, "date", "az", None))
    return jax.shard_map(local, mesh=mesh, in_specs=in_specs, out_specs=out_specs, check_vma=False)
```
